512 devices in a mesh: chan: 128 (over z, y, core), tm: 4 (over x).
Axes of the slice: x: 4, y: 8, z: 8, core: 2. Of those that a mesh axis runs over, the one named last changes fastest.
Arguments:
- voltage: bfloat16 [512, 64, 7168], P('chan', 'tm'), may hold values from -8 to 8
- fir_taps: float32 [12, 16], replicated, may hold values from -1.75 to 1.75
- zoom_width: int32 [224], replicated, may hold values from 1 to 16, 1792 in all
- zoom_shift: int32 [224], replicated, may hold values from 0 to 15
- owner_slot: int32 [1792], replicated, may hold values from 0 to 1791, each once
Outputs:
- fine_spectra: bfloat16 [1792, 64, 2, 512], P('chan', 'tm')
- visibility: bfloat16 [1792, 2, 512, 512], P('chan', None, 'tm')
The draws below stay inside these ranges and needn't reach their ends.
Inputs may be any that keep to these rules, and one draw needn't show every extreme that they name: `zoom_width`: the widths sum to 1792. `owner_slot`: every position occurs once.
All inputs are finite; a program needn't handle non-finite values.
Results may differ from the reference program's by a relative error of at most 0.0033.
Values may be sent and summed in bfloat16 or wider, within the bound.
No kernel may reach another device: no remote copies, remote signals or barrier semaphores. Data moves between devices by JAX's collectives and lax.ppermute only.
A program may use at most 64 MiB of HBM per device.

```python
import math
import jax
import jax.numpy as jnp
import numpy as np
from jax import lax

F = 16
TAPS = 12
INPUTS = 512
FINE = 1792
COARSE = 224
ZMAX = 16
SPECTRA = 64


def draw_voltage(key, part):
    key = jax.random.fold_in(key, 7)
    key_noise, key_sky, key_gain = jax.random.split(key, 3)
    shape = (INPUTS, SPECTRA, COARSE, 2, F)
    sky = jax.random.normal(key_sky, (4, SPECTRA, COARSE, 2, F), jnp.float32)
    gains = jax.random.normal(key_gain, (4, INPUTS, 2), jnp.float32) * 0.35
    total = 0.8 * jax.random.normal(key_noise, shape, jnp.float32)
    for source in range(4):
        sky_real = sky[source][None, :, :, 0]
        sky_imag = sky[source][None, :, :, 1]
        gain_real = gains[source, :, 0][:, None, None, None]
        gain_imag = gains[source, :, 1][:, None, None, None]
        real = gain_real * sky_real - gain_imag * sky_imag
        imag = gain_real * sky_imag + gain_imag * sky_real
        total = total + jnp.stack([real, imag], 3)
    return jnp.clip(total, -8.0, 8.0).reshape(INPUTS, SPECTRA, COARSE * 2 * F).astype(jnp.bfloat16)


def place_ends(entries, key, least, high):
    index_at = [jax.random.randint(jax.random.fold_in(key, axis), (), 0, length) for axis, length in enumerate(entries.shape)]
    main_axis = entries.shape.index(max(entries.shape))
    neighbour = index_at[:main_axis] + [(index_at[main_axis] + 1) % entries.shape[main_axis]] + index_at[main_axis + 1:]
    return entries.at[tuple(index_at)].set(least).at[tuple(neighbour)].set(high)


def split_up(amount, total, reach, lean):
    loads = [(1 << 20) // math.isqrt(standing ** lean) + 1 for standing in range(2, amount + 1)]
    surplus, holding = total - reach - (amount - 1), [1] * (amount - 1)
    while surplus > 0:
        candidates = [i for i in range(amount - 1) if holding[i] < reach]
        mass, remaining = sum([loads[i] for i in candidates]), surplus
        for i in candidates:
            addition = min(reach - holding[i], max(1, remaining * loads[i] // mass), surplus)
            holding[i] = holding[i] + addition
            surplus = surplus - addition
    return np.array([reach] + holding)


def ragged(stream_key, number_of, total, most, lean):
    if number_of == 2:
        one = jax.random.randint(stream_key, (), max(1, total - most), min(most, total - 1) + 1)
        return jnp.stack([one, total - one])
    sizes = jnp.asarray(split_up(number_of, total, most, lean), jnp.int32)
    pairs = (number_of - 1) // 2
    donor, receiver = sizes[1:1 + 2 * pairs:2], sizes[2:2 + 2 * pairs:2]
    margin = jnp.minimum(donor - 1, most - receiver)
    passed = jax.random.randint(jax.random.fold_in(stream_key, 1), (pairs,), 0, 1 << 20) % (margin + 1)
    sizes = sizes.at[1:1 + 2 * pairs:2].set(donor - passed).at[2:2 + 2 * pairs:2].set(receiver + passed)
    return sizes[jax.random.permutation(jax.random.fold_in(stream_key, 2), number_of)]


def gaussian(rng, extent, width, most, kind=jnp.bfloat16):
    array = width * jax.random.normal(rng, extent, jnp.float32)
    return jnp.clip(array, min=-most, max=most).astype(kind)


def setup_inputs(seed: int = 0) -> dict:
    seeds = jax.random.split(jax.random.key(seed), 6)
    return {
        "voltage": draw_voltage(jax.random.fold_in(seeds[5], 71), 0),
        "fir_taps": gaussian(seeds[1], (TAPS, F), TAPS ** -0.5, 1.75, jnp.float32),
        "zoom_width": ragged(seeds[2], COARSE, FINE, ZMAX, 1).astype(jnp.int32),
        "zoom_shift": place_ends(jax.random.randint(seeds[3], (COARSE,), 0, F), jax.random.fold_in(seeds[3], 1), 0, F - 1).astype(jnp.int32),
        "owner_slot": jax.random.permutation(seeds[4], FINE).astype(jnp.int32),
    }


def dft_table(phases, dtype):
    rows = jnp.arange(phases, dtype=jnp.int32)
    turns = (rows[:, None] * rows[None, :] % phases).astype(dtype)
    angle = turns * (2.0 * jnp.pi / phases)
    scale = 1.0 / jnp.sqrt(jnp.asarray(phases, dtype))
    cosine = jnp.cos(angle) * scale
    sine = jnp.sin(angle) * scale
    table = jnp.stack([jnp.stack([cosine, sine], 1), jnp.stack([-sine, cosine], 1)], 0)
    return jnp.transpose(table, (2, 3, 0, 1)).reshape(2 * phases, 2 * phases)

def slot_columns(zoom_width, zoom_shift, owner_slot, phases):
    fine = owner_slot.shape[0]
    coarse = zoom_width.shape[0]
    ends = jnp.cumsum(zoom_width).astype(jnp.int32)
    firsts = (ends - zoom_width).astype(jnp.int32)
    starts = (zoom_shift % (phases - zoom_width + 1)).astype(jnp.int32)
    channel = jnp.arange(fine, dtype=jnp.int32)
    member = ((channel[:, None] >= firsts[None, :]) & (channel[:, None] < ends[None, :])).astype(jnp.int32)
    coarse_of = lax.optimization_barrier(jnp.sum(member * jnp.arange(coarse, dtype=jnp.int32)[None, :], 1)).astype(jnp.int32)
    bin_of = (lax.optimization_barrier(jnp.sum(member * (starts - firsts)[None, :], 1)) + channel).astype(jnp.int32)
    base = (coarse_of * 2 * phases + bin_of).astype(jnp.int32)
    order = jnp.zeros((fine,), jnp.int32).at[owner_slot].set(channel)
    slotted = base[order]
    return jnp.stack([slotted, slotted + phases], 1).reshape(-1).astype(jnp.int32)

def reference(voltage, fir_taps, zoom_width, zoom_shift, owner_slot):
    inputs, spectra, samples = voltage.shape
    spread = fir_taps.shape[0] - 1
    phases = fir_taps.shape[1]
    coarse = samples // (2 * phases)
    fine = owner_slot.shape[0]
    table = dft_table(phases, jnp.float32)
    taps_full = jnp.tile(fir_taps, (1, 2 * coarse))
    columns = slot_columns(zoom_width, zoom_shift, owner_slot, phases)

    def channelize(single):
        series = jnp.pad(single.astype(jnp.float32), ((spread, 0), (0, 0)))
        filtered = jnp.zeros(single.shape, jnp.float32)
        for lag in range(spread + 1):
            filtered = filtered + taps_full[lag][None, :] * series[spread - lag:spread - lag + spectra]
        result = jnp.dot(filtered.reshape(spectra * coarse, 2 * phases), table, precision=lax.Precision.HIGHEST)
        result = result.reshape(spectra, samples)
        return jnp.take(result, columns, axis=1).astype(jnp.bfloat16)
    selected = lax.map(channelize, voltage)
    fine_spectra = jnp.transpose(selected.reshape(inputs, spectra, fine, 2), (2, 1, 3, 0))

    def correlate(block):
        data = block.astype(jnp.float32)
        other = jnp.stack([data[:, 1], -data[:, 0]], 1)
        left = jnp.stack([data, other], 0)
        return (jnp.einsum('psqa,sqb->pab', left, data) / spectra).astype(jnp.bfloat16)
    visibility = lax.map(correlate, fine_spectra)
    return (fine_spectra, visibility)
```

```python
import functools

import jax
import jax.numpy as jnp
import ml_dtypes
import numpy as np
from jax import lax
from jax.experimental import pallas as pl
from jax.experimental.pallas import tpu as pltpu
from jax.sharding import PartitionSpec as P

VMEM = pltpu.VMEM
BF16 = jnp.bfloat16
F32 = jnp.float32
LIMIT = 48 * 1024 * 1024


def dft_weights(phases, coarse):
    rows = np.arange(phases)
    angle = (rows[:, None] * rows[None, :] % phases) * (2.0 * np.pi / phases)
    cosine = np.cos(angle) / np.sqrt(phases)
    sine = np.sin(angle) / np.sqrt(phases)
    table = np.stack([np.stack([cosine, -sine], 0), np.stack([sine, cosine], 0)], 0)
    weights = np.einsum("pqjb,cd->cpjqdb", table, np.eye(coarse))
    weights = weights.reshape(coarse * 2 * phases, 2 * coarse * phases).astype(np.float32)
    high = weights.astype(ml_dtypes.bfloat16)
    low = (weights - high.astype(np.float32)).astype(ml_dtypes.bfloat16)
    return high, low


def channelize_kernel(
    base_ref, voltage_ref, recent_ref, older_ref, taps_ref, high_ref, low_ref, krow_ref, slot_ref,
    out_ref, window_ref, bins_ref, *, rows_wide,
):
    inputs, blocks, samples = voltage_ref.shape
    taps = taps_ref.shape[0]
    wide = 512
    lanes = 128
    window_ref[...] = jnp.zeros(window_ref.shape, F32)

    def chunk(step, carry):
        at = pl.multiple_of(step * wide, wide)
        filtered = []
        for i in range(inputs):
            parts = []
            for sub in range(wide // lanes):
                spot = pl.ds(pl.multiple_of(at + sub * lanes, lanes), lanes)
                older = older_ref[i, :, spot].astype(F32)
                series = jnp.concatenate(
                    [
                        jnp.zeros((8 - older.shape[0], lanes), F32),
                        older,
                        recent_ref[i, :, spot].astype(F32),
                        voltage_ref[i, :, spot].astype(F32),
                    ],
                    0,
                )
                total = taps_ref[0:1, :] * series[16:, :]
                for lag in range(1, taps):
                    total = total + taps_ref[lag : lag + 1, :] * series[16 - lag : 16 - lag + blocks, :]
                parts.append(total)
            filtered.append(jnp.concatenate(parts, 1))
        full = jnp.concatenate(filtered, 0)
        high = full.astype(BF16)
        low = (full - high.astype(F32)).astype(BF16)
        real, imag = [], []
        for half in range(2):
            spot = slice(half * 256, half * 256 + 256)
            spectra = jnp.dot(high[:, spot], high_ref[...], preferred_element_type=F32)
            spectra = spectra + jnp.dot(low[:, spot], high_ref[...], preferred_element_type=F32)
            spectra = spectra + jnp.dot(high[:, spot], low_ref[...], preferred_element_type=F32)
            real.append(spectra[:, :128])
            imag.append(spectra[:, 128:])
        table = jnp.concatenate([jnp.concatenate(real, 1), jnp.concatenate(imag, 1)], 0).astype(BF16)
        base = pl.multiple_of(base_ref[step], 16)
        row = lax.broadcasted_iota(jnp.int32, (rows_wide, 256), 0) + base
        member = jnp.where(row == krow_ref[pl.ds(step, 1), :], 1.0, 0.0).astype(BF16)
        picked = lax.dot_general(
            member, table, (((1,), (1,)), ((), ())), preferred_element_type=F32
        )
        window_ref[pl.ds(base, rows_wide), :] += picked
        return carry

    lax.fori_loop(0, samples // wide, chunk, 0)
    fine = slot_ref.shape[1]
    bins_ref[...] = window_ref[0:fine, :].astype(BF16)
    step_rows = 256

    def place(step, carry):
        at = pl.multiple_of(step * step_rows, step_rows)
        row = lax.broadcasted_iota(jnp.int32, (step_rows, fine), 0) + at
        member = jnp.where(row == slot_ref[...], 1.0, 0.0).astype(BF16)
        out_ref[pl.ds(at, step_rows), :] = jnp.dot(
            member, bins_ref[...], preferred_element_type=F32
        ).astype(BF16)
        return carry

    lax.fori_loop(0, out_ref.shape[0] // step_rows, place, 0)


def unpack_kernel(received_ref, out_ref, wide_ref, *, pad, inputs_dev):
    fine_dev = out_ref.shape[0]
    rows, lanes = received_ref.shape
    devices = rows // pad
    blocks = lanes // (2 * inputs_dev)
    wide_ref[...] = received_ref[...].astype(F32)
    inputs = inputs_dev * devices
    source = lax.broadcasted_iota(jnp.int32, (inputs, inputs), 0)
    target = lax.broadcasted_iota(jnp.int32, (inputs, inputs), 1)
    spread = jnp.where((source % devices) * inputs_dev + source // devices == target, 1.0, 0.0)
    spread = spread.astype(BF16)
    pieces = []
    for channel in range(fine_dev):
        turned = wide_ref[pl.ds(channel, devices, stride=pad), :].T.astype(BF16)
        for q in range(2):
            pieces.append(
                jnp.concatenate(
                    [
                        turned[(q * inputs_dev + i) * blocks : (q * inputs_dev + i + 1) * blocks, :]
                        for i in range(inputs_dev)
                    ],
                    1,
                )
            )
    joined = jnp.concatenate(pieces, 0)
    placed = jnp.dot(joined, spread, preferred_element_type=F32).astype(BF16)
    out_ref[...] = placed.reshape(out_ref.shape)


def correlate_kernel(mine_ref, own_ref, up_ref, down_ref, across_ref, out_ref, *, scale):
    mine = pl.ds(pl.multiple_of(mine_ref[0], 128), 128)
    refs = (own_ref, up_ref, down_ref, across_ref)
    half = own_ref.shape[1] // 2
    for channel in range(own_ref.shape[0]):
        right = jnp.concatenate([ref[channel] for ref in refs], 0)
        real, imag = [], []
        for ref in refs:
            rows = ref[channel, :, mine]
            real.append(rows)
            imag.append(rows[half:])
            imag.append(-rows[:half])
        left = jnp.concatenate([jnp.concatenate(real, 0), jnp.concatenate(imag, 0)], 1)
        product = lax.dot_general(
            left, right, (((0,), (0,)), ((), ())), preferred_element_type=F32
        )
        product = (product * scale).astype(BF16)
        out_ref[channel, 0] = product[:128]
        out_ref[channel, 1] = product[128:]


def window_rows(zoom_width, zoom_shift, phases):
    ends = jnp.cumsum(zoom_width)
    firsts = ends - zoom_width
    starts = zoom_shift % (phases - zoom_width + 1)
    bins = jnp.arange(phases, dtype=jnp.int32)[None, :] - starts[:, None]
    inside = (bins >= 0) & (bins < zoom_width[:, None])
    return firsts, jnp.where(inside, firsts[:, None] + bins, -1)


def channelize(voltage, recent, older, fir_taps, zoom_width, zoom_shift, owner_slot, devices, pad):
    inputs_dev, blocks, samples = voltage.shape
    phases = fir_taps.shape[1]
    fine = owner_slot.shape[0]
    fine_dev = fine // devices
    firsts, krow = window_rows(zoom_width, zoom_shift, phases)
    groups = 256 // phases
    base = firsts[::groups] // 16 * 16
    slot = (owner_slot // fine_dev) * pad + owner_slot % fine_dev
    high, low = dft_weights(phases, 8)
    rows_wide = 272
    whole = pl.BlockSpec(memory_space=VMEM)
    return pl.pallas_call(
        functools.partial(channelize_kernel, rows_wide=rows_wide),
        out_shape=jax.ShapeDtypeStruct((devices * pad, 2 * inputs_dev * blocks), BF16),
        in_specs=[pl.BlockSpec(memory_space=pltpu.SMEM)] + [whole] * 8,
        out_specs=whole,
        scratch_shapes=[
            pltpu.VMEM((fine + 256, 128), F32),
            pltpu.VMEM((fine, 128), BF16),
        ],
        compiler_params=pltpu.CompilerParams(vmem_limit_bytes=LIMIT),
        name="channelize",
    )(
        base, voltage, recent, older, jnp.tile(fir_taps, (1, 128 // phases)), jnp.asarray(high),
        jnp.asarray(low), krow.reshape(samples // 512, 256), slot[None, :],
    )


def unpack(received, fine_dev, inputs_dev, pad):
    rows, lanes = received.shape
    devices = rows // pad
    blocks = lanes // (2 * inputs_dev)
    whole = pl.BlockSpec(memory_space=VMEM)
    return pl.pallas_call(
        functools.partial(unpack_kernel, pad=pad, inputs_dev=inputs_dev),
        out_shape=jax.ShapeDtypeStruct((fine_dev, 2 * blocks, devices * inputs_dev), BF16),
        in_specs=[whole],
        out_specs=whole,
        scratch_shapes=[pltpu.VMEM((rows, lanes), F32)],
        compiler_params=pltpu.CompilerParams(vmem_limit_bytes=LIMIT),
        name="unpack",
    )(received)


def correlate(own, up, down, across, mine, scale):
    fine_dev, rows, inputs = own.shape
    step = 2
    block = pl.BlockSpec((step, rows, inputs), lambda n, m: (n, 0, 0))
    return pl.pallas_call(
        functools.partial(correlate_kernel, scale=scale),
        out_shape=jax.ShapeDtypeStruct((fine_dev, 2, 128, inputs), BF16),
        grid_spec=pltpu.PrefetchScalarGridSpec(
            num_scalar_prefetch=1,
            grid=(fine_dev // step,),
            in_specs=[block] * 4,
            out_specs=pl.BlockSpec((step, 2, 128, inputs), lambda n, m: (n, 0, 0, 0)),
        ),
        compiler_params=pltpu.CompilerParams(vmem_limit_bytes=LIMIT),
        name="correlate",
    )(mine, own, up, down, across)


def local(voltage, fir_taps, zoom_width, zoom_shift, owner_slot):
    inputs_dev, blocks, samples = voltage.shape
    devices = lax.axis_size("chan")
    groups = lax.axis_size("tm")
    fine_dev = owner_slot.shape[0] // devices
    pad = 16
    up = [(i, (i + 1) % groups) for i in range(groups)]
    down = [(i, (i - 1) % groups) for i in range(groups)]
    recent = lax.ppermute(voltage[:, blocks - 8 :, :], "tm", up[:-1])
    older = lax.ppermute(voltage[:, blocks - 12 : blocks - 8, :], "tm", up[:-1])
    sent = channelize(
        voltage, recent, older, fir_taps, zoom_width, zoom_shift, owner_slot, devices, pad
    )
    lanes = sent.shape[1]
    received = lax.all_to_all(
        sent.reshape(devices, pad, lanes), "chan", split_axis=0, concat_axis=0, tiled=True
    )
    own = unpack(received.reshape(devices * pad, lanes), fine_dev, inputs_dev, pad)
    half = fine_dev // 2
    from_up = lax.ppermute(own, "tm", up)
    from_down = lax.ppermute(own, "tm", down)
    across = jnp.concatenate(
        [lax.ppermute(from_up[:half], "tm", up), lax.ppermute(from_down[half:], "tm", down)], 0
    )
    spectra = jnp.transpose(own.reshape(fine_dev, 2, blocks, own.shape[2]), (0, 2, 1, 3))
    mine = (lax.axis_index("tm") * 128).astype(jnp.int32)[None]
    summed = correlate(own, from_up, from_down, across, mine, 1.0 / (blocks * groups))
    return spectra, summed


def solution(mesh):
    return jax.shard_map(
        local,
        mesh=mesh,
        in_specs=(P("chan", "tm", None), P(), P(), P(), P()),
        out_specs=(P("chan", "tm", None, None), P("chan", None, "tm", None)),
        check_vma=False,
    )
```

```python
import functools

import jax
import jax.numpy as jnp
import ml_dtypes
import numpy as np
from jax import lax
from jax.experimental import pallas as pl
from jax.experimental.pallas import tpu as pltpu
from jax.sharding import PartitionSpec as P

VMEM = pltpu.VMEM
BF16 = jnp.bfloat16
F32 = jnp.float32
LIMIT = 32 * 1024 * 1024
WIDE = 272


def dft_weights(phases, coarse):
    rows = np.arange(phases)
    angle = (rows[:, None] * rows[None, :] % phases) * (2.0 * np.pi / phases)
    cosine = np.cos(angle) / np.sqrt(phases)
    sine = np.sin(angle) / np.sqrt(phases)
    table = np.stack([np.stack([cosine, -sine], 0), np.stack([sine, cosine], 0)], 0)
    weights = np.einsum("pqjb,cd->cpjqdb", table, np.eye(coarse))
    weights = weights.reshape(coarse * 2 * phases, 2 * coarse * phases).astype(np.float32)
    high = weights.astype(ml_dtypes.bfloat16)
    low = (weights - high.astype(np.float32)).astype(ml_dtypes.bfloat16)
    return high, low


def tap_tables(taps_ref):
    row = lax.broadcasted_iota(jnp.int32, (8, 128), 0)
    tap = [jnp.broadcast_to(taps_ref[m : m + 1, :], (8, 128)) for m in range(taps_ref.shape[0])]
    zero = jnp.zeros((8, 128), F32)
    same = [jnp.where(row >= k, tap[k], zero) for k in range(1, 8)]
    beyond = [jnp.where(row < k, tap[8 + k], zero) for k in range(1, 4)]
    before = [jnp.where(row < k, tap[k], tap[8 + k] if k < 4 else zero) for k in range(1, 8)]
    return tap[0], tap[8], same, before, beyond


def own_kernel(
    base_ref, voltage_ref, taps_ref, high_ref, low_ref, krow_ref, slot_ref,
    filtered_ref, member_ref, place_ref, high_out_ref, low_out_ref, *, rows_wide,
):
    inputs, blocks, samples = voltage_ref.shape
    lanes = 128
    first, eighth, same, before, beyond = tap_tables(taps_ref)

    def group(step, carry):
        for i in range(inputs):
            for sub in range(2):
                spot = pl.ds(pl.multiple_of(step * 256 + sub * lanes, lanes), lanes)
                series = voltage_ref[i, :, spot].astype(F32)
                early, late = series[:8], series[8:]
                top = first * early
                bottom = first * late + eighth * early
                for k in range(1, 8):
                    early_k = pltpu.roll(early, k, 0)
                    top = top + same[k - 1] * early_k
                    bottom = bottom + before[k - 1] * early_k
                    bottom = bottom + same[k - 1] * pltpu.roll(late, k, 0)
                at = pl.ds(pl.multiple_of(step * 64 + i * blocks, blocks), blocks)
                filtered_ref[at, sub * lanes : (sub + 1) * lanes] = jnp.concatenate([top, bottom], 0)
        return carry

    lax.fori_loop(0, samples // 256, group, 0)

    def windows(step, carry):
        row = lax.broadcasted_iota(jnp.int32, (rows_wide, 256), 0) + base_ref[step]
        at = pl.ds(pl.multiple_of(step * rows_wide, 16), rows_wide)
        member_ref[at, :] = jnp.where(row == krow_ref[pl.ds(step, 1), :], 1.0, 0.0).astype(BF16)
        return carry

    lax.fori_loop(0, samples // 512, windows, 0)
    rows = 64
    fine = slot_ref.shape[1]

    def places(step, carry):
        at = pl.multiple_of(step * rows, rows)
        row = lax.broadcasted_iota(jnp.int32, (rows, fine), 0) + at
        place_ref[pl.ds(at, rows), :] = jnp.where(row == slot_ref[...], 1.0, 0.0).astype(BF16)
        return carry

    lax.fori_loop(0, place_ref.shape[0] // rows, places, 0)
    high_out_ref[...] = high_ref[...]
    low_out_ref[...] = low_ref[...]


def channelize_kernel(
    base_ref, filtered_ref, recent_ref, older_ref, taps_ref, high_ref, low_ref, member_ref, place_ref,
    out_ref, split_high_ref, split_low_ref, table_ref, window_ref, bins_ref, *, rows_wide,
):
    inputs, _, samples = recent_ref.shape
    blocks = 16
    lanes = 128
    _, eighth, _, before, beyond = tap_tables(taps_ref)
    window_ref[...] = jnp.zeros(window_ref.shape, F32)

    def group(step, carry):
        for i in range(inputs):
            for sub in range(2):
                spot = pl.ds(pl.multiple_of(step * 256 + sub * lanes, lanes), lanes)
                at = pl.ds(pl.multiple_of(step * 64 + i * blocks, blocks), blocks)
                here = slice(sub * lanes, (sub + 1) * lanes)
                own = filtered_ref[at, here]
                recent = recent_ref[i, :, spot].astype(F32)
                older = older_ref[i, :, spot].astype(F32)
                older = jnp.concatenate([older, jnp.zeros((8 - older.shape[0], lanes), F32)], 0)
                top = own[:8] + eighth * recent
                bottom = own[8:]
                for k in range(1, 8):
                    recent_k = pltpu.roll(recent, k, 0)
                    top = top + before[k - 1] * recent_k
                    if k < 4:
                        top = top + beyond[k - 1] * pltpu.roll(older, k + 4, 0)
                        bottom = bottom + beyond[k - 1] * recent_k
                full = jnp.concatenate([top, bottom], 0)
                high = full.astype(BF16)
                split_high_ref[at, here] = high
                split_low_ref[at, here] = (full - high.astype(F32)).astype(BF16)
        return carry

    lax.fori_loop(0, samples // 256, group, 0)

    def transform(step, carry):
        at = pl.ds(pl.multiple_of(step * 256, 256), 256)
        high = split_high_ref[at, :]
        spectra = jnp.dot(high, high_ref[...], preferred_element_type=F32)
        spectra = spectra + jnp.dot(split_low_ref[at, :], high_ref[...], preferred_element_type=F32)
        spectra = spectra + jnp.dot(high, low_ref[...], preferred_element_type=F32)
        spectra = spectra.astype(BF16)
        for j in range(4):
            for q in range(2):
                to = pl.ds(pl.multiple_of((step * 2 + j // 2) * 128 + q * 64, 64), 64)
                table_ref[to, (j % 2) * 128 : (j % 2) * 128 + 128] = spectra[
                    j * 64 : (j + 1) * 64, q * 128 : (q + 1) * 128
                ]
        return carry

    lax.fori_loop(0, samples // 1024, transform, 0)

    def windows(step, carry):
        base = pl.multiple_of(base_ref[step], 16)
        member = member_ref[pl.ds(pl.multiple_of(step * rows_wide, 16), rows_wide), :]
        table = table_ref[pl.ds(pl.multiple_of(step * 128, 128), 128), :]
        picked = lax.dot_general(
            member, table, (((1,), (1,)), ((), ())), preferred_element_type=F32
        )
        window_ref[pl.ds(base, rows_wide), :] += picked
        return carry

    lax.fori_loop(0, samples // 512, windows, 0)
    fine = place_ref.shape[1]
    bins_ref[...] = window_ref[0:fine, :].astype(BF16)
    step_rows = 512

    def places(step, carry):
        at = pl.ds(pl.multiple_of(step * step_rows, step_rows), step_rows)
        out_ref[at, :] = jnp.dot(
            place_ref[at, :], bins_ref[...], preferred_element_type=F32
        ).astype(BF16)
        return carry

    lax.fori_loop(0, out_ref.shape[0] // step_rows, places, 0)


def unpack_kernel(received_ref, out_ref, copies_ref, wide_ref, *, pad, inputs_dev):
    fine_dev = out_ref.shape[0]
    rows, lanes = received_ref.shape
    devices = rows // pad
    blocks = lanes // (2 * inputs_dev)
    wide_ref[...] = received_ref[...].astype(F32)
    inputs = inputs_dev * devices
    source = lax.broadcasted_iota(jnp.int32, (inputs, inputs), 0)
    target = lax.broadcasted_iota(jnp.int32, (inputs, inputs), 1)
    spread = jnp.where((source % devices) * inputs_dev + source // devices == target, 1.0, 0.0)
    spread = spread.astype(BF16)
    pieces = []
    for channel in range(fine_dev):
        turned = wide_ref[pl.ds(channel, devices, stride=pad), :].T.astype(BF16)
        for q in range(2):
            pieces.append(
                jnp.concatenate(
                    [
                        turned[(q * inputs_dev + i) * blocks : (q * inputs_dev + i + 1) * blocks, :]
                        for i in range(inputs_dev)
                    ],
                    1,
                )
            )
    joined = jnp.concatenate(pieces, 0)
    placed = jnp.dot(joined, spread, preferred_element_type=F32).astype(BF16)
    placed = placed.reshape(out_ref.shape)
    out_ref[...] = placed
    for group in range(copies_ref.shape[0]):
        copies_ref[group] = placed


def correlate_kernel(mine_ref, all_ref, out_ref, *, scale):
    mine = pl.ds(pl.multiple_of(mine_ref[0], 128), 128)
    groups, _, rows, _ = all_ref.shape
    half = rows // 2
    step = out_ref.shape[0]
    for local_channel in range(step):
        channel = pl.program_id(0) * step + local_channel
        right = jnp.concatenate([all_ref[g, channel] for g in range(groups)], 0)
        real, imag = [], []
        for g in range(groups):
            block = all_ref[g, channel, :, mine]
            real.append(block)
            imag.append(block[half:])
            imag.append(-block[:half])
        left = jnp.concatenate([jnp.concatenate(real, 0), jnp.concatenate(imag, 0)], 1)
        product = lax.dot_general(
            left, right, (((0,), (0,)), ((), ())), preferred_element_type=F32
        )
        product = (product * scale).astype(BF16)
        out_ref[local_channel, 0] = product[:128]
        out_ref[local_channel, 1] = product[128:]


def window_rows(zoom_width, zoom_shift, phases):
    ends = jnp.cumsum(zoom_width)
    firsts = ends - zoom_width
    starts = zoom_shift % (phases - zoom_width + 1)
    bins = jnp.arange(phases, dtype=jnp.int32)[None, :] - starts[:, None]
    inside = (bins >= 0) & (bins < zoom_width[:, None])
    return firsts, jnp.where(inside, firsts[:, None] + bins, -1)


def own_part(voltage, fir_taps, zoom_width, zoom_shift, owner_slot, devices, pad):
    inputs_dev, blocks, samples = voltage.shape
    phases = fir_taps.shape[1]
    fine = owner_slot.shape[0]
    fine_dev = fine // devices
    firsts, krow = window_rows(zoom_width, zoom_shift, phases)
    groups = 256 // phases
    base = firsts[::groups] // 16 * 16
    slot = (owner_slot // fine_dev) * pad + owner_slot % fine_dev
    high, low = dft_weights(phases, 8)
    taps = jnp.tile(fir_taps, (1, 128 // phases))
    whole = pl.BlockSpec(memory_space=VMEM)
    filtered, member, place, high, low = pl.pallas_call(
        functools.partial(own_kernel, rows_wide=WIDE),
        out_shape=(
            jax.ShapeDtypeStruct((inputs_dev * blocks * samples // 256, 256), F32),
            jax.ShapeDtypeStruct((samples // 512 * WIDE, 256), BF16),
            jax.ShapeDtypeStruct((devices * pad, fine), BF16),
            jax.ShapeDtypeStruct(high.shape, BF16),
            jax.ShapeDtypeStruct(low.shape, BF16),
        ),
        in_specs=[pl.BlockSpec(memory_space=pltpu.SMEM)] + [whole] * 6,
        out_specs=(whole,) * 5,
        compiler_params=pltpu.CompilerParams(vmem_limit_bytes=LIMIT),
        cost_estimate=pl.CostEstimate(flops=20_000_000_000, bytes_accessed=12_000_000, transcendentals=0),
        name="own_part",
    )(
        base, voltage, taps, jnp.asarray(high), jnp.asarray(low),
        krow.reshape(samples // 512, 256), slot[None, :],
    )
    return base, taps, filtered, high, low, member, place


def channelize(parts, recent, older):
    base, taps, filtered, high, low, member, place = parts
    inputs_dev, _, samples = recent.shape
    slots, fine = place.shape
    lanes = filtered.shape[0] * 256 // samples * 2
    whole = pl.BlockSpec(memory_space=VMEM)
    return pl.pallas_call(
        functools.partial(channelize_kernel, rows_wide=WIDE),
        out_shape=jax.ShapeDtypeStruct((slots, lanes), BF16),
        in_specs=[pl.BlockSpec(memory_space=pltpu.SMEM)] + [whole] * 8,
        out_specs=whole,
        scratch_shapes=[
            pltpu.VMEM(filtered.shape, BF16),
            pltpu.VMEM(filtered.shape, BF16),
            pltpu.VMEM((samples // 512 * 128, 256), BF16),
            pltpu.VMEM((fine + 256, 128), F32),
            pltpu.VMEM((fine, 128), BF16),
        ],
        compiler_params=pltpu.CompilerParams(vmem_limit_bytes=LIMIT),
        name="channelize",
    )(base, filtered, recent, older, taps, high, low, member, place)


def unpack(received, fine_dev, inputs_dev, pad, groups):
    rows, lanes = received.shape
    devices = rows // pad
    blocks = lanes // (2 * inputs_dev)
    whole = pl.BlockSpec(memory_space=VMEM)
    shape = (fine_dev, 2 * blocks, devices * inputs_dev)
    return pl.pallas_call(
        functools.partial(unpack_kernel, pad=pad, inputs_dev=inputs_dev),
        out_shape=(
            jax.ShapeDtypeStruct(shape, BF16),
            jax.ShapeDtypeStruct((groups,) + shape, BF16),
        ),
        in_specs=[whole],
        out_specs=(whole, whole),
        scratch_shapes=[pltpu.VMEM((rows, lanes), F32)],
        compiler_params=pltpu.CompilerParams(vmem_limit_bytes=LIMIT),
        name="unpack",
    )(received)


def correlate(gathered, mine, scale):
    _, fine_dev, _, inputs = gathered.shape
    step = 2
    return pl.pallas_call(
        functools.partial(correlate_kernel, scale=scale),
        out_shape=jax.ShapeDtypeStruct((fine_dev, 2, 128, inputs), BF16),
        grid=(fine_dev // step,),
        in_specs=[pl.BlockSpec(memory_space=pltpu.SMEM), pl.BlockSpec(memory_space=VMEM)],
        out_specs=pl.BlockSpec((step, 2, 128, inputs), lambda n: (n, 0, 0, 0)),
        compiler_params=pltpu.CompilerParams(vmem_limit_bytes=LIMIT),
        name="correlate",
    )(mine, gathered)


def local(voltage, fir_taps, zoom_width, zoom_shift, owner_slot):
    inputs_dev, blocks, samples = voltage.shape
    devices = lax.axis_size("chan")
    groups = lax.axis_size("tm")
    fine_dev = owner_slot.shape[0] // devices
    pad = 16
    up = [(i, i + 1) for i in range(groups - 1)]
    recent = lax.ppermute(voltage[:, blocks - 8 :, :], "tm", up)
    older = lax.ppermute(voltage[:, blocks - 12 : blocks - 8, :], "tm", up)
    parts = own_part(voltage, fir_taps, zoom_width, zoom_shift, owner_slot, devices, pad)
    sent = channelize(parts, recent, older)
    lanes = sent.shape[1]
    received = lax.all_to_all(
        sent.reshape(devices, pad, lanes), "chan", split_axis=0, concat_axis=0, tiled=True
    )
    own, copies = unpack(
        received.reshape(devices * pad, lanes), fine_dev, inputs_dev, pad, groups
    )
    gathered = lax.all_to_all(copies, "tm", split_axis=0, concat_axis=0, tiled=True)
    spectra = jnp.transpose(own.reshape(fine_dev, 2, blocks, own.shape[2]), (0, 2, 1, 3))
    mine = (lax.axis_index("tm") * 128).astype(jnp.int32)[None]
    summed = correlate(gathered, mine, 1.0 / (blocks * groups))
    return spectra, summed


def solution(mesh):
    return jax.shard_map(
        local,
        mesh=mesh,
        in_specs=(P("chan", "tm", None), P(), P(), P(), P()),
        out_specs=(P("chan", "tm", None, None), P("chan", None, "tm", None)),
        check_vma=False,
    )
```

```python
import functools

import jax
import jax.numpy as jnp
import ml_dtypes
import numpy as np
from jax import lax
from jax.experimental import pallas as pl
from jax.experimental.pallas import tpu as pltpu
from jax.sharding import PartitionSpec as P

VMEM = pltpu.VMEM
BF16 = jnp.bfloat16
F32 = jnp.float32
LIMIT = 32 * 1024 * 1024
WIDE = 272


def dft_weights(phases, coarse):
    rows = np.arange(phases)
    angle = (rows[:, None] * rows[None, :] % phases) * (2.0 * np.pi / phases)
    cosine = np.cos(angle) / np.sqrt(phases)
    sine = np.sin(angle) / np.sqrt(phases)
    table = np.stack([np.stack([cosine, -sine], 0), np.stack([sine, cosine], 0)], 0)
    weights = np.einsum("pqjb,cd->cpjqdb", table, np.eye(coarse))
    weights = weights.reshape(coarse * 2 * phases, 2 * coarse * phases).astype(np.float32)
    high = weights.astype(ml_dtypes.bfloat16)
    low = (weights - high.astype(np.float32)).astype(ml_dtypes.bfloat16)
    return high, low


def tap_tables(taps_ref):
    row = lax.broadcasted_iota(jnp.int32, (8, 128), 0)
    tap = [jnp.broadcast_to(taps_ref[m : m + 1, :], (8, 128)) for m in range(taps_ref.shape[0])]
    zero = jnp.zeros((8, 128), F32)
    same = [jnp.where(row >= k, tap[k], zero) for k in range(1, 8)]
    beyond = [jnp.where(row < k, tap[8 + k], zero) for k in range(1, 4)]
    before = [jnp.where(row < k, tap[k], tap[8 + k] if k < 4 else zero) for k in range(1, 8)]
    return tap[0], tap[8], same, before, beyond


def own_kernel(
    base_ref, voltage_ref, taps_ref, high_ref, low_ref, krow_ref, slot_ref,
    filtered_ref, member_ref, place_ref, high_out_ref, low_out_ref, *, rows_wide,
):
    inputs, blocks, samples = voltage_ref.shape
    lanes = 128
    first, eighth, same, before, beyond = tap_tables(taps_ref)

    def group(step, carry):
        for i in range(inputs):
            for sub in range(2):
                spot = pl.ds(pl.multiple_of(step * 256 + sub * lanes, lanes), lanes)
                series = voltage_ref[i, :, spot].astype(F32)
                early, late = series[:8], series[8:]
                top = first * early
                bottom = first * late + eighth * early
                for k in range(1, 8):
                    early_k = pltpu.roll(early, k, 0)
                    top = top + same[k - 1] * early_k
                    bottom = bottom + before[k - 1] * early_k
                    bottom = bottom + same[k - 1] * pltpu.roll(late, k, 0)
                at = pl.ds(pl.multiple_of(step * 64 + i * blocks, blocks), blocks)
                filtered_ref[at, sub * lanes : (sub + 1) * lanes] = jnp.concatenate([top, bottom], 0)
        return carry

    lax.fori_loop(0, samples // 256, group, 0)

    def windows(step, carry):
        row = lax.broadcasted_iota(jnp.int32, (rows_wide, 256), 0) + base_ref[step]
        at = pl.ds(pl.multiple_of(step * rows_wide, 16), rows_wide)
        member_ref[at, :] = jnp.where(row == krow_ref[pl.ds(step, 1), :], 1.0, 0.0).astype(BF16)
        return carry

    lax.fori_loop(0, samples // 512, windows, 0)
    rows = 64
    fine = slot_ref.shape[1]

    def places(step, carry):
        at = pl.multiple_of(step * rows, rows)
        row = lax.broadcasted_iota(jnp.int32, (rows, fine), 0) + at
        place_ref[pl.ds(at, rows), :] = jnp.where(row == slot_ref[...], 1.0, 0.0).astype(BF16)
        return carry

    lax.fori_loop(0, place_ref.shape[0] // rows, places, 0)
    high_out_ref[...] = high_ref[...]
    low_out_ref[...] = low_ref[...]


def channelize_kernel(
    base_ref, filtered_ref, recent_ref, older_ref, taps_ref, high_ref, low_ref, member_ref, place_ref,
    out_ref, split_high_ref, split_low_ref, table_ref, window_ref, bins_ref, *, rows_wide,
):
    inputs, _, samples = recent_ref.shape
    blocks = 16
    lanes = 128
    _, eighth, _, before, beyond = tap_tables(taps_ref)
    window_ref[...] = jnp.zeros(window_ref.shape, F32)

    def group(step, carry):
        for i in range(inputs):
            for sub in range(2):
                spot = pl.ds(pl.multiple_of(step * 256 + sub * lanes, lanes), lanes)
                at = pl.ds(pl.multiple_of(step * 64 + i * blocks, blocks), blocks)
                here = slice(sub * lanes, (sub + 1) * lanes)
                own = filtered_ref[at, here]
                recent = recent_ref[i, :, spot].astype(F32)
                older = older_ref[i, :, spot].astype(F32)
                older = jnp.concatenate([older, jnp.zeros((8 - older.shape[0], lanes), F32)], 0)
                top = own[:8] + eighth * recent
                bottom = own[8:]
                for k in range(1, 8):
                    recent_k = pltpu.roll(recent, k, 0)
                    top = top + before[k - 1] * recent_k
                    if k < 4:
                        top = top + beyond[k - 1] * pltpu.roll(older, k + 4, 0)
                        bottom = bottom + beyond[k - 1] * recent_k
                full = jnp.concatenate([top, bottom], 0)
                high = full.astype(BF16)
                split_high_ref[at, here] = high
                split_low_ref[at, here] = (full - high.astype(F32)).astype(BF16)
        return carry

    lax.fori_loop(0, samples // 256, group, 0)

    weights = jnp.concatenate([high_ref[...], high_ref[...], low_ref[...]], 0)
    for step in range(samples // 1024):
        at = slice(step * 256, step * 256 + 256)
        high = split_high_ref[at, :]
        split = jnp.concatenate([high, split_low_ref[at, :], high], 1)
        spectra = jnp.dot(split, weights, preferred_element_type=F32).astype(BF16)
        for j in range(4):
            for q in range(2):
                to = (step * 2 + j // 2) * 128 + q * 64
                table_ref[to : to + 64, (j % 2) * 128 : (j % 2) * 128 + 128] = spectra[
                    j * 64 : (j + 1) * 64, q * 128 : (q + 1) * 128
                ]

    for step in range(samples // 512):
        base = pl.multiple_of(base_ref[step], 16)
        picked = lax.dot_general(
            member_ref[step * rows_wide : (step + 1) * rows_wide, :],
            table_ref[step * 128 : (step + 1) * 128, :],
            (((1,), (1,)), ((), ())),
            preferred_element_type=F32,
        )
        window_ref[pl.ds(base, rows_wide), :] += picked

    fine = place_ref.shape[1]
    bins_ref[...] = window_ref[0:fine, :].astype(BF16)
    step_rows = 512
    for step in range(out_ref.shape[0] // step_rows):
        at = slice(step * step_rows, (step + 1) * step_rows)
        out_ref[at, :] = jnp.dot(
            place_ref[at, :], bins_ref[...], preferred_element_type=F32
        ).astype(BF16)


def unpack_kernel(received_ref, first_ref, second_ref, wide_ref, *, pad, inputs_dev):
    fine_dev = first_ref.shape[0] + second_ref.shape[0]
    rows, lanes = received_ref.shape
    devices = rows // pad
    blocks = lanes // (2 * inputs_dev)
    wide_ref[...] = received_ref[...].astype(F32)
    inputs = inputs_dev * devices
    source = lax.broadcasted_iota(jnp.int32, (inputs, inputs), 0)
    target = lax.broadcasted_iota(jnp.int32, (inputs, inputs), 1)
    spread = jnp.where((source % devices) * inputs_dev + source // devices == target, 1.0, 0.0)
    spread = spread.astype(BF16)
    pieces = []
    for channel in range(fine_dev):
        turned = wide_ref[pl.ds(channel, devices, stride=pad), :].T.astype(BF16)
        for q in range(2):
            pieces.append(
                jnp.concatenate(
                    [
                        turned[(q * inputs_dev + i) * blocks : (q * inputs_dev + i + 1) * blocks, :]
                        for i in range(inputs_dev)
                    ],
                    1,
                )
            )
    joined = jnp.concatenate(pieces, 0)
    placed = jnp.dot(joined, spread, preferred_element_type=F32).astype(BF16)
    placed = placed.reshape((fine_dev,) + first_ref.shape[1:])
    first_ref[...] = placed[: first_ref.shape[0]]
    second_ref[...] = placed[first_ref.shape[0] :]


def correlate_kernel(mine_ref, own_ref, up_ref, down_ref, across_ref, *rest, scale, part):
    out_ref, block_ref, sems = rest[-3:]
    mine = pl.ds(pl.multiple_of(mine_ref[0], 128), 128)
    refs = (own_ref, up_ref, down_ref, across_ref)
    half = own_ref.shape[1] // 2
    fine_half = own_ref.shape[0]
    copies = []
    for channel in range(fine_half):
        right = jnp.concatenate([ref[channel] for ref in refs], 0)
        real, imag = [], []
        for ref in refs:
            block = ref[channel, :, mine]
            real.append(block)
            imag.append(block[half:])
            imag.append(-block[:half])
        left = jnp.concatenate([jnp.concatenate(real, 0), jnp.concatenate(imag, 0)], 1)
        product = lax.dot_general(
            left, right, (((0,), (0,)), ((), ())), preferred_element_type=F32
        )
        product = (product * scale).astype(BF16)
        block_ref[channel, 0] = product[:128]
        block_ref[channel, 1] = product[128:]
        copies.append(
            pltpu.make_async_copy(
                block_ref.at[channel], out_ref.at[part * fine_half + channel], sems.at[channel]
            )
        )
        copies[-1].start()
    for copy in copies:
        copy.wait()


def window_rows(zoom_width, zoom_shift, phases):
    ends = jnp.cumsum(zoom_width)
    firsts = ends - zoom_width
    starts = zoom_shift % (phases - zoom_width + 1)
    bins = jnp.arange(phases, dtype=jnp.int32)[None, :] - starts[:, None]
    inside = (bins >= 0) & (bins < zoom_width[:, None])
    return firsts, jnp.where(inside, firsts[:, None] + bins, -1)


def own_part(voltage, fir_taps, zoom_width, zoom_shift, owner_slot, devices, pad):
    inputs_dev, blocks, samples = voltage.shape
    phases = fir_taps.shape[1]
    fine = owner_slot.shape[0]
    fine_dev = fine // devices
    firsts, krow = window_rows(zoom_width, zoom_shift, phases)
    groups = 256 // phases
    base = firsts[::groups] // 16 * 16
    slot = (owner_slot // fine_dev) * pad + owner_slot % fine_dev
    high, low = dft_weights(phases, 8)
    taps = jnp.tile(fir_taps, (1, 128 // phases))
    whole = pl.BlockSpec(memory_space=VMEM)
    filtered, member, place, high, low = pl.pallas_call(
        functools.partial(own_kernel, rows_wide=WIDE),
        out_shape=(
            jax.ShapeDtypeStruct((inputs_dev * blocks * samples // 256, 256), F32),
            jax.ShapeDtypeStruct((samples // 512 * WIDE, 256), BF16),
            jax.ShapeDtypeStruct((devices * pad, fine), BF16),
            jax.ShapeDtypeStruct(high.shape, BF16),
            jax.ShapeDtypeStruct(low.shape, BF16),
        ),
        in_specs=[pl.BlockSpec(memory_space=pltpu.SMEM)] + [whole] * 6,
        out_specs=(whole,) * 5,
        compiler_params=pltpu.CompilerParams(vmem_limit_bytes=LIMIT),
        cost_estimate=pl.CostEstimate(flops=20_000_000_000, bytes_accessed=12_000_000, transcendentals=0),
        name="own_part",
    )(
        base, voltage, taps, jnp.asarray(high), jnp.asarray(low),
        krow.reshape(samples // 512, 256), slot[None, :],
    )
    return base, taps, filtered, high, low, member, place


def channelize(parts, recent, older):
    base, taps, filtered, high, low, member, place = parts
    inputs_dev, _, samples = recent.shape
    slots, fine = place.shape
    lanes = filtered.shape[0] * 256 // samples * 2
    whole = pl.BlockSpec(memory_space=VMEM)
    return pl.pallas_call(
        functools.partial(channelize_kernel, rows_wide=WIDE),
        out_shape=jax.ShapeDtypeStruct((slots, lanes), BF16),
        in_specs=[pl.BlockSpec(memory_space=pltpu.SMEM)] + [whole] * 8,
        out_specs=whole,
        scratch_shapes=[
            pltpu.VMEM(filtered.shape, BF16),
            pltpu.VMEM(filtered.shape, BF16),
            pltpu.VMEM((samples // 512 * 128, 256), BF16),
            pltpu.VMEM((fine + 256, 128), F32),
            pltpu.VMEM((fine, 128), BF16),
        ],
        compiler_params=pltpu.CompilerParams(vmem_limit_bytes=LIMIT),
        name="channelize",
    )(base, filtered, recent, older, taps, high, low, member, place)


def unpack(received, fine_dev, inputs_dev, pad):
    rows, lanes = received.shape
    devices = rows // pad
    blocks = lanes // (2 * inputs_dev)
    whole = pl.BlockSpec(memory_space=VMEM)
    half = jax.ShapeDtypeStruct((fine_dev // 2, 2 * blocks, devices * inputs_dev), BF16)
    return pl.pallas_call(
        functools.partial(unpack_kernel, pad=pad, inputs_dev=inputs_dev),
        out_shape=(half, half),
        in_specs=[whole],
        out_specs=(whole, whole),
        scratch_shapes=[pltpu.VMEM((rows, lanes), F32)],
        compiler_params=pltpu.CompilerParams(vmem_limit_bytes=LIMIT),
        name="unpack",
    )(received)


def correlate(parts, mine, scale, part, earlier=None):
    fine_half, rows, inputs = parts[0].shape
    whole = pl.BlockSpec(memory_space=VMEM)
    apart = pl.BlockSpec(memory_space=pl.ANY)
    held = [] if earlier is None else [earlier]
    return pl.pallas_call(
        functools.partial(correlate_kernel, scale=scale, part=part),
        out_shape=jax.ShapeDtypeStruct((2 * fine_half, 2, 128, inputs), BF16),
        in_specs=[pl.BlockSpec(memory_space=pltpu.SMEM)] + [whole] * 4 + [apart] * len(held),
        out_specs=apart,
        scratch_shapes=[
            pltpu.VMEM((fine_half, 2, 128, inputs), BF16),
            pltpu.SemaphoreType.DMA((fine_half,)),
        ],
        input_output_aliases={5: 0} if held else {},
        compiler_params=pltpu.CompilerParams(vmem_limit_bytes=LIMIT),
        cost_estimate=pl.CostEstimate(
            flops=2 * fine_half * 256 * inputs * 4 * rows,
            bytes_accessed=4_000_000,
            transcendentals=0,
        ),
        name="correlate",
    )(mine, *parts, *held)


def local(voltage, fir_taps, zoom_width, zoom_shift, owner_slot):
    inputs_dev, blocks, samples = voltage.shape
    devices = lax.axis_size("chan")
    groups = lax.axis_size("tm")
    fine_dev = owner_slot.shape[0] // devices
    pad = 16
    up = [(i, (i + 1) % groups) for i in range(groups)]
    down = [(i, (i - 1) % groups) for i in range(groups)]
    recent = lax.ppermute(voltage[:, blocks - 8 :, :], "tm", up[:-1])
    older = lax.ppermute(voltage[:, blocks - 12 : blocks - 8, :], "tm", up[:-1])
    parts = own_part(voltage, fir_taps, zoom_width, zoom_shift, owner_slot, devices, pad)
    sent = channelize(parts, recent, older)
    lanes = sent.shape[1]
    received = lax.all_to_all(
        sent.reshape(devices, pad, lanes), "chan", split_axis=0, concat_axis=0, tiled=True
    )
    own_a, own_b = unpack(received.reshape(devices * pad, lanes), fine_dev, inputs_dev, pad)
    up_a = lax.ppermute(own_a, "tm", up)
    down_b = lax.ppermute(own_b, "tm", down)
    up_b = lax.ppermute(own_b, "tm", up)
    down_a = lax.ppermute(own_a, "tm", down)
    across_a = lax.ppermute(up_a, "tm", up)
    across_b = lax.ppermute(down_b, "tm", down)
    mine = (lax.axis_index("tm") * 128).astype(jnp.int32)[None]
    scale = 1.0 / (blocks * groups)
    summed = correlate((own_a, up_a, down_a, across_a), mine, scale, 0)
    summed = correlate((own_b, up_b, down_b, across_b), mine, scale, 1, summed)
    own = jnp.concatenate([own_a, own_b], 0)
    spectra = jnp.transpose(own.reshape(fine_dev, 2, blocks, own.shape[2]), (0, 2, 1, 3))
    return spectra, summed


def solution(mesh):
    return jax.shard_map(
        local,
        mesh=mesh,
        in_specs=(P("chan", "tm", None), P(), P(), P(), P()),
        out_specs=(P("chan", "tm", None, None), P("chan", None, "tm", None)),
        check_vma=False,
    )
```

```python
import functools
import math

import jax
import jax.numpy as jnp
from jax import lax
from jax.experimental import pallas as pl
from jax.experimental.pallas import tpu as pltpu
from jax.sharding import PartitionSpec as P

VMEM = pltpu.VMEM
BF16 = jnp.bfloat16
F32 = jnp.float32
LIMIT = 32 * 1024 * 1024
MOST = 64 * 1000 * 1000
WIDE = 272


def dft_weights(phases, coarse):
    size = 2 * phases * coarse
    source = lax.broadcasted_iota(jnp.int32, (size, size), 0)
    target = lax.broadcasted_iota(jnp.int32, (size, size), 1)
    j, p, c = source % phases, (source // phases) % 2, source // (2 * phases)
    b, d, q = target % phases, (target // phases) % coarse, target // (phases * coarse)
    turn = (j * b + jnp.where(p == q, 0, jnp.where(q == 0, 3, 1) * phases // 4)) % phases
    angles = [2.0 * math.pi * k / phases for k in range(phases)]
    table = jnp.zeros((size, size), F32)
    for k, angle in enumerate(angles):
        exact = round(math.cos(angle), 15) / math.sqrt(phases)
        table = jnp.where(turn == k, jnp.float32(exact), table)
    return split_sum(jnp.where(c == d, table, 0.0))


def spread_taps(taps):
    phases = taps.shape[1]
    wide = jnp.concatenate([taps, jnp.zeros((taps.shape[0], 128 - phases), F32)], 1)
    while phases < 128:
        wide = wide + pltpu.roll(wide, phases, 1)
        phases *= 2
    return wide


def tap_tables(taps):
    row = lax.broadcasted_iota(jnp.int32, (8, 128), 0)
    tap = [jnp.broadcast_to(taps[m : m + 1, :], (8, 128)) for m in range(taps.shape[0])]
    zero = jnp.zeros((8, 128), F32)
    same = [jnp.where(row >= k, tap[k], zero) for k in range(1, 8)]
    beyond = [jnp.where(row < k, tap[8 + k], zero) for k in range(1, 4)]
    before = [jnp.where(row < k, tap[k], tap[8 + k] if k < 4 else zero) for k in range(1, 8)]
    return tap[0], tap[8], same, before, beyond


def split_sum(value):
    high = value.astype(BF16)
    return high, (value - high.astype(F32)).astype(BF16)


def fetch_voltage(voltage_ref, held_ref, sem):
    return pltpu.make_async_copy(voltage_ref, held_ref, sem)


def window_table(krow):
    row = lax.broadcasted_iota(jnp.int32, (WIDE, krow.shape[1]), 0)
    return jnp.where(row == krow, 1.0, 0.0).astype(BF16)


def tail_kernel(
    width_ref, shift_ref, voltage_ref, taps_ref,
    out_ref, rest_ref, base_ref,
    held_ref, member_ref, split_high_ref, split_low_ref, table_ref, window_ref, sem,
):
    inputs, _, samples = held_ref.shape
    fine = window_ref.shape[0] - 256
    lanes = 128
    phases = 16
    copy = fetch_voltage(voltage_ref, held_ref, sem)
    copy.start()
    lane = lax.broadcasted_iota(jnp.int32, (1, lanes), 1)
    place = lane // phases
    bins = lane % phases
    first = jnp.int32(0)
    bases = []
    for step in range(samples // 512):
        base = (first // 16) * 16
        base_ref[step] = base
        bases.append(base)
        rows = []
        for half in range(2):
            width = jnp.zeros((1, lanes), jnp.int32)
            shift = jnp.zeros((1, lanes), jnp.int32)
            begin = jnp.zeros((1, lanes), jnp.int32)
            for c in range(8):
                at = step * 16 + half * 8 + c
                here = place == c
                wide = width_ref[at]
                width = jnp.where(here, wide, width)
                shift = jnp.where(here, shift_ref[at], shift)
                begin = jnp.where(here, first, begin)
                first = first + wide
            room = (phases + 1 - width).astype(F32)
            whole = jnp.floor((shift.astype(F32) + 0.5) / room)
            start = shift - (whole * room).astype(jnp.int32)
            offset = bins - start
            inside = (offset >= 0) & (offset < width)
            rows.append(jnp.where(inside, begin + offset, -1))
        krow = jnp.concatenate(rows, 1) - base
        rest_ref[step : step + 1, :] = krow.astype(F32)
        member_ref[step * WIDE : (step + 1) * WIDE, :] = window_table(krow)

    taps = spread_taps(taps_ref[...])
    rest_ref[16 : 16 + taps.shape[0], 0:lanes] = taps
    _, eighth, _, before, beyond = tap_tables(taps)
    high_table, low_table = dft_weights(phases, 8)
    weights = jnp.concatenate([high_table, high_table, low_table], 0)
    window_ref[...] = jnp.zeros(window_ref.shape, F32)
    copy.wait()

    def group(step, carry):
        for sub in range(2):
            spot = pl.ds(pl.multiple_of(step * 256 + sub * lanes, lanes), lanes)
            tops, bottoms = [], []
            for i in range(inputs):
                series = held_ref[i, :, spot].astype(F32)
                older, recent = series[:8], series[8:]
                top = eighth * recent
                bottom = jnp.zeros((8, lanes), F32)
                for k in range(1, 8):
                    recent_k = pltpu.roll(recent, k, 0)
                    top = top + before[k - 1] * recent_k
                    if k < 4:
                        top = top + beyond[k - 1] * pltpu.roll(older, k, 0)
                        bottom = bottom + beyond[k - 1] * recent_k
                tops.append(top)
                bottoms.append(bottom if i % 2 == 0 else pltpu.roll(bottom, 4, 0))
            packed = [bottoms[i] + bottoms[i + 1] for i in range(0, inputs, 2)]
            high, low = split_sum(jnp.concatenate(tops + packed, 0))
            at = pl.ds(pl.multiple_of(step * 48, 16), 48)
            split_high_ref[at, sub * lanes : (sub + 1) * lanes] = high
            split_low_ref[at, sub * lanes : (sub + 1) * lanes] = low
        return carry

    lax.fori_loop(0, samples // 256, group, 0)
    for step in range(samples // 1024):
        at = slice(step * 192, step * 192 + 192)
        high = split_high_ref[at, :]
        split = jnp.concatenate([high, split_low_ref[at, :], high], 1)
        spectra = jnp.dot(split, weights, preferred_element_type=F32).astype(BF16)
        for j in range(4):
            for q in range(2):
                to = (step * 2 + j // 2) * 96
                half = slice((j % 2) * lanes, (j % 2 + 1) * lanes)
                piece = spectra[j * 48 : (j + 1) * 48, q * lanes : (q + 1) * lanes]
                table_ref[to + q * 32 : to + q * 32 + 32, half] = piece[:32]
                table_ref[to + 64 + q * 16 : to + 64 + q * 16 + 16, half] = piece[32:]
    for step in range(samples // 512):
        picked = lax.dot_general(
            member_ref[step * WIDE : (step + 1) * WIDE, :],
            table_ref[step * 96 : (step + 1) * 96, :],
            (((1,), (1,)), ((), ())),
            preferred_element_type=F32,
        )
        window_ref[pl.ds(pl.multiple_of(bases[step], 16), WIDE), 0:96] += picked
    half, quarter = fine // 2, fine // 4
    at = lax.broadcasted_iota(jnp.int32, (half, lanes), 1)
    out_ref[0:half, :] = jnp.where(
        at < 64, window_ref[0:half, :], pltpu.roll(window_ref[half:fine, :], 64, 1)
    ).astype(BF16)
    at = lax.broadcasted_iota(jnp.int32, (quarter, lanes), 1)
    packed = jnp.zeros((quarter, lanes), F32)
    for j in range(4):
        moved = pltpu.roll(window_ref[j * quarter : (j + 1) * quarter, :], (64 + j * 32) % lanes, 1)
        packed = jnp.where(at // 32 == j, moved, packed)
    out_ref[half : half + quarter, :] = packed.astype(BF16)


def own_kernel(
    base_ref, voltage_ref, rest_ref, slot_ref,
    window_ref, place_ref,
    held_ref, split_high_ref, split_low_ref, table_ref, sem,
):
    inputs, blocks, samples = held_ref.shape
    lanes = 128
    copy = fetch_voltage(voltage_ref, held_ref, sem)
    copy.start()
    window_ref[...] = jnp.zeros(window_ref.shape, F32)
    fine = slot_ref.shape[1]
    rows = 64

    def places(step, carry):
        at = pl.multiple_of(step * rows, rows)
        row = lax.broadcasted_iota(jnp.int32, (rows, fine), 0) + at
        place_ref[pl.ds(at, rows), :] = jnp.where(row == slot_ref[...], 1.0, 0.0).astype(BF16)
        return carry

    lax.fori_loop(0, place_ref.shape[0] // rows, places, 0)
    first, eighth, same, before, _ = tap_tables(rest_ref[16:28, 0:lanes])
    high_table, low_table = dft_weights(16, 8)
    weights = jnp.concatenate([high_table, high_table, low_table], 0)
    copy.wait()

    def group(step, carry):
        for i in range(inputs):
            for sub in range(2):
                spot = pl.ds(pl.multiple_of(step * 256 + sub * lanes, lanes), lanes)
                series = held_ref[i, :, spot].astype(F32)
                early, late = series[:8], series[8:]
                top = first * early
                bottom = first * late + eighth * early
                for k in range(1, 8):
                    early_k = pltpu.roll(early, k, 0)
                    top = top + same[k - 1] * early_k
                    bottom = bottom + before[k - 1] * early_k
                    bottom = bottom + same[k - 1] * pltpu.roll(late, k, 0)
                at = pl.ds(pl.multiple_of(step * 64 + i * blocks, blocks), blocks)
                high, low = split_sum(jnp.concatenate([top, bottom], 0))
                split_high_ref[at, sub * lanes : (sub + 1) * lanes] = high
                split_low_ref[at, sub * lanes : (sub + 1) * lanes] = low
        return carry

    lax.fori_loop(0, samples // 256, group, 0)
    for step in range(samples // 1024):
        at = slice(step * 256, step * 256 + 256)
        high = split_high_ref[at, :]
        split = jnp.concatenate([high, split_low_ref[at, :], high], 1)
        parts = split_sum(jnp.dot(split, weights, preferred_element_type=F32))
        for j in range(4):
            for q in range(2):
                for p in range(2):
                    to = (step * 2 + j // 2) * 256 + p * 128 + q * 64
                    table_ref[to : to + 64, (j % 2) * 128 : (j % 2) * 128 + 128] = parts[p][
                        j * 64 : (j + 1) * 64, q * 128 : (q + 1) * 128
                    ]
    for step in range(samples // 512):
        picked = lax.dot_general(
            window_table(rest_ref[step : step + 1, :].astype(jnp.int32)),
            table_ref[step * 256 : (step + 1) * 256, :],
            (((1,), (1,)), ((), ())),
            preferred_element_type=F32,
        )
        base = pl.multiple_of(base_ref[step], 16)
        window_ref[pl.ds(base, WIDE), :] += picked[:, :lanes] + picked[:, lanes:]


def send_kernel(window_ref, tail_ref, place_ref, out_ref, bins_ref):
    fine, lanes = bins_ref.shape
    half, quarter = fine // 2, fine // 4
    source = lax.broadcasted_iota(jnp.int32, (lanes, lanes), 0)
    target = lax.broadcasted_iota(jnp.int32, (lanes, lanes), 1)
    late = source - 64
    early_lane = (source // 8) * 16 + source % 8
    late_lane = (late // 4) * 16 + 8 + late % 4
    spread = jnp.where(
        ((source < 64) & (target == early_lane))
        | ((source >= 64) & (source < 96) & (late % 4 < 3) & (target == late_lane)),
        1.0,
        0.0,
    ).astype(BF16)
    at = lax.broadcasted_iota(jnp.int32, (quarter, lanes), 1)
    for j in range(4):
        rows = slice((j % 2) * quarter, (j % 2 + 1) * quarter)
        early = tail_ref[rows, :].astype(F32)
        if j >= 2:
            early = pltpu.roll(early, 64, 1)
        late = tail_ref[half : half + quarter, :].astype(F32)
        late = pltpu.roll(late, (64 - j * 32) % lanes, 1)
        tail = jnp.where(at < 64, early, late).astype(BF16)
        added = jnp.dot(tail, spread, preferred_element_type=F32)
        rows = slice(j * quarter, (j + 1) * quarter)
        bins_ref[rows, :] = (window_ref[rows, :] + added).astype(BF16)
    step_rows = 512
    for step in range(out_ref.shape[0] // step_rows):
        at = slice(step * step_rows, (step + 1) * step_rows)
        out_ref[at, :] = jnp.dot(
            place_ref[at, :], bins_ref[...], preferred_element_type=F32
        ).astype(BF16)


def unpack_kernel(received_ref, first_ref, second_ref, wide_ref, *, pad, inputs_dev):
    fine_dev = first_ref.shape[0] + second_ref.shape[0]
    rows, lanes = received_ref.shape
    devices = rows // pad
    blocks = lanes // (2 * inputs_dev)
    wide_ref[...] = received_ref[...].astype(F32)
    inputs = inputs_dev * devices
    source = lax.broadcasted_iota(jnp.int32, (inputs, inputs), 0)
    target = lax.broadcasted_iota(jnp.int32, (inputs, inputs), 1)
    spread = jnp.where((source % devices) * inputs_dev + source // devices == target, 1.0, 0.0)
    spread = spread.astype(BF16)
    pieces = []
    for channel in range(fine_dev):
        turned = wide_ref[pl.ds(channel, devices, stride=pad), :].T.astype(BF16)
        for q in range(2):
            pieces.append(
                jnp.concatenate(
                    [
                        turned[(q * inputs_dev + i) * blocks : (q * inputs_dev + i + 1) * blocks, :]
                        for i in range(inputs_dev)
                    ],
                    1,
                )
            )
    joined = jnp.concatenate(pieces, 0)
    placed = jnp.dot(joined, spread, preferred_element_type=F32).astype(BF16)
    placed = placed.reshape((fine_dev,) + first_ref.shape[1:])
    first_ref[...] = placed[: first_ref.shape[0]]
    second_ref[...] = placed[first_ref.shape[0] :]


def correlate_kernel(mine_ref, own_ref, up_ref, down_ref, across_ref, *rest, scale, part):
    out_ref, block_ref, sems = rest[-3:]
    mine = pl.ds(pl.multiple_of(mine_ref[0], 128), 128)
    refs = (own_ref, up_ref, down_ref, across_ref)
    half = own_ref.shape[1] // 2
    fine_half = own_ref.shape[0]
    copies = []
    for channel in range(fine_half):
        right = jnp.concatenate([ref[channel] for ref in refs], 0)
        real, imag = [], []
        for ref in refs:
            block = ref[channel, :, mine]
            real.append(block)
            imag.append(block[half:])
            imag.append(-block[:half])
        left = jnp.concatenate([jnp.concatenate(real, 0), jnp.concatenate(imag, 0)], 1)
        product = lax.dot_general(
            left, right, (((0,), (0,)), ((), ())), preferred_element_type=F32
        )
        product = (product * scale).astype(BF16)
        block_ref[channel, 0] = product[:128]
        block_ref[channel, 1] = product[128:]
        copies.append(
            pltpu.make_async_copy(
                block_ref.at[channel], out_ref.at[part * fine_half + channel], sems.at[channel]
            )
        )
        copies[-1].start()
    for copy in copies:
        copy.wait()


WHOLE = pl.BlockSpec(memory_space=VMEM)
SCALARS = pl.BlockSpec(memory_space=pltpu.SMEM)
APART = pl.BlockSpec(memory_space=pl.ANY)


def tail_part(voltage, fir_taps, zoom_width, zoom_shift, fine):
    inputs_dev, blocks, samples = voltage.shape
    groups = samples // 256
    return pl.pallas_call(
        tail_kernel,
        out_shape=(
            jax.ShapeDtypeStruct((fine // 2 + fine // 4, 128), BF16),
            jax.ShapeDtypeStruct((32, 256), F32),
            jax.ShapeDtypeStruct((samples // 512,), jnp.int32),
        ),
        in_specs=[SCALARS, SCALARS, APART, WHOLE],
        out_specs=(WHOLE, WHOLE, SCALARS),
        scratch_shapes=[
            pltpu.VMEM(voltage.shape, BF16),
            pltpu.VMEM((samples // 512 * WIDE, 256), BF16),
            pltpu.VMEM((groups * 48, 256), BF16),
            pltpu.VMEM((groups * 48, 256), BF16),
            pltpu.VMEM((groups * 48, 256), BF16),
            pltpu.VMEM((fine + 256, 128), F32),
            pltpu.SemaphoreType.DMA,
        ],
        compiler_params=pltpu.CompilerParams(vmem_limit_bytes=MOST),
        name="tail_part",
    )(zoom_width, zoom_shift, voltage, fir_taps)


def own_part(voltage, rest, base, slot, slots):
    inputs_dev, blocks, samples = voltage.shape
    groups = samples // 256
    fine = slot.shape[1]
    return pl.pallas_call(
        own_kernel,
        out_shape=(
            jax.ShapeDtypeStruct((fine + 256, 128), F32),
            jax.ShapeDtypeStruct((slots, fine), BF16),
        ),
        in_specs=[SCALARS, APART, WHOLE, WHOLE],
        out_specs=(WHOLE, WHOLE),
        scratch_shapes=[
            pltpu.VMEM(voltage.shape, BF16),
            pltpu.VMEM((groups * 64, 256), BF16),
            pltpu.VMEM((groups * 64, 256), BF16),
            pltpu.VMEM((groups * 128, 256), BF16),
            pltpu.SemaphoreType.DMA,
        ],
        compiler_params=pltpu.CompilerParams(vmem_limit_bytes=LIMIT),
        cost_estimate=pl.CostEstimate(flops=5_000_000_000, bytes_accessed=12_000_000, transcendentals=0),
        name="own_part",
    )(base, voltage, rest, slot)


def send_part(window, tail, place):
    slots, fine = place.shape
    return pl.pallas_call(
        send_kernel,
        out_shape=jax.ShapeDtypeStruct((slots, 128), BF16),
        in_specs=[WHOLE] * 3,
        out_specs=WHOLE,
        scratch_shapes=[pltpu.VMEM((fine, 128), BF16)],
        compiler_params=pltpu.CompilerParams(vmem_limit_bytes=LIMIT),
        name="send_part",
    )(window, tail, place)


def unpack(received, fine_dev, inputs_dev, pad):
    rows, lanes = received.shape
    devices = rows // pad
    blocks = lanes // (2 * inputs_dev)
    whole = pl.BlockSpec(memory_space=VMEM)
    half = jax.ShapeDtypeStruct((fine_dev // 2, 2 * blocks, devices * inputs_dev), BF16)
    return pl.pallas_call(
        functools.partial(unpack_kernel, pad=pad, inputs_dev=inputs_dev),
        out_shape=(half, half),
        in_specs=[whole],
        out_specs=(whole, whole),
        scratch_shapes=[pltpu.VMEM((rows, lanes), F32)],
        compiler_params=pltpu.CompilerParams(vmem_limit_bytes=LIMIT),
        name="unpack",
    )(received)


def correlate(parts, mine, scale, part, earlier=None):
    fine_half, rows, inputs = parts[0].shape
    whole = pl.BlockSpec(memory_space=VMEM)
    apart = pl.BlockSpec(memory_space=pl.ANY)
    held = [] if earlier is None else [earlier]
    return pl.pallas_call(
        functools.partial(correlate_kernel, scale=scale, part=part),
        out_shape=jax.ShapeDtypeStruct((2 * fine_half, 2, 128, inputs), BF16),
        in_specs=[pl.BlockSpec(memory_space=pltpu.SMEM)] + [whole] * 4 + [apart] * len(held),
        out_specs=apart,
        scratch_shapes=[
            pltpu.VMEM((fine_half, 2, 128, inputs), BF16),
            pltpu.SemaphoreType.DMA((fine_half,)),
        ],
        input_output_aliases={5: 0} if held else {},
        compiler_params=pltpu.CompilerParams(vmem_limit_bytes=LIMIT),
        cost_estimate=pl.CostEstimate(
            flops=2 * fine_half * 256 * inputs * 4 * rows,
            bytes_accessed=4_000_000,
            transcendentals=0,
        ),
        name="correlate",
    )(mine, *parts, *held)


def local(voltage, fir_taps, zoom_width, zoom_shift, owner_slot):
    inputs_dev, blocks, samples = voltage.shape
    devices = lax.axis_size("chan")
    groups = lax.axis_size("tm")
    fine_dev = owner_slot.shape[0] // devices
    pad = 16
    up = [(i, (i + 1) % groups) for i in range(groups)]
    down = [(i, (i - 1) % groups) for i in range(groups)]
    fine = owner_slot.shape[0]
    tail, rest, base = tail_part(voltage, fir_taps, zoom_width, zoom_shift, fine)
    tail = lax.ppermute(tail, "tm", up[:-1])
    slot = (owner_slot // fine_dev) * pad + owner_slot % fine_dev
    window, place = own_part(voltage, rest, base, slot[None, :], devices * pad)
    sent = send_part(window, tail, place)
    lanes = sent.shape[1]
    received = lax.all_to_all(
        sent.reshape(devices, pad, lanes), "chan", split_axis=0, concat_axis=0, tiled=True
    )
    own_a, own_b = unpack(received.reshape(devices * pad, lanes), fine_dev, inputs_dev, pad)
    up_a = lax.ppermute(own_a, "tm", up)
    down_b = lax.ppermute(own_b, "tm", down)
    up_b = lax.ppermute(own_b, "tm", up)
    down_a = lax.ppermute(own_a, "tm", down)
    across_a = lax.ppermute(up_a, "tm", up)
    across_b = lax.ppermute(down_b, "tm", down)
    mine = (lax.axis_index("tm") * 128).astype(jnp.int32)[None]
    scale = 1.0 / (blocks * groups)
    summed = correlate((own_a, up_a, down_a, across_a), mine, scale, 0)
    summed = correlate((own_b, up_b, down_b, across_b), mine, scale, 1, summed)
    own = jnp.concatenate([own_a, own_b], 0)
    spectra = jnp.transpose(own.reshape(fine_dev, 2, blocks, own.shape[2]), (0, 2, 1, 3))
    return spectra, summed


def solution(mesh):
    return jax.shard_map(
        local,
        mesh=mesh,
        in_specs=(P("chan", "tm", None), P(), P(), P(), P()),
        out_specs=(P("chan", "tm", None, None), P("chan", None, "tm", None)),
        check_vma=False,
    )
```

```python
import functools
import math

import jax
import jax.numpy as jnp
from jax import lax
from jax.experimental import pallas as pl
from jax.experimental.pallas import tpu as pltpu
from jax.sharding import PartitionSpec as P

VMEM = pltpu.VMEM
BF16 = jnp.bfloat16
F32 = jnp.float32
LIMIT = 32 * 1024 * 1024
MOST = 64 * 1000 * 1000
WIDE = 272


def dft_weights(phases, coarse):
    shape = (2 * phases, 2 * phases * coarse)
    source = lax.broadcasted_iota(jnp.int32, shape, 0)
    target = lax.broadcasted_iota(jnp.int32, shape, 1)
    j, p = source % phases, source // phases
    b, d, q = target % phases, (target // phases) % coarse, target // (phases * coarse)
    turn = (j * b + jnp.where(p == q, 0, jnp.where(q == 0, 3, 1) * phases // 4)) % phases
    table = jnp.zeros(shape, F32)
    for k in range(phases):
        exact = round(math.cos(2.0 * math.pi * k / phases), 15) / math.sqrt(phases)
        table = jnp.where(turn == k, jnp.float32(exact), table)
    return split_sum(jnp.concatenate([jnp.where(d == c, table, 0.0) for c in range(coarse)], 0))


def spread_taps(taps):
    phases = taps.shape[1]
    wide = jnp.concatenate([taps, jnp.zeros((taps.shape[0], 128 - phases), F32)], 1)
    while phases < 128:
        wide = wide + pltpu.roll(wide, phases, 1)
        phases *= 2
    return wide


def tap_tables(taps):
    row = lax.broadcasted_iota(jnp.int32, (8, 128), 0)
    tap = [jnp.broadcast_to(taps[m : m + 1, :], (8, 128)) for m in range(taps.shape[0])]
    zero = jnp.zeros((8, 128), F32)
    same = [jnp.where(row >= k, tap[k], zero) for k in range(1, 8)]
    beyond = [jnp.where(row < k, tap[8 + k], zero) for k in range(1, 4)]
    before = [jnp.where(row < k, tap[k], tap[8 + k] if k < 4 else zero) for k in range(1, 8)]
    return tap[0], tap[8], same, before, beyond


def split_sum(value):
    high = value.astype(BF16)
    return high, (value - high.astype(F32)).astype(BF16)


def fetch_voltage(voltage_ref, held_ref, sem):
    return pltpu.make_async_copy(voltage_ref, held_ref, sem)


def window_table(krow):
    row = lax.broadcasted_iota(jnp.int32, (WIDE, krow.shape[1]), 0)
    return jnp.where(row == krow, 1.0, 0.0).astype(BF16)


def tail_kernel(
    width_ref, shift_ref, voltage_ref, taps_ref,
    out_ref, rest_ref, base_ref,
    held_ref, member_ref, split_high_ref, split_low_ref, table_ref, window_ref, sem,
):
    inputs, _, samples = held_ref.shape
    fine = window_ref.shape[0] - 256
    lanes = 128
    phases = 16
    copy = fetch_voltage(voltage_ref, held_ref, sem)
    copy.start()
    lane = lax.broadcasted_iota(jnp.int32, (1, lanes), 1)
    place = lane // phases
    bins = lane % phases
    first = jnp.int32(0)
    bases = []
    for step in range(samples // 512):
        base = (first // 16) * 16
        base_ref[step] = base
        bases.append(base)
        rows = []
        for half in range(2):
            width = jnp.zeros((1, lanes), jnp.int32)
            shift = jnp.zeros((1, lanes), jnp.int32)
            begin = jnp.zeros((1, lanes), jnp.int32)
            for c in range(8):
                at = step * 16 + half * 8 + c
                here = place == c
                wide = width_ref[at]
                width = jnp.where(here, wide, width)
                shift = jnp.where(here, shift_ref[at], shift)
                begin = jnp.where(here, first, begin)
                first = first + wide
            room = (phases + 1 - width).astype(F32)
            whole = jnp.floor((shift.astype(F32) + 0.5) / room)
            start = shift - (whole * room).astype(jnp.int32)
            offset = bins - start
            inside = (offset >= 0) & (offset < width)
            rows.append(jnp.where(inside, begin + offset, -1))
        krow = jnp.concatenate(rows, 1) - base
        rest_ref[step : step + 1, :] = krow.astype(F32)
        member_ref[step * WIDE : (step + 1) * WIDE, :] = window_table(krow)

    taps = spread_taps(taps_ref[...])
    rest_ref[16 : 16 + taps.shape[0], 0:lanes] = taps
    _, eighth, _, before, beyond = tap_tables(taps)
    high_table, low_table = dft_weights(phases, 8)
    weights = jnp.concatenate([high_table, high_table, low_table], 0)
    window_ref[...] = jnp.zeros(window_ref.shape, F32)
    copy.wait()

    def group(step, carry):
        for sub in range(2):
            spot = pl.ds(pl.multiple_of(step * 256 + sub * lanes, lanes), lanes)
            tops, bottoms = [], []
            for i in range(inputs):
                series = held_ref[i, :, spot].astype(F32)
                older, recent = series[:8], series[8:]
                top = eighth * recent
                bottom = jnp.zeros((8, lanes), F32)
                for k in range(1, 8):
                    recent_k = pltpu.roll(recent, k, 0)
                    top = top + before[k - 1] * recent_k
                    if k < 4:
                        top = top + beyond[k - 1] * pltpu.roll(older, k, 0)
                        bottom = bottom + beyond[k - 1] * recent_k
                tops.append(top)
                bottoms.append(bottom if i % 2 == 0 else pltpu.roll(bottom, 4, 0))
            packed = [bottoms[i] + bottoms[i + 1] for i in range(0, inputs, 2)]
            high, low = split_sum(jnp.concatenate(tops + packed, 0))
            at = pl.ds(pl.multiple_of(step * 48, 16), 48)
            split_high_ref[at, sub * lanes : (sub + 1) * lanes] = high
            split_low_ref[at, sub * lanes : (sub + 1) * lanes] = low
        return carry

    lax.fori_loop(0, samples // 256, group, 0)
    for step in range(samples // 1024):
        at = slice(step * 192, step * 192 + 192)
        high = split_high_ref[at, :]
        split = jnp.concatenate([high, split_low_ref[at, :], high], 1)
        spectra = jnp.dot(split, weights, preferred_element_type=F32).astype(BF16)
        for j in range(4):
            for q in range(2):
                to = (step * 2 + j // 2) * 96
                half = slice((j % 2) * lanes, (j % 2 + 1) * lanes)
                piece = spectra[j * 48 : (j + 1) * 48, q * lanes : (q + 1) * lanes]
                table_ref[to + q * 32 : to + q * 32 + 32, half] = piece[:32]
                table_ref[to + 64 + q * 16 : to + 64 + q * 16 + 16, half] = piece[32:]
    for step in range(samples // 512):
        picked = lax.dot_general(
            member_ref[step * WIDE : (step + 1) * WIDE, :],
            table_ref[step * 96 : (step + 1) * 96, :],
            (((1,), (1,)), ((), ())),
            preferred_element_type=F32,
        )
        window_ref[pl.ds(pl.multiple_of(bases[step], 16), WIDE), 0:96] += picked
    half, quarter = fine // 2, fine // 4
    at = lax.broadcasted_iota(jnp.int32, (half, lanes), 1)
    out_ref[0:half, :] = jnp.where(
        at < 64, window_ref[0:half, :], pltpu.roll(window_ref[half:fine, :], 64, 1)
    ).astype(BF16)
    at = lax.broadcasted_iota(jnp.int32, (quarter, lanes), 1)
    packed = jnp.zeros((quarter, lanes), F32)
    for j in range(4):
        moved = pltpu.roll(window_ref[j * quarter : (j + 1) * quarter, :], (64 + j * 32) % lanes, 1)
        packed = jnp.where(at // 32 == j, moved, packed)
    out_ref[half : half + quarter, :] = packed.astype(BF16)


def own_kernel(
    base_ref, voltage_ref, rest_ref,
    window_ref,
    held_ref, split_high_ref, split_low_ref, table_ref, sem,
):
    inputs, blocks, samples = held_ref.shape
    lanes = 128
    copy = fetch_voltage(voltage_ref, held_ref, sem)
    copy.start()
    window_ref[...] = jnp.zeros(window_ref.shape, F32)
    first, eighth, same, before, _ = tap_tables(rest_ref[16:28, 0:lanes])
    high_table, low_table = dft_weights(16, 8)
    weights = jnp.concatenate([high_table, high_table, low_table], 0)
    copy.wait()

    def group(step, carry):
        for i in range(inputs):
            for sub in range(2):
                spot = pl.ds(pl.multiple_of(step * 256 + sub * lanes, lanes), lanes)
                series = held_ref[i, :, spot].astype(F32)
                early, late = series[:8], series[8:]
                top = first * early
                bottom = first * late + eighth * early
                for k in range(1, 8):
                    early_k = pltpu.roll(early, k, 0)
                    top = top + same[k - 1] * early_k
                    bottom = bottom + before[k - 1] * early_k
                    bottom = bottom + same[k - 1] * pltpu.roll(late, k, 0)
                at = pl.ds(pl.multiple_of(step * 64 + i * blocks, blocks), blocks)
                high, low = split_sum(jnp.concatenate([top, bottom], 0))
                split_high_ref[at, sub * lanes : (sub + 1) * lanes] = high
                split_low_ref[at, sub * lanes : (sub + 1) * lanes] = low
        return carry

    lax.fori_loop(0, samples // 256, group, 0)
    for step in range(samples // 1024):
        at = slice(step * 256, step * 256 + 256)
        high = split_high_ref[at, :]
        split = jnp.concatenate([high, split_low_ref[at, :], high], 1)
        parts = split_sum(jnp.dot(split, weights, preferred_element_type=F32))
        for j in range(4):
            for q in range(2):
                for p in range(2):
                    to = (step * 2 + j // 2) * 256 + p * 128 + q * 64
                    table_ref[to : to + 64, (j % 2) * 128 : (j % 2) * 128 + 128] = parts[p][
                        j * 64 : (j + 1) * 64, q * 128 : (q + 1) * 128
                    ]
    for step in range(samples // 512):
        picked = lax.dot_general(
            window_table(rest_ref[step : step + 1, :].astype(jnp.int32)),
            table_ref[step * 256 : (step + 1) * 256, :],
            (((1,), (1,)), ((), ())),
            preferred_element_type=F32,
        )
        base = pl.multiple_of(base_ref[step], 16)
        window_ref[pl.ds(base, WIDE), :] += picked[:, :lanes] + picked[:, lanes:]


def place_kernel(slot_ref, place_ref):
    fine = slot_ref.shape[1]
    rows = 16
    row = lax.broadcasted_iota(jnp.int32, (rows, fine), 0)
    slot = jnp.broadcast_to(slot_ref[...], (rows, fine))
    row, slot = row.astype(jnp.int16), slot.astype(jnp.int16)
    one, zero = jnp.ones((rows, fine), BF16), jnp.zeros((rows, fine), BF16)

    def places(step, carry):
        at = pl.multiple_of(step * rows, rows)
        here = row + at.astype(jnp.int16)
        place_ref[pl.ds(at, rows), :] = jnp.where(here == slot, one, zero)
        return carry

    lax.fori_loop(0, place_ref.shape[0] // rows, places, 0, unroll=4)


def send_kernel(window_ref, tail_ref, place_ref, out_ref, bins_ref):
    fine, lanes = bins_ref.shape
    half, quarter = fine // 2, fine // 4
    source = lax.broadcasted_iota(jnp.int32, (lanes, lanes), 0)
    target = lax.broadcasted_iota(jnp.int32, (lanes, lanes), 1)
    late = source - 64
    early_lane = (source // 8) * 16 + source % 8
    late_lane = (late // 4) * 16 + 8 + late % 4
    spread = jnp.where(
        ((source < 64) & (target == early_lane))
        | ((source >= 64) & (source < 96) & (late % 4 < 3) & (target == late_lane)),
        1.0,
        0.0,
    ).astype(BF16)
    at = lax.broadcasted_iota(jnp.int32, (quarter, lanes), 1)
    for j in range(4):
        rows = slice((j % 2) * quarter, (j % 2 + 1) * quarter)
        early = tail_ref[rows, :].astype(F32)
        if j >= 2:
            early = pltpu.roll(early, 64, 1)
        late = tail_ref[half : half + quarter, :].astype(F32)
        late = pltpu.roll(late, (64 - j * 32) % lanes, 1)
        tail = jnp.where(at < 64, early, late).astype(BF16)
        added = jnp.dot(tail, spread, preferred_element_type=F32)
        rows = slice(j * quarter, (j + 1) * quarter)
        bins_ref[rows, :] = (window_ref[rows, :] + added).astype(BF16)
    step_rows = 448
    for step in range(out_ref.shape[0] // step_rows):
        at = slice(step * step_rows, (step + 1) * step_rows)
        out_ref[at, :] = jnp.dot(
            place_ref[at, :], bins_ref[...], preferred_element_type=F32
        ).astype(BF16)


def unpack_kernel(received_ref, first_ref, second_ref, wide_ref, *, inputs_dev):
    fine_dev = first_ref.shape[0] + second_ref.shape[0]
    rows, lanes = received_ref.shape
    devices = rows // fine_dev
    blocks = lanes // (2 * inputs_dev)
    wide_ref[...] = received_ref[...].astype(F32)
    inputs = inputs_dev * devices
    source = lax.broadcasted_iota(jnp.int32, (inputs, inputs), 0)
    target = lax.broadcasted_iota(jnp.int32, (inputs, inputs), 1)
    spread = jnp.where((source % devices) * inputs_dev + source // devices == target, 1.0, 0.0)
    spread = spread.astype(BF16)
    pieces = []
    for channel in range(fine_dev):
        turned = wide_ref[pl.ds(channel, devices, stride=fine_dev), :].T.astype(BF16)
        for q in range(2):
            pieces.append(
                jnp.concatenate(
                    [
                        turned[(q * inputs_dev + i) * blocks : (q * inputs_dev + i + 1) * blocks, :]
                        for i in range(inputs_dev)
                    ],
                    1,
                )
            )
    joined = jnp.concatenate(pieces, 0)
    placed = jnp.dot(joined, spread, preferred_element_type=F32).astype(BF16)
    placed = placed.reshape((fine_dev,) + first_ref.shape[1:])
    first_ref[...] = placed[: first_ref.shape[0]]
    second_ref[...] = placed[first_ref.shape[0] :]


def correlate_kernel(mine_ref, own_ref, up_ref, down_ref, across_ref, *rest, scale, first):
    out_ref, block_ref, sems = rest[-3:]
    mine = pl.ds(pl.multiple_of(mine_ref[0], 128), 128)
    refs = (own_ref, up_ref, down_ref, across_ref)
    half = own_ref.shape[1] // 2
    fine_half = own_ref.shape[0]
    copies = []
    for channel in range(fine_half):
        right = jnp.concatenate([ref[channel] for ref in refs], 0)
        real, imag = [], []
        for ref in refs:
            block = ref[channel, :, mine]
            real.append(block)
            imag.append(block[half:])
            imag.append(-block[:half])
        left = jnp.concatenate([jnp.concatenate(real, 0), jnp.concatenate(imag, 0)], 1)
        product = lax.dot_general(
            left, right, (((0,), (0,)), ((), ())), preferred_element_type=F32
        )
        product = (product * scale).astype(BF16)
        block_ref[channel, 0] = product[:128]
        block_ref[channel, 1] = product[128:]
        copies.append(
            pltpu.make_async_copy(
                block_ref.at[channel], out_ref.at[first + channel], sems.at[channel]
            )
        )
        copies[-1].start()
    for copy in copies:
        copy.wait()


WHOLE = pl.BlockSpec(memory_space=VMEM)
SCALARS = pl.BlockSpec(memory_space=pltpu.SMEM)
APART = pl.BlockSpec(memory_space=pl.ANY)


def tail_part(voltage, fir_taps, zoom_width, zoom_shift, fine):
    inputs_dev, blocks, samples = voltage.shape
    groups = samples // 256
    return pl.pallas_call(
        tail_kernel,
        out_shape=(
            jax.ShapeDtypeStruct((fine // 2 + fine // 4, 128), BF16),
            jax.ShapeDtypeStruct((32, 256), F32),
            jax.ShapeDtypeStruct((samples // 512,), jnp.int32),
        ),
        in_specs=[SCALARS, SCALARS, APART, WHOLE],
        out_specs=(WHOLE, WHOLE, SCALARS),
        scratch_shapes=[
            pltpu.VMEM(voltage.shape, BF16),
            pltpu.VMEM((samples // 512 * WIDE, 256), BF16),
            pltpu.VMEM((groups * 48, 256), BF16),
            pltpu.VMEM((groups * 48, 256), BF16),
            pltpu.VMEM((groups * 48, 256), BF16),
            pltpu.VMEM((fine + 256, 128), F32),
            pltpu.SemaphoreType.DMA,
        ],
        compiler_params=pltpu.CompilerParams(vmem_limit_bytes=MOST),
        name="tail_part",
    )(zoom_width, zoom_shift, voltage, fir_taps)


def own_part(voltage, rest, base, fine):
    inputs_dev, blocks, samples = voltage.shape
    groups = samples // 256
    return pl.pallas_call(
        own_kernel,
        out_shape=jax.ShapeDtypeStruct((fine + 256, 128), F32),
        in_specs=[SCALARS, APART, WHOLE],
        out_specs=WHOLE,
        scratch_shapes=[
            pltpu.VMEM(voltage.shape, BF16),
            pltpu.VMEM((groups * 64, 256), BF16),
            pltpu.VMEM((groups * 64, 256), BF16),
            pltpu.VMEM((groups * 128, 256), BF16),
            pltpu.SemaphoreType.DMA,
        ],
        compiler_params=pltpu.CompilerParams(vmem_limit_bytes=MOST),
        cost_estimate=pl.CostEstimate(flops=5_000_000_000, bytes_accessed=4_000_000, transcendentals=0),
        name="own_part",
    )(base, voltage, rest)


def place_part(slot):
    fine = slot.shape[1]
    return pl.pallas_call(
        place_kernel,
        out_shape=jax.ShapeDtypeStruct((fine, fine), BF16),
        in_specs=[WHOLE],
        out_specs=WHOLE,
        compiler_params=pltpu.CompilerParams(vmem_limit_bytes=LIMIT),
        cost_estimate=pl.CostEstimate(flops=5_000_000_000, bytes_accessed=4_000_000, transcendentals=0),
        name="place_part",
    )(slot)


def send_part(window, tail, place):
    slots, fine = place.shape
    return pl.pallas_call(
        send_kernel,
        out_shape=jax.ShapeDtypeStruct((slots, 128), BF16),
        in_specs=[WHOLE] * 3,
        out_specs=WHOLE,
        scratch_shapes=[pltpu.VMEM((fine, 128), BF16)],
        compiler_params=pltpu.CompilerParams(vmem_limit_bytes=LIMIT),
        name="send_part",
    )(window, tail, place)


def unpack(received, fine_dev, inputs_dev):
    rows, lanes = received.shape
    devices = rows // fine_dev
    blocks = lanes // (2 * inputs_dev)
    whole = pl.BlockSpec(memory_space=VMEM)
    first = (fine_dev * 4 + 6) // 7
    shapes = [(first, 2 * blocks, devices * inputs_dev), (fine_dev - first, 2 * blocks, devices * inputs_dev)]
    return pl.pallas_call(
        functools.partial(unpack_kernel, inputs_dev=inputs_dev),
        out_shape=tuple(jax.ShapeDtypeStruct(shape, BF16) for shape in shapes),
        in_specs=[whole],
        out_specs=(whole, whole),
        scratch_shapes=[pltpu.VMEM((rows, lanes), F32)],
        compiler_params=pltpu.CompilerParams(vmem_limit_bytes=LIMIT),
        name="unpack",
    )(received)


def correlate(parts, mine, scale, first, fine_dev, earlier=None):
    fine_half, rows, inputs = parts[0].shape
    whole = pl.BlockSpec(memory_space=VMEM)
    apart = pl.BlockSpec(memory_space=pl.ANY)
    held = [] if earlier is None else [earlier]
    return pl.pallas_call(
        functools.partial(correlate_kernel, scale=scale, first=first),
        out_shape=jax.ShapeDtypeStruct((fine_dev, 2, 128, inputs), BF16),
        in_specs=[pl.BlockSpec(memory_space=pltpu.SMEM)] + [whole] * 4 + [apart] * len(held),
        out_specs=apart,
        scratch_shapes=[
            pltpu.VMEM((fine_half, 2, 128, inputs), BF16),
            pltpu.SemaphoreType.DMA((fine_half,)),
        ],
        input_output_aliases={5: 0} if held else {},
        compiler_params=pltpu.CompilerParams(vmem_limit_bytes=LIMIT),
        cost_estimate=pl.CostEstimate(
            flops=2 * fine_half * 256 * inputs * 4 * rows,
            bytes_accessed=4_000_000,
            transcendentals=0,
        ),
        name="correlate",
    )(mine, *parts, *held)


def local(voltage, fir_taps, zoom_width, zoom_shift, owner_slot):
    inputs_dev, blocks, samples = voltage.shape
    devices = lax.axis_size("chan")
    groups = lax.axis_size("tm")
    fine = owner_slot.shape[0]
    fine_dev = fine // devices
    up = [(i, (i + 1) % groups) for i in range(groups)]
    down = [(i, (i - 1) % groups) for i in range(groups)]
    tail, rest, base = tail_part(voltage, fir_taps, zoom_width, zoom_shift, fine)
    tail = lax.ppermute(tail, "tm", up[:-1])
    window = own_part(voltage, rest, base, fine)
    slot, window = lax.optimization_barrier((owner_slot, window))
    place = place_part(slot[None, :])
    sent = send_part(window, tail, place)
    lanes = sent.shape[1]
    received = lax.all_to_all(
        sent.reshape(devices, fine_dev // 2, 2, lanes), "chan", split_axis=0, concat_axis=0, tiled=True
    )
    own_a, own_b = unpack(received.reshape(fine, lanes), fine_dev, inputs_dev)
    up_a = lax.ppermute(own_a, "tm", up)
    down_b = lax.ppermute(own_b, "tm", down)
    up_b = lax.ppermute(own_b, "tm", up)
    down_a = lax.ppermute(own_a, "tm", down)
    across_a = lax.ppermute(up_a, "tm", up)
    onward, up_b = lax.optimization_barrier((down_b, up_b))
    across_b = lax.ppermute(onward, "tm", down)
    mine = (lax.axis_index("tm") * 128).astype(jnp.int32)[None]
    scale = 1.0 / (blocks * groups)
    summed = correlate((own_a, up_a, down_a, across_a), mine, scale, 0, fine_dev)
    summed = correlate(
        (own_b, up_b, onward, across_b), mine, scale, own_a.shape[0], fine_dev, summed
    )
    own = jnp.concatenate([own_a, own_b], 0)
    spectra = jnp.transpose(own.reshape(fine_dev, 2, blocks, own.shape[2]), (0, 2, 1, 3))
    return spectra, summed


def solution(mesh):
    return jax.shard_map(
        local,
        mesh=mesh,
        in_specs=(P("chan", "tm", None), P(), P(), P(), P()),
        out_specs=(P("chan", "tm", None, None), P("chan", None, "tm", None)),
        check_vma=False,
    )
```

```python
import functools
import math

import jax
import jax.numpy as jnp
from jax import lax
from jax.experimental import pallas as pl
from jax.experimental.pallas import tpu as pltpu
from jax.sharding import PartitionSpec as P

VMEM = pltpu.VMEM
BF16 = jnp.bfloat16
F32 = jnp.float32
LIMIT = 32 * 1024 * 1024
MOST = 64 * 1000 * 1000
WIDE = 272


def dft_weights(phases, coarse):
    shape = (2 * phases, 2 * phases * coarse)
    source = lax.broadcasted_iota(jnp.int32, shape, 0)
    target = lax.broadcasted_iota(jnp.int32, shape, 1)
    j, p = source % phases, source // phases
    b, d, q = target % phases, (target // phases) % coarse, target // (phases * coarse)
    turn = (j * b + jnp.where(p == q, 0, jnp.where(q == 0, 3, 1) * phases // 4)) % phases
    table = jnp.zeros(shape, F32)
    for k in range(phases):
        exact = round(math.cos(2.0 * math.pi * k / phases), 15) / math.sqrt(phases)
        table = jnp.where(turn == k, jnp.float32(exact), table)
    return split_sum(jnp.concatenate([jnp.where(d == c, table, 0.0) for c in range(coarse)], 0))


def spread_taps(taps):
    phases = taps.shape[1]
    wide = jnp.concatenate([taps, jnp.zeros((taps.shape[0], 128 - phases), F32)], 1)
    while phases < 128:
        wide = wide + pltpu.roll(wide, phases, 1)
        phases *= 2
    return wide


def tap_tables(taps):
    row = lax.broadcasted_iota(jnp.int32, (8, 128), 0)
    tap = [jnp.broadcast_to(taps[m : m + 1, :], (8, 128)) for m in range(taps.shape[0])]
    zero = jnp.zeros((8, 128), F32)
    same = [jnp.where(row >= k, tap[k], zero) for k in range(1, 8)]
    beyond = [jnp.where(row < k, tap[8 + k], zero) for k in range(1, 4)]
    before = [jnp.where(row < k, tap[k], tap[8 + k] if k < 4 else zero) for k in range(1, 8)]
    return tap[0], tap[8], same, before, beyond


def split_sum(value):
    high = value.astype(BF16)
    return high, (value - high.astype(F32)).astype(BF16)


def fetch_voltage(voltage_ref, held_ref, sem):
    return pltpu.make_async_copy(voltage_ref, held_ref, sem)


def window_table(krow):
    row = lax.broadcasted_iota(jnp.int32, (WIDE, krow.shape[1]), 0)
    return jnp.where(row == krow, 1.0, 0.0).astype(BF16)


def tail_kernel(
    width_ref, shift_ref, voltage_ref, taps_ref,
    out_ref, rest_ref, base_ref,
    held_ref, member_ref, split_high_ref, split_low_ref, table_ref, window_ref, sem,
):
    inputs, _, samples = held_ref.shape
    fine = window_ref.shape[0] - 256
    lanes = 128
    phases = 16
    copy = fetch_voltage(voltage_ref, held_ref, sem)
    copy.start()
    lane = lax.broadcasted_iota(jnp.int32, (1, lanes), 1)
    place = lane // phases
    bins = lane % phases
    first = jnp.int32(0)
    bases = []
    for step in range(samples // 512):
        base = (first // 16) * 16
        base_ref[step] = base
        bases.append(base)
        rows = []
        for half in range(2):
            width = jnp.zeros((1, lanes), jnp.int32)
            shift = jnp.zeros((1, lanes), jnp.int32)
            begin = jnp.zeros((1, lanes), jnp.int32)
            for c in range(8):
                at = step * 16 + half * 8 + c
                here = place == c
                wide = width_ref[at]
                width = jnp.where(here, wide, width)
                shift = jnp.where(here, shift_ref[at], shift)
                begin = jnp.where(here, first, begin)
                first = first + wide
            room = (phases + 1 - width).astype(F32)
            whole = jnp.floor((shift.astype(F32) + 0.5) / room)
            start = shift - (whole * room).astype(jnp.int32)
            offset = bins - start
            inside = (offset >= 0) & (offset < width)
            rows.append(jnp.where(inside, begin + offset, -1))
        krow = jnp.concatenate(rows, 1) - base
        rest_ref[step : step + 1, :] = krow.astype(F32)
        member_ref[step * WIDE : (step + 1) * WIDE, :] = window_table(krow)

    taps = spread_taps(taps_ref[...])
    rest_ref[16 : 16 + taps.shape[0], 0:lanes] = taps
    _, eighth, _, before, beyond = tap_tables(taps)
    high_table, low_table = dft_weights(phases, 8)
    weights = jnp.concatenate([high_table, high_table, low_table], 0)
    window_ref[...] = jnp.zeros(window_ref.shape, F32)
    copy.wait()

    def group(step, carry):
        for sub in range(2):
            spot = pl.ds(pl.multiple_of(step * 256 + sub * lanes, lanes), lanes)
            tops, bottoms = [], []
            for i in range(inputs):
                series = held_ref[i, :, spot].astype(F32)
                older, recent = series[:8], series[8:]
                top = eighth * recent
                bottom = jnp.zeros((8, lanes), F32)
                for k in range(1, 8):
                    recent_k = pltpu.roll(recent, k, 0)
                    top = top + before[k - 1] * recent_k
                    if k < 4:
                        top = top + beyond[k - 1] * pltpu.roll(older, k, 0)
                        bottom = bottom + beyond[k - 1] * recent_k
                tops.append(top)
                bottoms.append(bottom if i % 2 == 0 else pltpu.roll(bottom, 4, 0))
            packed = [bottoms[i] + bottoms[i + 1] for i in range(0, inputs, 2)]
            high, low = split_sum(jnp.concatenate(tops + packed, 0))
            at = pl.ds(pl.multiple_of(step * 48, 16), 48)
            split_high_ref[at, sub * lanes : (sub + 1) * lanes] = high
            split_low_ref[at, sub * lanes : (sub + 1) * lanes] = low
        return carry

    lax.fori_loop(0, samples // 256, group, 0)
    for step in range(samples // 1024):
        at = slice(step * 192, step * 192 + 192)
        high = split_high_ref[at, :]
        split = jnp.concatenate([high, split_low_ref[at, :], high], 1)
        spectra = jnp.dot(split, weights, preferred_element_type=F32).astype(BF16)
        for j in range(4):
            for q in range(2):
                to = (step * 2 + j // 2) * 96
                half = slice((j % 2) * lanes, (j % 2 + 1) * lanes)
                piece = spectra[j * 48 : (j + 1) * 48, q * lanes : (q + 1) * lanes]
                table_ref[to + q * 32 : to + q * 32 + 32, half] = piece[:32]
                table_ref[to + 64 + q * 16 : to + 64 + q * 16 + 16, half] = piece[32:]
    for step in range(samples // 512):
        picked = lax.dot_general(
            member_ref[step * WIDE : (step + 1) * WIDE, :],
            table_ref[step * 96 : (step + 1) * 96, :],
            (((1,), (1,)), ((), ())),
            preferred_element_type=F32,
        )
        window_ref[pl.ds(pl.multiple_of(bases[step], 16), WIDE), 0:96] += picked
    half, quarter = fine // 2, fine // 4
    at = lax.broadcasted_iota(jnp.int32, (half, lanes), 1)
    out_ref[0:half, :] = jnp.where(
        at < 64, window_ref[0:half, :], pltpu.roll(window_ref[half:fine, :], 64, 1)
    ).astype(BF16)
    at = lax.broadcasted_iota(jnp.int32, (quarter, lanes), 1)
    packed = jnp.zeros((quarter, lanes), F32)
    for j in range(4):
        moved = pltpu.roll(window_ref[j * quarter : (j + 1) * quarter, :], (64 + j * 32) % lanes, 1)
        packed = jnp.where(at // 32 == j, moved, packed)
    out_ref[half : half + quarter, :] = packed.astype(BF16)


def own_kernel(
    base_ref, voltage_ref, rest_ref,
    window_ref,
    held_ref, split_high_ref, split_low_ref, table_ref, sem,
):
    inputs, blocks, samples = held_ref.shape
    lanes = 128
    copy = fetch_voltage(voltage_ref, held_ref, sem)
    copy.start()
    window_ref[...] = jnp.zeros(window_ref.shape, F32)
    first, eighth, same, before, _ = tap_tables(rest_ref[16:28, 0:lanes])
    high_table, low_table = dft_weights(16, 8)
    weights = jnp.concatenate([high_table, high_table, low_table], 0)
    copy.wait()

    def group(step, carry):
        for i in range(inputs):
            for sub in range(2):
                spot = pl.ds(pl.multiple_of(step * 256 + sub * lanes, lanes), lanes)
                series = held_ref[i, :, spot].astype(F32)
                early, late = series[:8], series[8:]
                top = first * early
                bottom = first * late + eighth * early
                for k in range(1, 8):
                    early_k = pltpu.roll(early, k, 0)
                    top = top + same[k - 1] * early_k
                    bottom = bottom + before[k - 1] * early_k
                    bottom = bottom + same[k - 1] * pltpu.roll(late, k, 0)
                at = pl.ds(pl.multiple_of(step * 64 + i * blocks, blocks), blocks)
                high, low = split_sum(jnp.concatenate([top, bottom], 0))
                split_high_ref[at, sub * lanes : (sub + 1) * lanes] = high
                split_low_ref[at, sub * lanes : (sub + 1) * lanes] = low
        return carry

    lax.fori_loop(0, samples // 256, group, 0)
    for step in range(samples // 1024):
        at = slice(step * 256, step * 256 + 256)
        high = split_high_ref[at, :]
        split = jnp.concatenate([high, split_low_ref[at, :], high], 1)
        parts = split_sum(jnp.dot(split, weights, preferred_element_type=F32))
        for j in range(4):
            for q in range(2):
                for p in range(2):
                    to = (step * 2 + j // 2) * 256 + p * 128 + q * 64
                    table_ref[to : to + 64, (j % 2) * 128 : (j % 2) * 128 + 128] = parts[p][
                        j * 64 : (j + 1) * 64, q * 128 : (q + 1) * 128
                    ]
    for step in range(samples // 512):
        picked = lax.dot_general(
            window_table(rest_ref[step : step + 1, :].astype(jnp.int32)),
            table_ref[step * 256 : (step + 1) * 256, :],
            (((1,), (1,)), ((), ())),
            preferred_element_type=F32,
        )
        base = pl.multiple_of(base_ref[step], 16)
        window_ref[pl.ds(base, WIDE), :] += picked[:, :lanes] + picked[:, lanes:]


def place_kernel(slot_ref, place_ref):
    fine = slot_ref.shape[1]
    rows = 16
    row = lax.broadcasted_iota(jnp.int32, (rows, fine), 0)
    slot = jnp.broadcast_to(slot_ref[...], (rows, fine))
    row, slot = row.astype(jnp.int16), slot.astype(jnp.int16)
    one, zero = jnp.ones((rows, fine), BF16), jnp.zeros((rows, fine), BF16)

    def places(step, carry):
        at = pl.multiple_of(step * rows, rows)
        here = row + at.astype(jnp.int16)
        place_ref[pl.ds(at, rows), :] = jnp.where(here == slot, one, zero)
        return carry

    lax.fori_loop(0, place_ref.shape[0] // rows, places, 0, unroll=4)


def send_kernel(window_ref, tail_ref, place_ref, out_ref, bins_ref):
    fine, lanes = bins_ref.shape
    half, quarter = fine // 2, fine // 4
    source = lax.broadcasted_iota(jnp.int32, (lanes, lanes), 0)
    target = lax.broadcasted_iota(jnp.int32, (lanes, lanes), 1)
    late = source - 64
    early_lane = (source // 8) * 16 + source % 8
    late_lane = (late // 4) * 16 + 8 + late % 4
    spread = jnp.where(
        ((source < 64) & (target == early_lane))
        | ((source >= 64) & (source < 96) & (late % 4 < 3) & (target == late_lane)),
        1.0,
        0.0,
    ).astype(BF16)
    at = lax.broadcasted_iota(jnp.int32, (quarter, lanes), 1)
    for j in range(4):
        rows = slice((j % 2) * quarter, (j % 2 + 1) * quarter)
        early = tail_ref[rows, :].astype(F32)
        if j >= 2:
            early = pltpu.roll(early, 64, 1)
        late = tail_ref[half : half + quarter, :].astype(F32)
        late = pltpu.roll(late, (64 - j * 32) % lanes, 1)
        tail = jnp.where(at < 64, early, late).astype(BF16)
        added = jnp.dot(tail, spread, preferred_element_type=F32)
        rows = slice(j * quarter, (j + 1) * quarter)
        bins_ref[rows, :] = (window_ref[rows, :] + added).astype(BF16)
    step_rows = 448
    for step in range(out_ref.shape[0] // step_rows):
        at = slice(step * step_rows, (step + 1) * step_rows)
        out_ref[at, :] = jnp.dot(
            place_ref[at, :], bins_ref[...], preferred_element_type=F32
        ).astype(BF16)


def unpack_kernel(received_ref, out_ref, wide_ref, *, inputs_dev):
    fine_dev = out_ref.shape[0]
    rows, lanes = received_ref.shape
    devices = rows // fine_dev
    blocks = lanes // (2 * inputs_dev)
    wide_ref[...] = received_ref[...].astype(F32)
    inputs = inputs_dev * devices
    source = lax.broadcasted_iota(jnp.int32, (inputs, inputs), 0)
    target = lax.broadcasted_iota(jnp.int32, (inputs, inputs), 1)
    spread = jnp.where((source % devices) * inputs_dev + source // devices == target, 1.0, 0.0)
    spread = spread.astype(BF16)
    pieces = []
    for channel in range(fine_dev):
        turned = wide_ref[pl.ds(channel, devices, stride=fine_dev), :].T.astype(BF16)
        for q in range(2):
            pieces.append(
                jnp.concatenate(
                    [
                        turned[(q * inputs_dev + i) * blocks : (q * inputs_dev + i + 1) * blocks, :]
                        for i in range(inputs_dev)
                    ],
                    1,
                )
            )
    joined = jnp.concatenate(pieces, 0)
    placed = jnp.dot(joined, spread, preferred_element_type=F32).astype(BF16)
    out_ref[...] = placed.reshape(out_ref.shape)


def correlate_kernel(mine_ref, own_ref, ahead_ref, behind_ref, across_ref, *rest, scale, first):
    out_ref, block_ref, sems = rest[-3:]
    mine = pl.ds(pl.multiple_of(mine_ref[0], 128), 128)
    half = own_ref.shape[1] // 2
    copies = []
    for channel in range(across_ref.shape[0]):
        refs = [ref.at[first + channel] for ref in (own_ref, ahead_ref, behind_ref)]
        refs.append(across_ref.at[channel])
        right = jnp.concatenate([ref[...] for ref in refs], 0)
        real, imag = [], []
        for ref in refs:
            block = ref[:, mine]
            real.append(block)
            imag.append(block[half:])
            imag.append(-block[:half])
        left = jnp.concatenate([jnp.concatenate(real, 0), jnp.concatenate(imag, 0)], 1)
        product = lax.dot_general(
            left, right, (((0,), (0,)), ((), ())), preferred_element_type=F32
        )
        product = (product * scale).astype(BF16)
        block_ref[channel, 0] = product[:128]
        block_ref[channel, 1] = product[128:]
        copies.append(
            pltpu.make_async_copy(
                block_ref.at[channel], out_ref.at[first + channel], sems.at[channel]
            )
        )
        copies[-1].start()
    for copy in copies:
        copy.wait()


WHOLE = pl.BlockSpec(memory_space=VMEM)
SCALARS = pl.BlockSpec(memory_space=pltpu.SMEM)
APART = pl.BlockSpec(memory_space=pl.ANY)


def tail_part(voltage, fir_taps, zoom_width, zoom_shift, fine):
    inputs_dev, blocks, samples = voltage.shape
    groups = samples // 256
    return pl.pallas_call(
        tail_kernel,
        out_shape=(
            jax.ShapeDtypeStruct((fine // 2 + fine // 4, 128), BF16),
            jax.ShapeDtypeStruct((32, 256), F32),
            jax.ShapeDtypeStruct((samples // 512,), jnp.int32),
        ),
        in_specs=[SCALARS, SCALARS, APART, WHOLE],
        out_specs=(WHOLE, WHOLE, SCALARS),
        scratch_shapes=[
            pltpu.VMEM(voltage.shape, BF16),
            pltpu.VMEM((samples // 512 * WIDE, 256), BF16),
            pltpu.VMEM((groups * 48, 256), BF16),
            pltpu.VMEM((groups * 48, 256), BF16),
            pltpu.VMEM((groups * 48, 256), BF16),
            pltpu.VMEM((fine + 256, 128), F32),
            pltpu.SemaphoreType.DMA,
        ],
        compiler_params=pltpu.CompilerParams(vmem_limit_bytes=MOST),
        name="tail_part",
    )(zoom_width, zoom_shift, voltage, fir_taps)


def own_part(voltage, rest, base, fine):
    inputs_dev, blocks, samples = voltage.shape
    groups = samples // 256
    return pl.pallas_call(
        own_kernel,
        out_shape=jax.ShapeDtypeStruct((fine + 256, 128), F32),
        in_specs=[SCALARS, APART, WHOLE],
        out_specs=WHOLE,
        scratch_shapes=[
            pltpu.VMEM(voltage.shape, BF16),
            pltpu.VMEM((groups * 64, 256), BF16),
            pltpu.VMEM((groups * 64, 256), BF16),
            pltpu.VMEM((groups * 128, 256), BF16),
            pltpu.SemaphoreType.DMA,
        ],
        compiler_params=pltpu.CompilerParams(vmem_limit_bytes=MOST),
        cost_estimate=pl.CostEstimate(flops=5_000_000_000, bytes_accessed=4_000_000, transcendentals=0),
        name="own_part",
    )(base, voltage, rest)


def place_part(slot):
    fine = slot.shape[1]
    return pl.pallas_call(
        place_kernel,
        out_shape=jax.ShapeDtypeStruct((fine, fine), BF16),
        in_specs=[WHOLE],
        out_specs=WHOLE,
        compiler_params=pltpu.CompilerParams(vmem_limit_bytes=LIMIT),
        cost_estimate=pl.CostEstimate(flops=5_000_000_000, bytes_accessed=4_000_000, transcendentals=0),
        name="place_part",
    )(slot)


def send_part(window, tail, place):
    slots, fine = place.shape
    return pl.pallas_call(
        send_kernel,
        out_shape=jax.ShapeDtypeStruct((slots, 128), BF16),
        in_specs=[WHOLE] * 3,
        out_specs=WHOLE,
        scratch_shapes=[pltpu.VMEM((fine, 128), BF16)],
        compiler_params=pltpu.CompilerParams(vmem_limit_bytes=LIMIT),
        name="send_part",
    )(window, tail, place)


def unpack(received, fine_dev, inputs_dev):
    rows, lanes = received.shape
    devices = rows // fine_dev
    blocks = lanes // (2 * inputs_dev)
    whole = pl.BlockSpec(memory_space=VMEM)
    return pl.pallas_call(
        functools.partial(unpack_kernel, inputs_dev=inputs_dev),
        out_shape=jax.ShapeDtypeStruct((fine_dev, 2 * blocks, devices * inputs_dev), BF16),
        in_specs=[whole],
        out_specs=whole,
        scratch_shapes=[pltpu.VMEM((rows, lanes), F32)],
        compiler_params=pltpu.CompilerParams(vmem_limit_bytes=LIMIT),
        name="unpack",
    )(received)


def correlate(near, across, mine, scale, first, earlier=None):
    fine_dev, rows, inputs = near[0].shape
    fine_part = across.shape[0]
    whole = pl.BlockSpec(memory_space=VMEM)
    apart = pl.BlockSpec(memory_space=pl.ANY)
    held = [] if earlier is None else [earlier]
    return pl.pallas_call(
        functools.partial(correlate_kernel, scale=scale, first=first),
        out_shape=jax.ShapeDtypeStruct((fine_dev, 2, 128, inputs), BF16),
        in_specs=[pl.BlockSpec(memory_space=pltpu.SMEM)] + [whole] * 4 + [apart] * len(held),
        out_specs=apart,
        scratch_shapes=[
            pltpu.VMEM((fine_part, 2, 128, inputs), BF16),
            pltpu.SemaphoreType.DMA((fine_part,)),
        ],
        input_output_aliases={5: 0} if held else {},
        compiler_params=pltpu.CompilerParams(vmem_limit_bytes=LIMIT),
        cost_estimate=pl.CostEstimate(
            flops=2 * fine_part * 256 * inputs * 4 * rows,
            bytes_accessed=4_000_000,
            transcendentals=0,
        ),
        name="correlate",
    )(mine, *near, across, *held)


def local(voltage, fir_taps, zoom_width, zoom_shift, owner_slot):
    inputs_dev, blocks, samples = voltage.shape
    devices = lax.axis_size("chan")
    groups = lax.axis_size("tm")
    fine = owner_slot.shape[0]
    fine_dev = fine // devices
    up = [(i, i + 1) for i in range(groups - 1)]
    tail, rest, base = tail_part(voltage, fir_taps, zoom_width, zoom_shift, fine)
    tail = lax.ppermute(tail, "tm", up)
    window = own_part(voltage, rest, base, fine)
    slot, window = lax.optimization_barrier((owner_slot, window))
    place = place_part(slot[None, :])
    sent = send_part(window, tail, place)
    lanes = sent.shape[1]
    received = lax.all_to_all(
        sent.reshape(devices, fine_dev // 2, 2, lanes), "chan", split_axis=0, concat_axis=0, tiled=True
    )
    own = unpack(received.reshape(fine, lanes), fine_dev, inputs_dev)

    def around(turn):
        pairs = []
        for c in range(devices):
            for g in range(groups):
                to = (g + (turn if c % 2 == 0 else -turn)) % groups
                pairs.append((c * groups + g, c * groups + to))
        return pairs

    both = ("chan", "tm")
    ahead = lax.ppermute(own, both, around(1))
    behind = lax.ppermute(own, both, around(-1))
    first = fine_dev * 9 // 14
    across_a = lax.ppermute(ahead[:first], both, around(1))
    across_b = lax.ppermute(ahead[first:], both, around(1))
    mine = (lax.axis_index("tm") * 128).astype(jnp.int32)[None]
    scale = 1.0 / (blocks * groups)
    near = (own, ahead, behind)
    summed = correlate(near, across_a, mine, scale, 0)
    summed = correlate(near, across_b, mine, scale, first, summed)
    spectra = jnp.transpose(own.reshape(fine_dev, 2, blocks, own.shape[2]), (0, 2, 1, 3))
    return spectra, summed


def solution(mesh):
    return jax.shard_map(
        local,
        mesh=mesh,
        in_specs=(P("chan", "tm", None), P(), P(), P(), P()),
        out_specs=(P("chan", "tm", None, None), P("chan", None, "tm", None)),
        check_vma=False,
    )
```

```python
import functools
import math

import jax
import jax.numpy as jnp
from jax import lax
from jax.experimental import pallas as pl
from jax.experimental.pallas import tpu as pltpu
from jax.sharding import PartitionSpec as P

VMEM = pltpu.VMEM
BF16 = jnp.bfloat16
F32 = jnp.float32
LIMIT = 32 * 1024 * 1024
MOST = 64 * 1000 * 1000
WIDE = 272


def dft_weights(phases, coarse):
    shape = (2 * phases, 2 * phases * coarse)
    source = lax.broadcasted_iota(jnp.int32, shape, 0)
    target = lax.broadcasted_iota(jnp.int32, shape, 1)
    j, p = source % phases, source // phases
    b, d, q = target % phases, (target // phases) % coarse, target // (phases * coarse)
    turn = (j * b + jnp.where(p == q, 0, jnp.where(q == 0, 3, 1) * phases // 4)) % phases
    table = jnp.zeros(shape, F32)
    for k in range(phases):
        exact = round(math.cos(2.0 * math.pi * k / phases), 15) / math.sqrt(phases)
        table = jnp.where(turn == k, jnp.float32(exact), table)
    return split_sum(jnp.concatenate([jnp.where(d == c, table, 0.0) for c in range(coarse)], 0))


def spread_taps(taps):
    phases = taps.shape[1]
    wide = jnp.concatenate([taps, jnp.zeros((taps.shape[0], 128 - phases), F32)], 1)
    while phases < 128:
        wide = wide + pltpu.roll(wide, phases, 1)
        phases *= 2
    return wide


def tap_tables(taps):
    row = lax.broadcasted_iota(jnp.int32, (8, 128), 0)
    tap = [jnp.broadcast_to(taps[m : m + 1, :], (8, 128)) for m in range(taps.shape[0])]
    zero = jnp.zeros((8, 128), F32)
    same = [jnp.where(row >= k, tap[k], zero) for k in range(1, 8)]
    beyond = [jnp.where(row < k, tap[8 + k], zero) for k in range(1, 4)]
    before = [jnp.where(row < k, tap[k], tap[8 + k] if k < 4 else zero) for k in range(1, 8)]
    return tap[0], tap[8], same, before, beyond


def split_sum(value):
    high = value.astype(BF16)
    return high, (value - high.astype(F32)).astype(BF16)


def fetch_voltage(voltage_ref, held_ref, sem):
    return pltpu.make_async_copy(voltage_ref, held_ref, sem)


def window_table(krow):
    row = lax.broadcasted_iota(jnp.int32, (WIDE, krow.shape[1]), 0)
    return jnp.where(row == krow, 1.0, 0.0).astype(BF16)


def tail_kernel(
    width_ref, shift_ref, voltage_ref, taps_ref,
    out_ref, rest_ref, base_ref,
    held_ref, member_ref, split_high_ref, split_low_ref, table_ref, window_ref, sem,
):
    inputs, _, samples = held_ref.shape
    fine = window_ref.shape[0] - 256
    lanes = 128
    phases = 16
    copy = fetch_voltage(voltage_ref, held_ref, sem)
    copy.start()
    lane = lax.broadcasted_iota(jnp.int32, (1, lanes), 1)
    place = lane // phases
    bins = lane % phases
    first = jnp.int32(0)
    bases = []
    for step in range(samples // 512):
        base = (first // 16) * 16
        base_ref[step] = base
        bases.append(base)
        rows = []
        for half in range(2):
            width = jnp.zeros((1, lanes), jnp.int32)
            shift = jnp.zeros((1, lanes), jnp.int32)
            begin = jnp.zeros((1, lanes), jnp.int32)
            for c in range(8):
                at = step * 16 + half * 8 + c
                here = place == c
                wide = width_ref[at]
                width = jnp.where(here, wide, width)
                shift = jnp.where(here, shift_ref[at], shift)
                begin = jnp.where(here, first, begin)
                first = first + wide
            room = (phases + 1 - width).astype(F32)
            whole = jnp.floor((shift.astype(F32) + 0.5) / room)
            start = shift - (whole * room).astype(jnp.int32)
            offset = bins - start
            inside = (offset >= 0) & (offset < width)
            rows.append(jnp.where(inside, begin + offset, -1))
        krow = jnp.concatenate(rows, 1) - base
        rest_ref[step : step + 1, :] = krow.astype(F32)
        member_ref[step * WIDE : (step + 1) * WIDE, :] = window_table(krow)

    taps = spread_taps(taps_ref[...])
    rest_ref[16 : 16 + taps.shape[0], 0:lanes] = taps
    _, eighth, _, before, beyond = tap_tables(taps)
    high_table, low_table = dft_weights(phases, 8)
    weights = jnp.concatenate([high_table, high_table, low_table], 0)
    window_ref[...] = jnp.zeros(window_ref.shape, F32)
    copy.wait()

    def group(step, carry):
        for sub in range(2):
            spot = pl.ds(pl.multiple_of(step * 256 + sub * lanes, lanes), lanes)
            tops, bottoms = [], []
            for i in range(inputs):
                series = held_ref[i, :, spot].astype(F32)
                older, recent = series[:8], series[8:]
                top = eighth * recent
                bottom = jnp.zeros((8, lanes), F32)
                for k in range(1, 8):
                    recent_k = pltpu.roll(recent, k, 0)
                    top = top + before[k - 1] * recent_k
                    if k < 4:
                        top = top + beyond[k - 1] * pltpu.roll(older, k, 0)
                        bottom = bottom + beyond[k - 1] * recent_k
                tops.append(top)
                bottoms.append(bottom if i % 2 == 0 else pltpu.roll(bottom, 4, 0))
            packed = [bottoms[i] + bottoms[i + 1] for i in range(0, inputs, 2)]
            high, low = split_sum(jnp.concatenate(tops + packed, 0))
            at = pl.ds(pl.multiple_of(step * 48, 16), 48)
            split_high_ref[at, sub * lanes : (sub + 1) * lanes] = high
            split_low_ref[at, sub * lanes : (sub + 1) * lanes] = low
        return carry

    lax.fori_loop(0, samples // 256, group, 0)
    for step in range(samples // 1024):
        at = slice(step * 192, step * 192 + 192)
        high = split_high_ref[at, :]
        split = jnp.concatenate([high, split_low_ref[at, :], high], 1)
        spectra = jnp.dot(split, weights, preferred_element_type=F32).astype(BF16)
        for j in range(4):
            for q in range(2):
                to = (step * 2 + j // 2) * 96
                half = slice((j % 2) * lanes, (j % 2 + 1) * lanes)
                piece = spectra[j * 48 : (j + 1) * 48, q * lanes : (q + 1) * lanes]
                table_ref[to + q * 32 : to + q * 32 + 32, half] = piece[:32]
                table_ref[to + 64 + q * 16 : to + 64 + q * 16 + 16, half] = piece[32:]
    for step in range(samples // 512):
        picked = lax.dot_general(
            member_ref[step * WIDE : (step + 1) * WIDE, :],
            table_ref[step * 96 : (step + 1) * 96, :],
            (((1,), (1,)), ((), ())),
            preferred_element_type=F32,
        )
        window_ref[pl.ds(pl.multiple_of(bases[step], 16), WIDE), 0:96] += picked
    half, quarter = fine // 2, fine // 4
    at = lax.broadcasted_iota(jnp.int32, (half, lanes), 1)
    out_ref[0:half, :] = jnp.where(
        at < 64, window_ref[0:half, :], pltpu.roll(window_ref[half:fine, :], 64, 1)
    ).astype(BF16)
    at = lax.broadcasted_iota(jnp.int32, (quarter, lanes), 1)
    packed = jnp.zeros((quarter, lanes), F32)
    for j in range(4):
        moved = pltpu.roll(window_ref[j * quarter : (j + 1) * quarter, :], (64 + j * 32) % lanes, 1)
        packed = jnp.where(at // 32 == j, moved, packed)
    out_ref[half : half + quarter, :] = packed.astype(BF16)


def own_kernel(
    base_ref, voltage_ref, rest_ref,
    window_ref,
    held_ref, split_high_ref, split_low_ref, table_ref, sem,
):
    inputs, blocks, samples = held_ref.shape
    lanes = 128
    copy = fetch_voltage(voltage_ref, held_ref, sem)
    copy.start()
    window_ref[...] = jnp.zeros(window_ref.shape, F32)
    first, eighth, same, before, _ = tap_tables(rest_ref[16:28, 0:lanes])
    high_table, low_table = dft_weights(16, 8)
    weights = jnp.concatenate([high_table, high_table, low_table], 0)
    copy.wait()

    def group(step, carry):
        for i in range(inputs):
            for sub in range(2):
                spot = pl.ds(pl.multiple_of(step * 256 + sub * lanes, lanes), lanes)
                series = held_ref[i, :, spot].astype(F32)
                early, late = series[:8], series[8:]
                top = first * early
                bottom = first * late + eighth * early
                for k in range(1, 8):
                    early_k = pltpu.roll(early, k, 0)
                    top = top + same[k - 1] * early_k
                    bottom = bottom + before[k - 1] * early_k
                    bottom = bottom + same[k - 1] * pltpu.roll(late, k, 0)
                at = pl.ds(pl.multiple_of(step * 64 + i * blocks, blocks), blocks)
                high, low = split_sum(jnp.concatenate([top, bottom], 0))
                split_high_ref[at, sub * lanes : (sub + 1) * lanes] = high
                split_low_ref[at, sub * lanes : (sub + 1) * lanes] = low
        return carry

    lax.fori_loop(0, samples // 256, group, 0)
    for step in range(samples // 1024):
        at = slice(step * 256, step * 256 + 256)
        high = split_high_ref[at, :]
        split = jnp.concatenate([high, split_low_ref[at, :], high], 1)
        parts = split_sum(jnp.dot(split, weights, preferred_element_type=F32))
        for j in range(4):
            for q in range(2):
                for p in range(2):
                    to = (step * 2 + j // 2) * 256 + p * 128 + q * 64
                    table_ref[to : to + 64, (j % 2) * 128 : (j % 2) * 128 + 128] = parts[p][
                        j * 64 : (j + 1) * 64, q * 128 : (q + 1) * 128
                    ]
    for step in range(samples // 512):
        picked = lax.dot_general(
            window_table(rest_ref[step : step + 1, :].astype(jnp.int32)),
            table_ref[step * 256 : (step + 1) * 256, :],
            (((1,), (1,)), ((), ())),
            preferred_element_type=F32,
        )
        base = pl.multiple_of(base_ref[step], 16)
        window_ref[pl.ds(base, WIDE), :] += picked[:, :lanes] + picked[:, lanes:]


def place_kernel(slot_ref, place_ref):
    fine = slot_ref.shape[1]
    rows = 16
    row = lax.broadcasted_iota(jnp.int32, (rows, fine), 0)
    slot = jnp.broadcast_to(slot_ref[...], (rows, fine))
    row, slot = row.astype(jnp.int16), slot.astype(jnp.int16)
    one, zero = jnp.ones((rows, fine), BF16), jnp.zeros((rows, fine), BF16)

    def places(step, carry):
        at = pl.multiple_of(step * rows, rows)
        here = row + at.astype(jnp.int16)
        place_ref[pl.ds(at, rows), :] = jnp.where(here == slot, one, zero)
        return carry

    lax.fori_loop(0, place_ref.shape[0] // rows, places, 0, unroll=4)


def send_kernel(window_ref, tail_ref, place_ref, out_ref, bins_ref):
    fine, lanes = bins_ref.shape
    half, quarter = fine // 2, fine // 4
    source = lax.broadcasted_iota(jnp.int32, (lanes, lanes), 0)
    target = lax.broadcasted_iota(jnp.int32, (lanes, lanes), 1)
    late = source - 64
    early_lane = (source // 8) * 16 + source % 8
    late_lane = (late // 4) * 16 + 8 + late % 4
    spread = jnp.where(
        ((source < 64) & (target == early_lane))
        | ((source >= 64) & (source < 96) & (late % 4 < 3) & (target == late_lane)),
        1.0,
        0.0,
    ).astype(BF16)
    at = lax.broadcasted_iota(jnp.int32, (quarter, lanes), 1)
    for j in range(4):
        rows = slice((j % 2) * quarter, (j % 2 + 1) * quarter)
        early = tail_ref[rows, :].astype(F32)
        if j >= 2:
            early = pltpu.roll(early, 64, 1)
        late = tail_ref[half : half + quarter, :].astype(F32)
        late = pltpu.roll(late, (64 - j * 32) % lanes, 1)
        tail = jnp.where(at < 64, early, late).astype(BF16)
        added = jnp.dot(tail, spread, preferred_element_type=F32)
        rows = slice(j * quarter, (j + 1) * quarter)
        bins_ref[rows, :] = (window_ref[rows, :] + added).astype(BF16)
    step_rows = 448
    for step in range(out_ref.shape[0] // step_rows):
        at = slice(step * step_rows, (step + 1) * step_rows)
        out_ref[at, :] = jnp.dot(
            place_ref[at, :], bins_ref[...], preferred_element_type=F32
        ).astype(BF16)


def unpack_kernel(received_ref, out_ref, wide_ref, *, inputs_dev):
    fine_dev = out_ref.shape[0]
    rows, lanes = received_ref.shape
    devices = rows // fine_dev
    blocks = lanes // (2 * inputs_dev)
    wide_ref[...] = received_ref[...].astype(F32)
    inputs = inputs_dev * devices
    source = lax.broadcasted_iota(jnp.int32, (inputs, inputs), 0)
    target = lax.broadcasted_iota(jnp.int32, (inputs, inputs), 1)
    spread = jnp.where((source % devices) * inputs_dev + source // devices == target, 1.0, 0.0)
    spread = spread.astype(BF16)
    pieces = []
    for channel in range(fine_dev):
        turned = wide_ref[pl.ds(channel, devices, stride=fine_dev), :].T.astype(BF16)
        for q in range(2):
            pieces.append(
                jnp.concatenate(
                    [
                        turned[(q * inputs_dev + i) * blocks : (q * inputs_dev + i + 1) * blocks, :]
                        for i in range(inputs_dev)
                    ],
                    1,
                )
            )
    joined = jnp.concatenate(pieces, 0)
    placed = jnp.dot(joined, spread, preferred_element_type=F32).astype(BF16)
    out_ref[...] = placed.reshape(out_ref.shape)


def correlate_kernel(mine_ref, own_ref, ahead_ref, behind_ref, across_ref, *rest, scale, first):
    out_ref, block_ref, sems = rest[-3:]
    mine = pl.ds(pl.multiple_of(mine_ref[0], 128), 128)
    half = own_ref.shape[1] // 2
    copies = []
    for channel in range(across_ref.shape[0]):
        refs = [ref.at[first + channel] for ref in (own_ref, ahead_ref, behind_ref)]
        refs.append(across_ref.at[channel])
        right = jnp.concatenate([ref[...] for ref in refs], 0)
        real, imag = [], []
        for ref in refs:
            block = ref[:, mine]
            real.append(block)
            imag.append(block[half:])
            imag.append(-block[:half])
        left = jnp.concatenate([jnp.concatenate(real, 0), jnp.concatenate(imag, 0)], 1)
        product = lax.dot_general(
            left, right, (((0,), (0,)), ((), ())), preferred_element_type=F32
        )
        product = (product * scale).astype(BF16)
        block_ref[channel, 0] = product[:128]
        block_ref[channel, 1] = product[128:]
        copies.append(
            pltpu.make_async_copy(
                block_ref.at[channel], out_ref.at[first + channel], sems.at[channel]
            )
        )
        copies[-1].start()
    for copy in copies:
        copy.wait()


WHOLE = pl.BlockSpec(memory_space=VMEM)
SCALARS = pl.BlockSpec(memory_space=pltpu.SMEM)
APART = pl.BlockSpec(memory_space=pl.ANY)


def tail_part(voltage, fir_taps, zoom_width, zoom_shift, fine):
    inputs_dev, blocks, samples = voltage.shape
    groups = samples // 256
    return pl.pallas_call(
        tail_kernel,
        out_shape=(
            jax.ShapeDtypeStruct((fine // 2 + fine // 4, 128), BF16),
            jax.ShapeDtypeStruct((32, 256), F32),
            jax.ShapeDtypeStruct((samples // 512,), jnp.int32),
        ),
        in_specs=[SCALARS, SCALARS, APART, WHOLE],
        out_specs=(WHOLE, WHOLE, SCALARS),
        scratch_shapes=[
            pltpu.VMEM(voltage.shape, BF16),
            pltpu.VMEM((samples // 512 * WIDE, 256), BF16),
            pltpu.VMEM((groups * 48, 256), BF16),
            pltpu.VMEM((groups * 48, 256), BF16),
            pltpu.VMEM((groups * 48, 256), BF16),
            pltpu.VMEM((fine + 256, 128), F32),
            pltpu.SemaphoreType.DMA,
        ],
        compiler_params=pltpu.CompilerParams(vmem_limit_bytes=MOST),
        name="tail_part",
    )(zoom_width, zoom_shift, voltage, fir_taps)


def own_part(voltage, rest, base, fine):
    inputs_dev, blocks, samples = voltage.shape
    groups = samples // 256
    return pl.pallas_call(
        own_kernel,
        out_shape=jax.ShapeDtypeStruct((fine + 256, 128), F32),
        in_specs=[SCALARS, APART, WHOLE],
        out_specs=WHOLE,
        scratch_shapes=[
            pltpu.VMEM(voltage.shape, BF16),
            pltpu.VMEM((groups * 64, 256), BF16),
            pltpu.VMEM((groups * 64, 256), BF16),
            pltpu.VMEM((groups * 128, 256), BF16),
            pltpu.SemaphoreType.DMA,
        ],
        compiler_params=pltpu.CompilerParams(vmem_limit_bytes=MOST),
        cost_estimate=pl.CostEstimate(flops=5_000_000_000, bytes_accessed=4_000_000, transcendentals=0),
        name="own_part",
    )(base, voltage, rest)


def place_part(slot):
    fine = slot.shape[1]
    return pl.pallas_call(
        place_kernel,
        out_shape=jax.ShapeDtypeStruct((fine, fine), BF16),
        in_specs=[WHOLE],
        out_specs=WHOLE,
        compiler_params=pltpu.CompilerParams(vmem_limit_bytes=LIMIT),
        cost_estimate=pl.CostEstimate(flops=5_000_000_000, bytes_accessed=4_000_000, transcendentals=0),
        name="place_part",
    )(slot)


def send_part(window, tail, place):
    slots, fine = place.shape
    return pl.pallas_call(
        send_kernel,
        out_shape=jax.ShapeDtypeStruct((slots, 128), BF16),
        in_specs=[WHOLE] * 3,
        out_specs=WHOLE,
        scratch_shapes=[pltpu.VMEM((fine, 128), BF16)],
        compiler_params=pltpu.CompilerParams(vmem_limit_bytes=LIMIT),
        name="send_part",
    )(window, tail, place)


def unpack(received, fine_dev, inputs_dev):
    rows, lanes = received.shape
    devices = rows // fine_dev
    blocks = lanes // (2 * inputs_dev)
    whole = pl.BlockSpec(memory_space=VMEM)
    return pl.pallas_call(
        functools.partial(unpack_kernel, inputs_dev=inputs_dev),
        out_shape=jax.ShapeDtypeStruct((fine_dev, 2 * blocks, devices * inputs_dev), BF16),
        in_specs=[whole],
        out_specs=whole,
        scratch_shapes=[pltpu.VMEM((rows, lanes), F32)],
        compiler_params=pltpu.CompilerParams(vmem_limit_bytes=LIMIT),
        name="unpack",
    )(received)


def correlate(near, across, mine, scale, first, earlier=None):
    fine_dev, rows, inputs = near[0].shape
    fine_part = across.shape[0]
    whole = pl.BlockSpec(memory_space=VMEM)
    apart = pl.BlockSpec(memory_space=pl.ANY)
    held = [] if earlier is None else [earlier]
    return pl.pallas_call(
        functools.partial(correlate_kernel, scale=scale, first=first),
        out_shape=jax.ShapeDtypeStruct((fine_dev, 2, 128, inputs), BF16),
        in_specs=[pl.BlockSpec(memory_space=pltpu.SMEM)] + [whole] * 4 + [apart] * len(held),
        out_specs=apart,
        scratch_shapes=[
            pltpu.VMEM((fine_part, 2, 128, inputs), BF16),
            pltpu.SemaphoreType.DMA((fine_part,)),
        ],
        input_output_aliases={5: 0} if held else {},
        compiler_params=pltpu.CompilerParams(vmem_limit_bytes=LIMIT),
        cost_estimate=pl.CostEstimate(
            flops=2 * fine_part * 256 * inputs * 4 * rows,
            bytes_accessed=4_000_000,
            transcendentals=0,
        ),
        name="correlate",
    )(mine, *near, across, *held)


def local(voltage, fir_taps, zoom_width, zoom_shift, owner_slot):
    inputs_dev, blocks, samples = voltage.shape
    devices = lax.axis_size("chan")
    groups = lax.axis_size("tm")
    fine = owner_slot.shape[0]
    fine_dev = fine // devices
    up = [(i, i + 1) for i in range(groups - 1)]
    tail, rest, base = tail_part(voltage, fir_taps, zoom_width, zoom_shift, fine)
    tail = lax.ppermute(tail, "tm", up)
    window = own_part(voltage, rest, base, fine)
    slot, window = lax.optimization_barrier((owner_slot, window))
    place = place_part(slot[None, :])
    sent = send_part(window, tail, place)
    lanes = sent.shape[1]
    received = lax.all_to_all(
        sent.reshape(devices, fine_dev // 2, 2, lanes), "chan", split_axis=0, concat_axis=0, tiled=True
    )
    own = unpack(received.reshape(fine, lanes), fine_dev, inputs_dev)

    def around(turn):
        pairs = []
        for c in range(devices):
            for g in range(groups):
                to = (g + (turn if c % 2 == 0 else -turn)) % groups
                pairs.append((c * groups + g, c * groups + to))
        return pairs

    both = ("chan", "tm")
    ahead = lax.ppermute(own, both, around(1))
    behind = lax.ppermute(own, both, around(-1))
    first = fine_dev // 2
    across_b = lax.ppermute(own[first:], both, around(2))
    spectra = jnp.transpose(own.reshape(fine_dev, 2, blocks, own.shape[2]), (0, 2, 1, 3))
    ahead, spectra = lax.optimization_barrier((ahead, spectra))
    across_a = lax.ppermute(ahead[:first], both, around(1))
    mine = (lax.axis_index("tm") * 128).astype(jnp.int32)[None]
    scale = 1.0 / (blocks * groups)
    near = (own, ahead, behind)
    summed = correlate(near, across_b, mine, scale, first)
    summed = correlate(near, across_a, mine, scale, 0, summed)
    return spectra, summed


def solution(mesh):
    return jax.shard_map(
        local,
        mesh=mesh,
        in_specs=(P("chan", "tm", None), P(), P(), P(), P()),
        out_specs=(P("chan", "tm", None, None), P("chan", None, "tm", None)),
        check_vma=False,
    )
```

```python
import functools
import math

import jax
import jax.numpy as jnp
from jax import lax
from jax.experimental import pallas as pl
from jax.experimental.pallas import tpu as pltpu
from jax.sharding import PartitionSpec as P

VMEM = pltpu.VMEM
BF16 = jnp.bfloat16
F32 = jnp.float32
LIMIT = 32 * 1024 * 1024
MOST = 64 * 1000 * 1000
WIDE = 272


def dft_weights(phases, coarse):
    shape = (2 * phases, 2 * phases * coarse)
    source = lax.broadcasted_iota(jnp.int32, shape, 0)
    target = lax.broadcasted_iota(jnp.int32, shape, 1)
    j, p = source % phases, source // phases
    b, d, q = target % phases, (target // phases) % coarse, target // (phases * coarse)
    turn = (j * b + jnp.where(p == q, 0, jnp.where(q == 0, 3, 1) * phases // 4)) % phases
    table = jnp.zeros(shape, F32)
    for k in range(phases):
        exact = round(math.cos(2.0 * math.pi * k / phases), 15) / math.sqrt(phases)
        table = jnp.where(turn == k, jnp.float32(exact), table)
    return split_sum(jnp.concatenate([jnp.where(d == c, table, 0.0) for c in range(coarse)], 0))


def spread_taps(taps):
    phases = taps.shape[1]
    wide = jnp.concatenate([taps, jnp.zeros((taps.shape[0], 128 - phases), F32)], 1)
    while phases < 128:
        wide = wide + pltpu.roll(wide, phases, 1)
        phases *= 2
    return wide


def tap_tables(taps):
    row = lax.broadcasted_iota(jnp.int32, (8, 128), 0)
    tap = [jnp.broadcast_to(taps[m : m + 1, :], (8, 128)) for m in range(taps.shape[0])]
    zero = jnp.zeros((8, 128), F32)
    same = [jnp.where(row >= k, tap[k], zero) for k in range(1, 8)]
    beyond = [jnp.where(row < k, tap[8 + k], zero) for k in range(1, 4)]
    before = [jnp.where(row < k, tap[k], tap[8 + k] if k < 4 else zero) for k in range(1, 8)]
    return tap[0], tap[8], same, before, beyond


def split_sum(value):
    high = value.astype(BF16)
    return high, (value - high.astype(F32)).astype(BF16)


def fetch_voltage(voltage_ref, held_ref, sem):
    return pltpu.make_async_copy(voltage_ref, held_ref, sem)


def window_table(krow):
    row = lax.broadcasted_iota(jnp.int32, (WIDE, krow.shape[1]), 0)
    return jnp.where(row == krow, 1.0, 0.0).astype(BF16)


def tail_kernel(
    width_ref, shift_ref, voltage_ref, taps_ref,
    out_ref, rest_ref, base_ref,
    held_ref, member_ref, split_high_ref, split_low_ref, table_ref, window_ref, sem,
):
    inputs, _, samples = held_ref.shape
    fine = window_ref.shape[0] - 256
    lanes = 128
    phases = 16
    copy = fetch_voltage(voltage_ref, held_ref, sem)
    copy.start()
    lane = lax.broadcasted_iota(jnp.int32, (1, lanes), 1)
    place = lane // phases
    bins = lane % phases
    first = jnp.int32(0)
    bases = []
    for step in range(samples // 512):
        base = (first // 16) * 16
        base_ref[step] = base
        bases.append(base)
        rows = []
        for half in range(2):
            width = jnp.zeros((1, lanes), jnp.int32)
            shift = jnp.zeros((1, lanes), jnp.int32)
            begin = jnp.zeros((1, lanes), jnp.int32)
            for c in range(8):
                at = step * 16 + half * 8 + c
                here = place == c
                wide = width_ref[at]
                width = jnp.where(here, wide, width)
                shift = jnp.where(here, shift_ref[at], shift)
                begin = jnp.where(here, first, begin)
                first = first + wide
            room = (phases + 1 - width).astype(F32)
            whole = jnp.floor((shift.astype(F32) + 0.5) / room)
            start = shift - (whole * room).astype(jnp.int32)
            offset = bins - start
            inside = (offset >= 0) & (offset < width)
            rows.append(jnp.where(inside, begin + offset, -1))
        krow = jnp.concatenate(rows, 1) - base
        rest_ref[step : step + 1, :] = krow.astype(F32)
        member_ref[step * WIDE : (step + 1) * WIDE, :] = window_table(krow)

    taps = spread_taps(taps_ref[...])
    rest_ref[16 : 16 + taps.shape[0], 0:lanes] = taps
    _, eighth, _, before, beyond = tap_tables(taps)
    high_table, low_table = dft_weights(phases, 8)
    weights = jnp.concatenate([high_table, high_table, low_table], 0)
    window_ref[...] = jnp.zeros(window_ref.shape, F32)
    copy.wait()

    def group(step, carry):
        for sub in range(2):
            spot = pl.ds(pl.multiple_of(step * 256 + sub * lanes, lanes), lanes)
            tops, bottoms = [], []
            for i in range(inputs):
                series = held_ref[i, :, spot].astype(F32)
                older, recent = series[:8], series[8:]
                top = eighth * recent
                bottom = jnp.zeros((8, lanes), F32)
                for k in range(1, 8):
                    recent_k = pltpu.roll(recent, k, 0)
                    top = top + before[k - 1] * recent_k
                    if k < 4:
                        top = top + beyond[k - 1] * pltpu.roll(older, k, 0)
                        bottom = bottom + beyond[k - 1] * recent_k
                tops.append(top)
                bottoms.append(bottom if i % 2 == 0 else pltpu.roll(bottom, 4, 0))
            packed = [bottoms[i] + bottoms[i + 1] for i in range(0, inputs, 2)]
            high, low = split_sum(jnp.concatenate(tops + packed, 0))
            at = pl.ds(pl.multiple_of(step * 48, 16), 48)
            split_high_ref[at, sub * lanes : (sub + 1) * lanes] = high
            split_low_ref[at, sub * lanes : (sub + 1) * lanes] = low
        return carry

    lax.fori_loop(0, samples // 256, group, 0)
    for step in range(samples // 1024):
        at = slice(step * 192, step * 192 + 192)
        high = split_high_ref[at, :]
        split = jnp.concatenate([high, split_low_ref[at, :], high], 1)
        spectra = jnp.dot(split, weights, preferred_element_type=F32).astype(BF16)
        for j in range(4):
            for q in range(2):
                to = (step * 2 + j // 2) * 96
                half = slice((j % 2) * lanes, (j % 2 + 1) * lanes)
                piece = spectra[j * 48 : (j + 1) * 48, q * lanes : (q + 1) * lanes]
                table_ref[to + q * 32 : to + q * 32 + 32, half] = piece[:32]
                table_ref[to + 64 + q * 16 : to + 64 + q * 16 + 16, half] = piece[32:]
    for step in range(samples // 512):
        picked = lax.dot_general(
            member_ref[step * WIDE : (step + 1) * WIDE, :],
            table_ref[step * 96 : (step + 1) * 96, :],
            (((1,), (1,)), ((), ())),
            preferred_element_type=F32,
        )
        window_ref[pl.ds(pl.multiple_of(bases[step], 16), WIDE), 0:96] += picked
    half, quarter = fine // 2, fine // 4
    at = lax.broadcasted_iota(jnp.int32, (half, lanes), 1)
    out_ref[0:half, :] = jnp.where(
        at < 64, window_ref[0:half, :], pltpu.roll(window_ref[half:fine, :], 64, 1)
    ).astype(BF16)
    at = lax.broadcasted_iota(jnp.int32, (quarter, lanes), 1)
    packed = jnp.zeros((quarter, lanes), F32)
    for j in range(4):
        moved = pltpu.roll(window_ref[j * quarter : (j + 1) * quarter, :], (64 + j * 32) % lanes, 1)
        packed = jnp.where(at // 32 == j, moved, packed)
    out_ref[half : half + quarter, :] = packed.astype(BF16)


def own_kernel(
    base_ref, voltage_ref, rest_ref,
    window_ref,
    held_ref, split_high_ref, split_low_ref, table_ref, sem,
):
    inputs, blocks, samples = held_ref.shape
    lanes = 128
    copy = fetch_voltage(voltage_ref, held_ref, sem)
    copy.start()
    window_ref[...] = jnp.zeros(window_ref.shape, F32)
    first, eighth, same, before, _ = tap_tables(rest_ref[16:28, 0:lanes])
    high_table, low_table = dft_weights(16, 8)
    weights = jnp.concatenate([high_table, high_table, low_table], 0)
    copy.wait()

    def group(step, carry):
        for i in range(inputs):
            for sub in range(2):
                spot = pl.ds(pl.multiple_of(step * 256 + sub * lanes, lanes), lanes)
                series = held_ref[i, :, spot].astype(F32)
                early, late = series[:8], series[8:]
                top = first * early
                bottom = first * late + eighth * early
                for k in range(1, 8):
                    early_k = pltpu.roll(early, k, 0)
                    top = top + same[k - 1] * early_k
                    bottom = bottom + before[k - 1] * early_k
                    bottom = bottom + same[k - 1] * pltpu.roll(late, k, 0)
                at = pl.ds(pl.multiple_of(step * 64 + i * blocks, blocks), blocks)
                high, low = split_sum(jnp.concatenate([top, bottom], 0))
                split_high_ref[at, sub * lanes : (sub + 1) * lanes] = high
                split_low_ref[at, sub * lanes : (sub + 1) * lanes] = low
        return carry

    lax.fori_loop(0, samples // 256, group, 0)
    for step in range(samples // 1024):
        at = slice(step * 256, step * 256 + 256)
        high = split_high_ref[at, :]
        split = jnp.concatenate([high, split_low_ref[at, :], high], 1)
        parts = split_sum(jnp.dot(split, weights, preferred_element_type=F32))
        for j in range(4):
            for q in range(2):
                for p in range(2):
                    to = (step * 2 + j // 2) * 256 + p * 128 + q * 64
                    table_ref[to : to + 64, (j % 2) * 128 : (j % 2) * 128 + 128] = parts[p][
                        j * 64 : (j + 1) * 64, q * 128 : (q + 1) * 128
                    ]
    for step in range(samples // 512):
        picked = lax.dot_general(
            window_table(rest_ref[step : step + 1, :].astype(jnp.int32)),
            table_ref[step * 256 : (step + 1) * 256, :],
            (((1,), (1,)), ((), ())),
            preferred_element_type=F32,
        )
        base = pl.multiple_of(base_ref[step], 16)
        window_ref[pl.ds(base, WIDE), :] += picked[:, :lanes] + picked[:, lanes:]


def place_kernel(parity_ref, slot_ref, place_ref, *, fine_dev):
    fine = slot_ref.shape[1]
    rows = 16
    row = lax.broadcasted_iota(jnp.int32, (rows, fine), 0).astype(jnp.int16)
    slot = slot_ref[...]
    owner = jnp.floor((slot.astype(F32) + 0.5) / fine_dev).astype(jnp.int32)
    target = (owner // 2) * (2 * fine_dev) + slot - owner * fine_dev
    target = jnp.where(owner % 2 == parity_ref[0], target, -fine)
    first = jnp.broadcast_to(target, (rows, fine)).astype(jnp.int16)
    second = jnp.broadcast_to(target + fine_dev, (rows, fine)).astype(jnp.int16)
    one, zero = jnp.ones((rows, fine), BF16), jnp.zeros((rows, fine), BF16)

    def places(step, carry):
        at = pl.multiple_of(step * rows, rows)
        here = row + at.astype(jnp.int16)
        place_ref[pl.ds(at, rows), :] = jnp.where(
            here == first, one, jnp.where(here == second, one, zero)
        )
        return carry

    lax.fori_loop(0, place_ref.shape[0] // rows, places, 0, unroll=4)


def join_kernel(window_ref, tail_ref, bins_ref):
    fine, lanes = bins_ref.shape
    half, quarter = fine // 2, fine // 4
    source = lax.broadcasted_iota(jnp.int32, (lanes, lanes), 0)
    target = lax.broadcasted_iota(jnp.int32, (lanes, lanes), 1)
    late = source - 64
    early_lane = (source // 8) * 16 + source % 8
    late_lane = (late // 4) * 16 + 8 + late % 4
    spread = jnp.where(
        ((source < 64) & (target == early_lane))
        | ((source >= 64) & (source < 96) & (late % 4 < 3) & (target == late_lane)),
        1.0,
        0.0,
    ).astype(BF16)
    at = lax.broadcasted_iota(jnp.int32, (quarter, lanes), 1)
    for j in range(4):
        rows = slice((j % 2) * quarter, (j % 2 + 1) * quarter)
        early = tail_ref[rows, :].astype(F32)
        if j >= 2:
            early = pltpu.roll(early, 64, 1)
        late = tail_ref[half : half + quarter, :].astype(F32)
        late = pltpu.roll(late, (64 - j * 32) % lanes, 1)
        tail = jnp.where(at < 64, early, late).astype(BF16)
        added = jnp.dot(tail, spread, preferred_element_type=F32)
        rows = slice(j * quarter, (j + 1) * quarter)
        bins_ref[rows, :] = (window_ref[rows, :] + added).astype(BF16)


def send_kernel(parity_ref, bins_ref, other_ref, place_ref, out_ref, *, fine_dev):
    even = jnp.broadcast_to(parity_ref[0], bins_ref.shape) == 0
    bins, other = bins_ref[...], other_ref[...]
    pair = jnp.concatenate([jnp.where(even, bins, other), jnp.where(even, other, bins)], 1)
    lanes = bins.shape[1]
    step_rows = 16 * 2 * fine_dev
    row = lax.broadcasted_iota(jnp.int32, (step_rows, lanes), 0) % (2 * fine_dev)
    for step in range(out_ref.shape[0] // step_rows):
        at = slice(step * step_rows, (step + 1) * step_rows)
        moved = jnp.dot(place_ref[at, :], pair, preferred_element_type=F32)
        out_ref[at, :] = jnp.where(row < fine_dev, moved[:, :lanes], moved[:, lanes:]).astype(BF16)


def unpack_kernel(received_ref, out_ref, wide_ref, *, inputs_dev):
    fine_dev = out_ref.shape[0]
    rows, lanes = received_ref.shape
    devices = rows // fine_dev
    blocks = lanes // (2 * inputs_dev)
    wide_ref[...] = received_ref[...].astype(F32)
    inputs = inputs_dev * devices
    source = lax.broadcasted_iota(jnp.int32, (inputs, inputs), 0)
    target = lax.broadcasted_iota(jnp.int32, (inputs, inputs), 1)
    spread = jnp.where((source % devices) * inputs_dev + source // devices == target, 1.0, 0.0)
    spread = spread.astype(BF16)
    pieces = []
    for channel in range(fine_dev):
        turned = wide_ref[pl.ds(channel, devices, stride=fine_dev), :].T.astype(BF16)
        for q in range(2):
            pieces.append(
                jnp.concatenate(
                    [
                        turned[(q * inputs_dev + i) * blocks : (q * inputs_dev + i + 1) * blocks, :]
                        for i in range(inputs_dev)
                    ],
                    1,
                )
            )
    joined = jnp.concatenate(pieces, 0)
    placed = jnp.dot(joined, spread, preferred_element_type=F32).astype(BF16)
    out_ref[...] = placed.reshape(out_ref.shape)


def correlate_kernel(mine_ref, own_ref, ahead_ref, behind_ref, across_ref, *rest, scale, first):
    out_ref, block_ref, sems = rest[-3:]
    mine = pl.ds(pl.multiple_of(mine_ref[0], 128), 128)
    half = own_ref.shape[1] // 2
    copies = []
    for channel in range(across_ref.shape[0]):
        refs = [ref.at[first + channel] for ref in (own_ref, ahead_ref, behind_ref)]
        refs.append(across_ref.at[channel])
        right = jnp.concatenate([ref[...] for ref in refs], 0)
        real, imag = [], []
        for ref in refs:
            block = ref[:, mine]
            real.append(block)
            imag.append(block[half:])
            imag.append(-block[:half])
        left = jnp.concatenate([jnp.concatenate(real, 0), jnp.concatenate(imag, 0)], 1)
        product = lax.dot_general(
            left, right, (((0,), (0,)), ((), ())), preferred_element_type=F32
        )
        product = (product * scale).astype(BF16)
        block_ref[channel, 0] = product[:128]
        block_ref[channel, 1] = product[128:]
        copies.append(
            pltpu.make_async_copy(
                block_ref.at[channel], out_ref.at[first + channel], sems.at[channel]
            )
        )
        copies[-1].start()
    for copy in copies:
        copy.wait()


WHOLE = pl.BlockSpec(memory_space=VMEM)
SCALARS = pl.BlockSpec(memory_space=pltpu.SMEM)
APART = pl.BlockSpec(memory_space=pl.ANY)


def tail_part(voltage, fir_taps, zoom_width, zoom_shift, fine):
    inputs_dev, blocks, samples = voltage.shape
    groups = samples // 256
    return pl.pallas_call(
        tail_kernel,
        out_shape=(
            jax.ShapeDtypeStruct((fine // 2 + fine // 4, 128), BF16),
            jax.ShapeDtypeStruct((32, 256), F32),
            jax.ShapeDtypeStruct((samples // 512,), jnp.int32),
        ),
        in_specs=[SCALARS, SCALARS, APART, WHOLE],
        out_specs=(WHOLE, WHOLE, SCALARS),
        scratch_shapes=[
            pltpu.VMEM(voltage.shape, BF16),
            pltpu.VMEM((samples // 512 * WIDE, 256), BF16),
            pltpu.VMEM((groups * 48, 256), BF16),
            pltpu.VMEM((groups * 48, 256), BF16),
            pltpu.VMEM((groups * 48, 256), BF16),
            pltpu.VMEM((fine + 256, 128), F32),
            pltpu.SemaphoreType.DMA,
        ],
        compiler_params=pltpu.CompilerParams(vmem_limit_bytes=MOST),
        name="tail_part",
    )(zoom_width, zoom_shift, voltage, fir_taps)


def own_part(voltage, rest, base, fine):
    inputs_dev, blocks, samples = voltage.shape
    groups = samples // 256
    return pl.pallas_call(
        own_kernel,
        out_shape=jax.ShapeDtypeStruct((fine + 256, 128), F32),
        in_specs=[SCALARS, APART, WHOLE],
        out_specs=WHOLE,
        scratch_shapes=[
            pltpu.VMEM(voltage.shape, BF16),
            pltpu.VMEM((groups * 64, 256), BF16),
            pltpu.VMEM((groups * 64, 256), BF16),
            pltpu.VMEM((groups * 128, 256), BF16),
            pltpu.SemaphoreType.DMA,
        ],
        compiler_params=pltpu.CompilerParams(vmem_limit_bytes=MOST),
        cost_estimate=pl.CostEstimate(flops=5_000_000_000, bytes_accessed=4_000_000, transcendentals=0),
        name="own_part",
    )(base, voltage, rest)


def place_part(parity, slot, fine_dev):
    fine = slot.shape[1]
    return pl.pallas_call(
        functools.partial(place_kernel, fine_dev=fine_dev),
        out_shape=jax.ShapeDtypeStruct((fine, fine), BF16),
        in_specs=[SCALARS, WHOLE],
        out_specs=WHOLE,
        compiler_params=pltpu.CompilerParams(vmem_limit_bytes=LIMIT),
        cost_estimate=pl.CostEstimate(flops=5_000_000_000, bytes_accessed=4_000_000, transcendentals=0),
        name="place_part",
    )(parity, slot)


def join_part(window, tail, fine):
    return pl.pallas_call(
        join_kernel,
        out_shape=jax.ShapeDtypeStruct((fine, 128), BF16),
        in_specs=[WHOLE] * 2,
        out_specs=WHOLE,
        compiler_params=pltpu.CompilerParams(vmem_limit_bytes=LIMIT),
        name="join_part",
    )(window, tail)


def send_part(parity, bins, other, place, fine_dev):
    return pl.pallas_call(
        functools.partial(send_kernel, fine_dev=fine_dev),
        out_shape=jax.ShapeDtypeStruct(bins.shape, BF16),
        in_specs=[SCALARS] + [WHOLE] * 3,
        out_specs=WHOLE,
        compiler_params=pltpu.CompilerParams(vmem_limit_bytes=LIMIT),
        name="send_part",
    )(parity, bins, other, place)


def unpack(received, fine_dev, inputs_dev):
    rows, lanes = received.shape
    devices = rows // fine_dev
    blocks = lanes // (2 * inputs_dev)
    whole = pl.BlockSpec(memory_space=VMEM)
    return pl.pallas_call(
        functools.partial(unpack_kernel, inputs_dev=inputs_dev),
        out_shape=jax.ShapeDtypeStruct((fine_dev, 2 * blocks, devices * inputs_dev), BF16),
        in_specs=[whole],
        out_specs=whole,
        scratch_shapes=[pltpu.VMEM((rows, lanes), F32)],
        compiler_params=pltpu.CompilerParams(vmem_limit_bytes=LIMIT),
        name="unpack",
    )(received)


def correlate(near, across, mine, scale, first, earlier=None):
    fine_dev, rows, inputs = near[0].shape
    fine_part = across.shape[0]
    whole = pl.BlockSpec(memory_space=VMEM)
    apart = pl.BlockSpec(memory_space=pl.ANY)
    held = [] if earlier is None else [earlier]
    return pl.pallas_call(
        functools.partial(correlate_kernel, scale=scale, first=first),
        out_shape=jax.ShapeDtypeStruct((fine_dev, 2, 128, inputs), BF16),
        in_specs=[pl.BlockSpec(memory_space=pltpu.SMEM)] + [whole] * 4 + [apart] * len(held),
        out_specs=apart,
        scratch_shapes=[
            pltpu.VMEM((fine_part, 2, 128, inputs), BF16),
            pltpu.SemaphoreType.DMA((fine_part,)),
        ],
        input_output_aliases={5: 0} if held else {},
        compiler_params=pltpu.CompilerParams(vmem_limit_bytes=LIMIT),
        cost_estimate=pl.CostEstimate(
            flops=2 * fine_part * 256 * inputs * 4 * rows,
            bytes_accessed=4_000_000,
            transcendentals=0,
        ),
        name="correlate",
    )(mine, *near, across, *held)


def local(voltage, fir_taps, zoom_width, zoom_shift, owner_slot):
    inputs_dev, blocks, samples = voltage.shape
    devices = lax.axis_size("chan")
    groups = lax.axis_size("tm")
    fine = owner_slot.shape[0]
    fine_dev = fine // devices
    up = [(i, i + 1) for i in range(groups - 1)]
    tail, rest, base = tail_part(voltage, fir_taps, zoom_width, zoom_shift, fine)
    tail = lax.ppermute(tail, "tm", up)
    window = own_part(voltage, rest, base, fine)
    slot, window = lax.optimization_barrier((owner_slot, window))
    parity = (lax.axis_index("chan") % 2).astype(jnp.int32)[None]
    place = place_part(parity, slot[None, :], fine_dev)
    window, place = lax.optimization_barrier((window, place))
    bins = join_part(window, tail, fine)
    other = lax.ppermute(bins, "chan", [(c, c ^ 1) for c in range(devices)])
    sent = send_part(parity, bins, other, place, fine_dev)
    lanes = sent.shape[1]
    received = lax.all_to_all(
        sent.reshape(devices // 2, fine_dev, 2, lanes),
        "chan",
        split_axis=0,
        concat_axis=0,
        axis_index_groups=[list(range(core, devices, 2)) for core in range(2)],
        tiled=True,
    )
    own = unpack(received.reshape(fine, lanes), fine_dev, inputs_dev)

    def around(turn):
        pairs = []
        for c in range(devices):
            for g in range(groups):
                to = (g + (turn if c % 2 == 0 else -turn)) % groups
                pairs.append((c * groups + g, c * groups + to))
        return pairs

    both = ("chan", "tm")
    ahead = lax.ppermute(own, both, around(1))
    behind = lax.ppermute(own, both, around(-1))
    spectra = jnp.transpose(own.reshape(fine_dev, 2, blocks, own.shape[2]), (0, 2, 1, 3))
    ahead, spectra = lax.optimization_barrier((ahead, spectra))
    first = fine_dev * 9 // 14
    across_a = lax.ppermute(ahead[:first], both, around(1))
    across_b = lax.ppermute(ahead[first:], both, around(1))
    mine = (lax.axis_index("tm") * 128).astype(jnp.int32)[None]
    scale = 1.0 / (blocks * groups)
    near = (own, ahead, behind)
    summed = correlate(near, across_a, mine, scale, 0)
    summed = correlate(near, across_b, mine, scale, first, summed)
    return spectra, summed


def solution(mesh):
    return jax.shard_map(
        local,
        mesh=mesh,
        in_specs=(P("chan", "tm", None), P(), P(), P(), P()),
        out_specs=(P("chan", "tm", None, None), P("chan", None, "tm", None)),
        check_vma=False,
    )
```

```python
import functools
import math

import jax
import jax.numpy as jnp
from jax import lax
from jax.experimental import pallas as pl
from jax.experimental.pallas import tpu as pltpu
from jax.sharding import PartitionSpec as P

VMEM = pltpu.VMEM
BF16 = jnp.bfloat16
F32 = jnp.float32
LIMIT = 32 * 1024 * 1024
MOST = 64 * 1000 * 1000
WIDE = 272


def dft_weights(phases, coarse):
    shape = (2 * phases, 2 * phases * coarse)
    source = lax.broadcasted_iota(jnp.int32, shape, 0)
    target = lax.broadcasted_iota(jnp.int32, shape, 1)
    j, p = source % phases, source // phases
    b, d, q = target % phases, (target // phases) % coarse, target // (phases * coarse)
    turn = (j * b + jnp.where(p == q, 0, jnp.where(q == 0, 3, 1) * phases // 4)) % phases
    table = jnp.zeros(shape, F32)
    for k in range(phases):
        exact = round(math.cos(2.0 * math.pi * k / phases), 15) / math.sqrt(phases)
        table = jnp.where(turn == k, jnp.float32(exact), table)
    return split_sum(jnp.concatenate([jnp.where(d == c, table, 0.0) for c in range(coarse)], 0))


def spread_taps(taps):
    phases = taps.shape[1]
    wide = jnp.concatenate([taps, jnp.zeros((taps.shape[0], 128 - phases), F32)], 1)
    while phases < 128:
        wide = wide + pltpu.roll(wide, phases, 1)
        phases *= 2
    return wide


def tap_tables(taps):
    row = lax.broadcasted_iota(jnp.int32, (8, 128), 0)
    tap = [jnp.broadcast_to(taps[m : m + 1, :], (8, 128)) for m in range(taps.shape[0])]
    zero = jnp.zeros((8, 128), F32)
    same = [jnp.where(row >= k, tap[k], zero) for k in range(1, 8)]
    beyond = [jnp.where(row < k, tap[8 + k], zero) for k in range(1, 4)]
    before = [jnp.where(row < k, tap[k], tap[8 + k] if k < 4 else zero) for k in range(1, 8)]
    return tap[0], tap[8], same, before, beyond


def split_sum(value):
    high = value.astype(BF16)
    return high, (value - high.astype(F32)).astype(BF16)


def fetch(sems, *pairs):
    copies = [
        pltpu.make_async_copy(source, target, sems.at[i]) for i, (source, target) in enumerate(pairs)
    ]
    for copy in copies:
        copy.start()
    return copies


def window_table(krow):
    row = lax.broadcasted_iota(jnp.int32, (WIDE, krow.shape[1]), 0)
    return jnp.where(row == krow, 1.0, 0.0).astype(BF16)


def tail_kernel(
    width_from, shift_from, voltage_ref, taps_from,
    out_ref, rest_ref, base_ref,
    width_ref, shift_ref, taps_ref, held_ref, member_ref, split_high_ref, split_low_ref, table_ref, window_ref, sems,
):
    inputs, _, samples = held_ref.shape
    fine = window_ref.shape[0] - 256
    lanes = 128
    phases = 16
    copies = fetch(
        sems,
        (width_from, width_ref),
        (shift_from, shift_ref),
        (taps_from, taps_ref),
        (voltage_ref, held_ref),
    )
    copies[0].wait()
    copies[1].wait()
    lane = lax.broadcasted_iota(jnp.int32, (1, lanes), 1)
    place = lane // phases
    bins = lane % phases
    first = jnp.int32(0)
    bases = []
    for step in range(samples // 512):
        base = (first // 16) * 16
        base_ref[step] = base
        bases.append(base)
        rows = []
        for half in range(2):
            width = jnp.zeros((1, lanes), jnp.int32)
            shift = jnp.zeros((1, lanes), jnp.int32)
            begin = jnp.zeros((1, lanes), jnp.int32)
            for c in range(8):
                at = step * 16 + half * 8 + c
                here = place == c
                wide = width_ref[at]
                width = jnp.where(here, wide, width)
                shift = jnp.where(here, shift_ref[at], shift)
                begin = jnp.where(here, first, begin)
                first = first + wide
            room = (phases + 1 - width).astype(F32)
            whole = jnp.floor((shift.astype(F32) + 0.5) / room)
            start = shift - (whole * room).astype(jnp.int32)
            offset = bins - start
            inside = (offset >= 0) & (offset < width)
            rows.append(jnp.where(inside, begin + offset, -1))
        krow = jnp.concatenate(rows, 1) - base
        rest_ref[step : step + 1, :] = krow.astype(F32)
        member_ref[step * WIDE : (step + 1) * WIDE, :] = window_table(krow)

    copies[2].wait()
    taps = spread_taps(taps_ref[...])
    rest_ref[16 : 16 + taps.shape[0], 0:lanes] = taps
    _, eighth, _, before, beyond = tap_tables(taps)
    high_table, low_table = dft_weights(phases, 8)
    weights = jnp.concatenate([high_table, high_table, low_table], 0)
    window_ref[...] = jnp.zeros(window_ref.shape, F32)
    copies[3].wait()

    def group(step, carry):
        for sub in range(2):
            spot = pl.ds(pl.multiple_of(step * 256 + sub * lanes, lanes), lanes)
            tops, bottoms = [], []
            for i in range(inputs):
                series = held_ref[i, :, spot].astype(F32)
                older, recent = series[:8], series[8:]
                top = eighth * recent
                bottom = jnp.zeros((8, lanes), F32)
                for k in range(1, 8):
                    recent_k = pltpu.roll(recent, k, 0)
                    top = top + before[k - 1] * recent_k
                    if k < 4:
                        top = top + beyond[k - 1] * pltpu.roll(older, k, 0)
                        bottom = bottom + beyond[k - 1] * recent_k
                tops.append(top)
                bottoms.append(bottom if i % 2 == 0 else pltpu.roll(bottom, 4, 0))
            packed = [bottoms[i] + bottoms[i + 1] for i in range(0, inputs, 2)]
            high, low = split_sum(jnp.concatenate(tops + packed, 0))
            at = pl.ds(pl.multiple_of(step * 48, 16), 48)
            split_high_ref[at, sub * lanes : (sub + 1) * lanes] = high
            split_low_ref[at, sub * lanes : (sub + 1) * lanes] = low
        return carry

    lax.fori_loop(0, samples // 256, group, 0)
    for step in range(samples // 1024):
        at = slice(step * 192, step * 192 + 192)
        high = split_high_ref[at, :]
        split = jnp.concatenate([high, split_low_ref[at, :], high], 1)
        spectra = jnp.dot(split, weights, preferred_element_type=F32).astype(BF16)
        for j in range(4):
            for q in range(2):
                to = (step * 2 + j // 2) * 96
                half = slice((j % 2) * lanes, (j % 2 + 1) * lanes)
                piece = spectra[j * 48 : (j + 1) * 48, q * lanes : (q + 1) * lanes]
                table_ref[to + q * 32 : to + q * 32 + 32, half] = piece[:32]
                table_ref[to + 64 + q * 16 : to + 64 + q * 16 + 16, half] = piece[32:]
    for step in range(samples // 512):
        picked = lax.dot_general(
            member_ref[step * WIDE : (step + 1) * WIDE, :],
            table_ref[step * 96 : (step + 1) * 96, :],
            (((1,), (1,)), ((), ())),
            preferred_element_type=F32,
        )
        window_ref[pl.ds(pl.multiple_of(bases[step], 16), WIDE), 0:96] += picked
    half, quarter = fine // 2, fine // 4
    at = lax.broadcasted_iota(jnp.int32, (half, lanes), 1)
    out_ref[0:half, :] = jnp.where(
        at < 64, window_ref[0:half, :], pltpu.roll(window_ref[half:fine, :], 64, 1)
    ).astype(BF16)
    at = lax.broadcasted_iota(jnp.int32, (quarter, lanes), 1)
    packed = jnp.zeros((quarter, lanes), F32)
    for j in range(4):
        moved = pltpu.roll(window_ref[j * quarter : (j + 1) * quarter, :], (64 + j * 32) % lanes, 1)
        packed = jnp.where(at // 32 == j, moved, packed)
    out_ref[half : half + quarter, :] = packed.astype(BF16)


def own_kernel(
    base_from, voltage_ref, rest_from,
    window_ref,
    base_ref, rest_ref, held_ref, split_high_ref, split_low_ref, table_ref, sems,
):
    inputs, blocks, samples = held_ref.shape
    lanes = 128
    copies = fetch(sems, (rest_from, rest_ref), (base_from, base_ref), (voltage_ref, held_ref))
    window_ref[...] = jnp.zeros(window_ref.shape, F32)
    high_table, low_table = dft_weights(16, 8)
    weights = jnp.concatenate([high_table, high_table, low_table], 0)
    for copy in copies:
        copy.wait()
    first, eighth, same, before, _ = tap_tables(rest_ref[16:28, 0:lanes])

    def group(step, carry):
        for i in range(inputs):
            for sub in range(2):
                spot = pl.ds(pl.multiple_of(step * 256 + sub * lanes, lanes), lanes)
                series = held_ref[i, :, spot].astype(F32)
                early, late = series[:8], series[8:]
                top = first * early
                bottom = first * late + eighth * early
                for k in range(1, 8):
                    early_k = pltpu.roll(early, k, 0)
                    top = top + same[k - 1] * early_k
                    bottom = bottom + before[k - 1] * early_k
                    bottom = bottom + same[k - 1] * pltpu.roll(late, k, 0)
                at = pl.ds(pl.multiple_of(step * 64 + i * blocks, blocks), blocks)
                high, low = split_sum(jnp.concatenate([top, bottom], 0))
                split_high_ref[at, sub * lanes : (sub + 1) * lanes] = high
                split_low_ref[at, sub * lanes : (sub + 1) * lanes] = low
        return carry

    lax.fori_loop(0, samples // 256, group, 0)
    for step in range(samples // 1024):
        at = slice(step * 256, step * 256 + 256)
        high = split_high_ref[at, :]
        split = jnp.concatenate([high, split_low_ref[at, :], high], 1)
        parts = split_sum(jnp.dot(split, weights, preferred_element_type=F32))
        for j in range(4):
            for q in range(2):
                for p in range(2):
                    to = (step * 2 + j // 2) * 256 + p * 128 + q * 64
                    table_ref[to : to + 64, (j % 2) * 128 : (j % 2) * 128 + 128] = parts[p][
                        j * 64 : (j + 1) * 64, q * 128 : (q + 1) * 128
                    ]
    for step in range(samples // 512):
        picked = lax.dot_general(
            window_table(rest_ref[step : step + 1, :].astype(jnp.int32)),
            table_ref[step * 256 : (step + 1) * 256, :],
            (((1,), (1,)), ((), ())),
            preferred_element_type=F32,
        )
        base = pl.multiple_of(base_ref[step], 16)
        window_ref[pl.ds(base, WIDE), :] += picked[:, :lanes] + picked[:, lanes:]


def place_kernel(slot_ref, place_ref):
    fine = slot_ref.shape[1]
    rows = 16
    row = lax.broadcasted_iota(jnp.int32, (rows, fine), 0)
    slot = jnp.broadcast_to(slot_ref[...], (rows, fine))
    row, slot = row.astype(jnp.int16), slot.astype(jnp.int16)
    one, zero = jnp.ones((rows, fine), BF16), jnp.zeros((rows, fine), BF16)

    def places(step, carry):
        at = pl.multiple_of(step * rows, rows)
        here = row + at.astype(jnp.int16)
        place_ref[pl.ds(at, rows), :] = jnp.where(here == slot, one, zero)
        return carry

    lax.fori_loop(0, place_ref.shape[0] // rows, places, 0, unroll=4)


def send_kernel(window_ref, tail_ref, place_ref, out_ref, bins_ref):
    fine, lanes = bins_ref.shape
    half, quarter = fine // 2, fine // 4
    source = lax.broadcasted_iota(jnp.int32, (lanes, lanes), 0)
    target = lax.broadcasted_iota(jnp.int32, (lanes, lanes), 1)
    late = source - 64
    early_lane = (source // 8) * 16 + source % 8
    late_lane = (late // 4) * 16 + 8 + late % 4
    spread = jnp.where(
        ((source < 64) & (target == early_lane))
        | ((source >= 64) & (source < 96) & (late % 4 < 3) & (target == late_lane)),
        1.0,
        0.0,
    ).astype(BF16)
    at = lax.broadcasted_iota(jnp.int32, (quarter, lanes), 1)
    for j in range(4):
        rows = slice((j % 2) * quarter, (j % 2 + 1) * quarter)
        early = tail_ref[rows, :].astype(F32)
        if j >= 2:
            early = pltpu.roll(early, 64, 1)
        late = tail_ref[half : half + quarter, :].astype(F32)
        late = pltpu.roll(late, (64 - j * 32) % lanes, 1)
        tail = jnp.where(at < 64, early, late).astype(BF16)
        added = jnp.dot(tail, spread, preferred_element_type=F32)
        rows = slice(j * quarter, (j + 1) * quarter)
        bins_ref[rows, :] = (window_ref[rows, :] + added).astype(BF16)
    step_rows = 448
    for step in range(out_ref.shape[0] // step_rows):
        at = slice(step * step_rows, (step + 1) * step_rows)
        out_ref[at, :] = jnp.dot(
            place_ref[at, :], bins_ref[...], preferred_element_type=F32
        ).astype(BF16)


def unpack_kernel(received_ref, out_ref, wide_ref, *, inputs_dev):
    fine_dev = out_ref.shape[0]
    rows, lanes = received_ref.shape
    devices = rows // fine_dev
    blocks = lanes // (2 * inputs_dev)
    wide_ref[...] = received_ref[...].astype(F32)
    inputs = inputs_dev * devices
    source = lax.broadcasted_iota(jnp.int32, (inputs, inputs), 0)
    target = lax.broadcasted_iota(jnp.int32, (inputs, inputs), 1)
    spread = jnp.where((source % devices) * inputs_dev + source // devices == target, 1.0, 0.0)
    spread = spread.astype(BF16)
    pieces = []
    for channel in range(fine_dev):
        turned = wide_ref[pl.ds(channel, devices, stride=fine_dev), :].T.astype(BF16)
        for q in range(2):
            pieces.append(
                jnp.concatenate(
                    [
                        turned[(q * inputs_dev + i) * blocks : (q * inputs_dev + i + 1) * blocks, :]
                        for i in range(inputs_dev)
                    ],
                    1,
                )
            )
    joined = jnp.concatenate(pieces, 0)
    placed = jnp.dot(joined, spread, preferred_element_type=F32).astype(BF16)
    out_ref[...] = placed.reshape(out_ref.shape)


def correlate_kernel(mine_ref, own_ref, ahead_ref, behind_ref, across_ref, *rest, scale, first):
    out_ref, block_ref, sems = rest[-3:]
    mine = pl.ds(pl.multiple_of(mine_ref[0], 128), 128)
    half = own_ref.shape[1] // 2
    copies = []
    for channel in range(across_ref.shape[0]):
        refs = [ref.at[first + channel] for ref in (own_ref, ahead_ref, behind_ref)]
        refs.append(across_ref.at[channel])
        right = jnp.concatenate([ref[...] for ref in refs], 0)
        real, imag = [], []
        for ref in refs:
            block = ref[:, mine]
            real.append(block)
            imag.append(block[half:])
            imag.append(-block[:half])
        left = jnp.concatenate([jnp.concatenate(real, 0), jnp.concatenate(imag, 0)], 1)
        product = lax.dot_general(
            left, right, (((0,), (0,)), ((), ())), preferred_element_type=F32
        )
        product = (product * scale).astype(BF16)
        block_ref[channel, 0] = product[:128]
        block_ref[channel, 1] = product[128:]
        copies.append(
            pltpu.make_async_copy(
                block_ref.at[channel], out_ref.at[first + channel], sems.at[channel]
            )
        )
        copies[-1].start()
    for copy in copies:
        copy.wait()


WHOLE = pl.BlockSpec(memory_space=VMEM)
SCALARS = pl.BlockSpec(memory_space=pltpu.SMEM)
APART = pl.BlockSpec(memory_space=pl.ANY)


def tail_part(voltage, fir_taps, zoom_width, zoom_shift, fine):
    inputs_dev, blocks, samples = voltage.shape
    groups = samples // 256
    return pl.pallas_call(
        tail_kernel,
        out_shape=(
            jax.ShapeDtypeStruct((fine // 2 + fine // 4, 128), BF16),
            jax.ShapeDtypeStruct((32, 256), F32),
            jax.ShapeDtypeStruct((samples // 512,), jnp.int32),
        ),
        in_specs=[APART] * 4,
        out_specs=(WHOLE, WHOLE, SCALARS),
        scratch_shapes=[
            pltpu.SMEM(zoom_width.shape, jnp.int32),
            pltpu.SMEM(zoom_shift.shape, jnp.int32),
            pltpu.VMEM(fir_taps.shape, F32),
            pltpu.VMEM(voltage.shape, BF16),
            pltpu.VMEM((samples // 512 * WIDE, 256), BF16),
            pltpu.VMEM((groups * 48, 256), BF16),
            pltpu.VMEM((groups * 48, 256), BF16),
            pltpu.VMEM((groups * 48, 256), BF16),
            pltpu.VMEM((fine + 256, 128), F32),
            pltpu.SemaphoreType.DMA((4,)),
        ],
        compiler_params=pltpu.CompilerParams(vmem_limit_bytes=MOST),
        name="tail_part",
    )(zoom_width, zoom_shift, voltage, fir_taps)


def own_part(voltage, rest, base, fine):
    inputs_dev, blocks, samples = voltage.shape
    groups = samples // 256
    return pl.pallas_call(
        own_kernel,
        out_shape=jax.ShapeDtypeStruct((fine + 256, 128), F32),
        in_specs=[APART] * 3,
        out_specs=WHOLE,
        scratch_shapes=[
            pltpu.SMEM(base.shape, jnp.int32),
            pltpu.VMEM(rest.shape, F32),
            pltpu.VMEM(voltage.shape, BF16),
            pltpu.VMEM((groups * 64, 256), BF16),
            pltpu.VMEM((groups * 64, 256), BF16),
            pltpu.VMEM((groups * 128, 256), BF16),
            pltpu.SemaphoreType.DMA((3,)),
        ],
        compiler_params=pltpu.CompilerParams(vmem_limit_bytes=MOST),
        cost_estimate=pl.CostEstimate(flops=5_000_000_000, bytes_accessed=4_000_000, transcendentals=0),
        name="own_part",
    )(base, voltage, rest)


def place_part(slot):
    fine = slot.shape[1]
    return pl.pallas_call(
        place_kernel,
        out_shape=jax.ShapeDtypeStruct((fine, fine), BF16),
        in_specs=[WHOLE],
        out_specs=WHOLE,
        compiler_params=pltpu.CompilerParams(vmem_limit_bytes=LIMIT),
        cost_estimate=pl.CostEstimate(flops=5_000_000_000, bytes_accessed=4_000_000, transcendentals=0),
        name="place_part",
    )(slot)


def send_part(window, tail, place):
    slots, fine = place.shape
    return pl.pallas_call(
        send_kernel,
        out_shape=jax.ShapeDtypeStruct((slots, 128), BF16),
        in_specs=[WHOLE] * 3,
        out_specs=WHOLE,
        scratch_shapes=[pltpu.VMEM((fine, 128), BF16)],
        compiler_params=pltpu.CompilerParams(vmem_limit_bytes=LIMIT),
        name="send_part",
    )(window, tail, place)


def unpack(received, fine_dev, inputs_dev):
    rows, lanes = received.shape
    devices = rows // fine_dev
    blocks = lanes // (2 * inputs_dev)
    whole = pl.BlockSpec(memory_space=VMEM)
    return pl.pallas_call(
        functools.partial(unpack_kernel, inputs_dev=inputs_dev),
        out_shape=jax.ShapeDtypeStruct((fine_dev, 2 * blocks, devices * inputs_dev), BF16),
        in_specs=[whole],
        out_specs=whole,
        scratch_shapes=[pltpu.VMEM((rows, lanes), F32)],
        compiler_params=pltpu.CompilerParams(vmem_limit_bytes=LIMIT),
        name="unpack",
    )(received)


def correlate(near, across, mine, scale, first, earlier=None):
    fine_dev, rows, inputs = near[0].shape
    fine_part = across.shape[0]
    whole = pl.BlockSpec(memory_space=VMEM)
    apart = pl.BlockSpec(memory_space=pl.ANY)
    held = [] if earlier is None else [earlier]
    return pl.pallas_call(
        functools.partial(correlate_kernel, scale=scale, first=first),
        out_shape=jax.ShapeDtypeStruct((fine_dev, 2, 128, inputs), BF16),
        in_specs=[pl.BlockSpec(memory_space=pltpu.SMEM)] + [whole] * 4 + [apart] * len(held),
        out_specs=apart,
        scratch_shapes=[
            pltpu.VMEM((fine_part, 2, 128, inputs), BF16),
            pltpu.SemaphoreType.DMA((fine_part,)),
        ],
        input_output_aliases={5: 0} if held else {},
        compiler_params=pltpu.CompilerParams(vmem_limit_bytes=LIMIT),
        cost_estimate=pl.CostEstimate(
            flops=2 * fine_part * 256 * inputs * 4 * rows,
            bytes_accessed=4_000_000,
            transcendentals=0,
        ),
        name="correlate",
    )(mine, *near, across, *held)


def local(voltage, fir_taps, zoom_width, zoom_shift, owner_slot):
    inputs_dev, blocks, samples = voltage.shape
    devices = lax.axis_size("chan")
    groups = lax.axis_size("tm")
    fine = owner_slot.shape[0]
    fine_dev = fine // devices
    up = [(i, i + 1) for i in range(groups - 1)]
    tail, rest, base = tail_part(voltage, fir_taps, zoom_width, zoom_shift, fine)
    tail = lax.ppermute(tail, "tm", up)
    window = own_part(voltage, rest, base, fine)
    slot, window = lax.optimization_barrier((owner_slot, window))
    place = place_part(slot[None, :])
    sent = send_part(window, tail, place)
    lanes = sent.shape[1]
    received = lax.all_to_all(
        sent.reshape(devices, fine_dev // 2, 2, lanes), "chan", split_axis=0, concat_axis=0, tiled=True
    )
    own = unpack(received.reshape(fine, lanes), fine_dev, inputs_dev)

    def around(turn):
        pairs = []
        for c in range(devices):
            for g in range(groups):
                to = (g + (turn if c % 2 == 0 else -turn)) % groups
                pairs.append((c * groups + g, c * groups + to))
        return pairs

    both = ("chan", "tm")
    ahead = lax.ppermute(own, both, around(1))
    spectra = jnp.transpose(own.reshape(fine_dev, 2, blocks, own.shape[2]), (0, 2, 1, 3))
    later, spectra = lax.optimization_barrier((own, spectra))
    behind = lax.ppermute(later, both, around(-1))
    first = fine_dev * 9 // 14
    across_a = lax.ppermute(ahead[:first], both, around(1))
    across_b = lax.ppermute(ahead[first:], both, around(1))
    mine = (lax.axis_index("tm") * 128).astype(jnp.int32)[None]
    scale = 1.0 / (blocks * groups)
    near = (own, ahead, behind)
    summed = correlate(near, across_a, mine, scale, 0)
    summed = correlate(near, across_b, mine, scale, first, summed)
    return spectra, summed


def solution(mesh):
    return jax.shard_map(
        local,
        mesh=mesh,
        in_specs=(P("chan", "tm", None), P(), P(), P(), P()),
        out_specs=(P("chan", "tm", None, None), P("chan", None, "tm", None)),
        check_vma=False,
    )
```

```python
import functools
import math

import jax
import jax.numpy as jnp
from jax import lax
from jax.experimental import pallas as pl
from jax.experimental.pallas import tpu as pltpu
from jax.sharding import PartitionSpec as P

VMEM = pltpu.VMEM
BF16 = jnp.bfloat16
F32 = jnp.float32
LIMIT = 32 * 1024 * 1024
MOST = 64 * 1000 * 1000
WIDE = 272


def dft_weights(phases, coarse):
    shape = (2 * phases, 2 * phases * coarse)
    source = lax.broadcasted_iota(jnp.int32, shape, 0)
    target = lax.broadcasted_iota(jnp.int32, shape, 1)
    j, p = source % phases, source // phases
    b, d, q = target % phases, (target // phases) % coarse, target // (phases * coarse)
    turn = (j * b + jnp.where(p == q, 0, jnp.where(q == 0, 3, 1) * phases // 4)) % phases
    table = jnp.zeros(shape, F32)
    for k in range(phases):
        exact = round(math.cos(2.0 * math.pi * k / phases), 15) / math.sqrt(phases)
        table = jnp.where(turn == k, jnp.float32(exact), table)
    return split_sum(jnp.concatenate([jnp.where(d == c, table, 0.0) for c in range(coarse)], 0))


def spread_taps(taps):
    phases = taps.shape[1]
    wide = jnp.concatenate([taps, jnp.zeros((taps.shape[0], 128 - phases), F32)], 1)
    while phases < 128:
        wide = wide + pltpu.roll(wide, phases, 1)
        phases *= 2
    return wide


def tap_tables(taps):
    row = lax.broadcasted_iota(jnp.int32, (8, 128), 0)
    tap = [jnp.broadcast_to(taps[m : m + 1, :], (8, 128)) for m in range(taps.shape[0])]
    zero = jnp.zeros((8, 128), F32)
    same = [jnp.where(row >= k, tap[k], zero) for k in range(1, 8)]
    beyond = [jnp.where(row < k, tap[8 + k], zero) for k in range(1, 4)]
    before = [jnp.where(row < k, tap[k], tap[8 + k] if k < 4 else zero) for k in range(1, 8)]
    return tap[0], tap[8], same, before, beyond


def split_sum(value):
    high = value.astype(BF16)
    return high, (value - high.astype(F32)).astype(BF16)


def fetch(sems, *pairs):
    copies = [
        pltpu.make_async_copy(source, target, sems.at[i]) for i, (source, target) in enumerate(pairs)
    ]
    for copy in copies:
        copy.start()
    return copies


def window_table(krow):
    shape = (WIDE, krow.shape[1])
    row = lax.broadcasted_iota(jnp.int32, shape, 0).astype(jnp.int16)
    column = jnp.broadcast_to(krow, shape).astype(jnp.int16)
    return jnp.where(row == column, jnp.ones(shape, BF16), jnp.zeros(shape, BF16))


def store_windows(window_ref, base, picked, step):
    base = pl.multiple_of(base, 16)
    lanes = slice(0, picked.shape[1])
    if step > 0:
        meet = pl.ds(base, 16)
        window_ref[meet, lanes] = window_ref[meet, lanes] + picked[:16]
        window_ref[pl.ds(pl.multiple_of(base + 16, 16), WIDE - 16), lanes] = picked[16:]
    else:
        window_ref[0:WIDE, lanes] = picked


def tail_kernel(
    width_from, shift_from, voltage_ref, taps_from,
    out_ref, rest_ref, base_ref,
    width_ref, shift_ref, taps_ref, held_ref, member_ref, split_high_ref, split_low_ref, table_ref, window_ref, sems,
):
    inputs, _, samples = held_ref.shape
    fine = window_ref.shape[0] - 256
    lanes = 128
    phases = 16
    copies = fetch(
        sems,
        (width_from, width_ref),
        (shift_from, shift_ref),
        (taps_from, taps_ref),
        (voltage_ref, held_ref),
    )
    high_table, low_table = dft_weights(phases, 8)
    weights = jnp.concatenate([high_table, high_table, low_table], 0)
    copies[0].wait()
    copies[1].wait()
    lane = lax.broadcasted_iota(jnp.int32, (1, lanes), 1)
    place = lane // phases
    bins = lane % phases
    first = jnp.int32(0)
    bases = []
    for step in range(samples // 512):
        base = (first // 16) * 16
        base_ref[step] = base
        bases.append(base)
        rows = []
        for half in range(2):
            width = jnp.zeros((1, lanes), jnp.int32)
            shift = jnp.zeros((1, lanes), jnp.int32)
            begin = jnp.zeros((1, lanes), jnp.int32)
            for c in range(8):
                at = step * 16 + half * 8 + c
                here = place == c
                wide = width_ref[at]
                width = jnp.where(here, wide, width)
                shift = jnp.where(here, shift_ref[at], shift)
                begin = jnp.where(here, first, begin)
                first = first + wide
            room = (phases + 1 - width).astype(F32)
            whole = jnp.floor((shift.astype(F32) + 0.5) / room)
            start = shift - (whole * room).astype(jnp.int32)
            offset = bins - start
            inside = (offset >= 0) & (offset < width)
            rows.append(jnp.where(inside, begin + offset, -1))
        krow = jnp.concatenate(rows, 1) - base
        rest_ref[step : step + 1, :] = krow.astype(F32)
        member_ref[step * WIDE : (step + 1) * WIDE, :] = window_table(krow)

    copies[2].wait()
    taps = spread_taps(taps_ref[...])
    rest_ref[16 : 16 + taps.shape[0], 0:lanes] = taps
    _, eighth, _, before, beyond = tap_tables(taps)
    window_ref[:, 96:lanes] = jnp.zeros((window_ref.shape[0], lanes - 96), F32)
    copies[3].wait()

    def group(step, carry):
        for sub in range(2):
            spot = pl.ds(pl.multiple_of(step * 256 + sub * lanes, lanes), lanes)
            tops, bottoms = [], []
            for i in range(inputs):
                series = held_ref[i, :, spot].astype(F32)
                older, recent = series[:8], series[8:]
                top = eighth * recent
                bottom = jnp.zeros((8, lanes), F32)
                for k in range(1, 8):
                    recent_k = pltpu.roll(recent, k, 0)
                    top = top + before[k - 1] * recent_k
                    if k < 4:
                        top = top + beyond[k - 1] * pltpu.roll(older, k, 0)
                        bottom = bottom + beyond[k - 1] * recent_k
                tops.append(top)
                bottoms.append(bottom if i % 2 == 0 else pltpu.roll(bottom, 4, 0))
            packed = [bottoms[i] + bottoms[i + 1] for i in range(0, inputs, 2)]
            high, low = split_sum(jnp.concatenate(tops + packed, 0))
            at = pl.ds(pl.multiple_of(step * 48, 16), 48)
            split_high_ref[at, sub * lanes : (sub + 1) * lanes] = high
            split_low_ref[at, sub * lanes : (sub + 1) * lanes] = low
        return carry

    lax.fori_loop(0, samples // 256, group, 0)
    for step in range(samples // 1024):
        at = slice(step * 192, step * 192 + 192)
        high = split_high_ref[at, :]
        split = jnp.concatenate([high, split_low_ref[at, :], high], 1)
        spectra = jnp.dot(split, weights, preferred_element_type=F32).astype(BF16)
        for j in range(4):
            for q in range(2):
                to = (step * 2 + j // 2) * 96
                half = slice((j % 2) * lanes, (j % 2 + 1) * lanes)
                piece = spectra[j * 48 : (j + 1) * 48, q * lanes : (q + 1) * lanes]
                table_ref[to + q * 32 : to + q * 32 + 32, half] = piece[:32]
                table_ref[to + 64 + q * 16 : to + 64 + q * 16 + 16, half] = piece[32:]
    for step in range(samples // 512):
        picked = lax.dot_general(
            member_ref[step * WIDE : (step + 1) * WIDE, :],
            table_ref[step * 96 : (step + 1) * 96, :],
            (((1,), (1,)), ((), ())),
            preferred_element_type=F32,
        )
        store_windows(window_ref, bases[step], picked, step)
    half, quarter = fine // 2, fine // 4
    at = lax.broadcasted_iota(jnp.int32, (half, lanes), 1)
    out_ref[0:half, :] = jnp.where(
        at < 64, window_ref[0:half, :], pltpu.roll(window_ref[half:fine, :], 64, 1)
    ).astype(BF16)
    at = lax.broadcasted_iota(jnp.int32, (quarter, lanes), 1)
    packed = jnp.zeros((quarter, lanes), F32)
    for j in range(4):
        moved = pltpu.roll(window_ref[j * quarter : (j + 1) * quarter, :], (64 + j * 32) % lanes, 1)
        packed = jnp.where(at // 32 == j, moved, packed)
    out_ref[half : half + quarter, :] = packed.astype(BF16)


def own_kernel(
    base_from, voltage_ref, rest_from,
    window_ref,
    base_ref, rest_ref, held_ref, split_high_ref, split_low_ref, table_ref, sems,
):
    inputs, blocks, samples = held_ref.shape
    lanes = 128
    copies = fetch(sems, (rest_from, rest_ref), (base_from, base_ref), (voltage_ref, held_ref))
    high_table, low_table = dft_weights(16, 8)
    weights = jnp.concatenate([high_table, high_table, low_table], 0)
    for copy in copies:
        copy.wait()
    first, eighth, same, before, _ = tap_tables(rest_ref[16:28, 0:lanes])

    def group(step, carry):
        for i in range(inputs):
            for sub in range(2):
                spot = pl.ds(pl.multiple_of(step * 256 + sub * lanes, lanes), lanes)
                series = held_ref[i, :, spot].astype(F32)
                early, late = series[:8], series[8:]
                top = first * early
                bottom = first * late + eighth * early
                for k in range(1, 8):
                    early_k = pltpu.roll(early, k, 0)
                    top = top + same[k - 1] * early_k
                    bottom = bottom + before[k - 1] * early_k
                    bottom = bottom + same[k - 1] * pltpu.roll(late, k, 0)
                at = pl.ds(pl.multiple_of(step * 64 + i * blocks, blocks), blocks)
                high, low = split_sum(jnp.concatenate([top, bottom], 0))
                split_high_ref[at, sub * lanes : (sub + 1) * lanes] = high
                split_low_ref[at, sub * lanes : (sub + 1) * lanes] = low
        return carry

    lax.fori_loop(0, samples // 256, group, 0)
    for step in range(samples // 1024):
        at = slice(step * 256, step * 256 + 256)
        high = split_high_ref[at, :]
        split = jnp.concatenate([high, split_low_ref[at, :], high], 1)
        parts = split_sum(jnp.dot(split, weights, preferred_element_type=F32))
        for j in range(4):
            for q in range(2):
                for p in range(2):
                    to = (step * 2 + j // 2) * 256 + p * 128 + q * 64
                    table_ref[to : to + 64, (j % 2) * 128 : (j % 2) * 128 + 128] = parts[p][
                        j * 64 : (j + 1) * 64, q * 128 : (q + 1) * 128
                    ]
    for step in range(samples // 512):
        picked = lax.dot_general(
            window_table(rest_ref[step : step + 1, :].astype(jnp.int32)),
            table_ref[step * 256 : (step + 1) * 256, :],
            (((1,), (1,)), ((), ())),
            preferred_element_type=F32,
        )
        store_windows(window_ref, base_ref[step], picked[:, :lanes] + picked[:, lanes:], step)


def place_kernel(slot_ref, place_ref):
    fine = slot_ref.shape[1]
    rows = 16
    row = lax.broadcasted_iota(jnp.int32, (rows, fine), 0)
    slot = jnp.broadcast_to(slot_ref[...], (rows, fine))
    row, slot = row.astype(jnp.int16), slot.astype(jnp.int16)
    one, zero = jnp.ones((rows, fine), BF16), jnp.zeros((rows, fine), BF16)

    def places(step, carry):
        at = pl.multiple_of(step * rows, rows)
        here = row + at.astype(jnp.int16)
        place_ref[pl.ds(at, rows), :] = jnp.where(here == slot, one, zero)
        return carry

    lax.fori_loop(0, place_ref.shape[0] // rows, places, 0, unroll=4)


def send_kernel(window_ref, tail_ref, place_ref, out_ref, bins_ref):
    fine, lanes = bins_ref.shape
    half, quarter = fine // 2, fine // 4
    source = lax.broadcasted_iota(jnp.int32, (lanes, lanes), 0)
    target = lax.broadcasted_iota(jnp.int32, (lanes, lanes), 1)
    late = source - 64
    early_lane = (source // 8) * 16 + source % 8
    late_lane = (late // 4) * 16 + 8 + late % 4
    spread = jnp.where(
        ((source < 64) & (target == early_lane))
        | ((source >= 64) & (source < 96) & (late % 4 < 3) & (target == late_lane)),
        1.0,
        0.0,
    ).astype(BF16)
    at = lax.broadcasted_iota(jnp.int32, (quarter, lanes), 1)
    for j in range(4):
        rows = slice((j % 2) * quarter, (j % 2 + 1) * quarter)
        early = tail_ref[rows, :].astype(F32)
        if j >= 2:
            early = pltpu.roll(early, 64, 1)
        late = tail_ref[half : half + quarter, :].astype(F32)
        late = pltpu.roll(late, (64 - j * 32) % lanes, 1)
        tail = jnp.where(at < 64, early, late).astype(BF16)
        added = jnp.dot(tail, spread, preferred_element_type=F32)
        rows = slice(j * quarter, (j + 1) * quarter)
        bins_ref[rows, :] = (window_ref[rows, :] + added).astype(BF16)
    step_rows = 448
    for step in range(out_ref.shape[0] // step_rows):
        at = slice(step * step_rows, (step + 1) * step_rows)
        out_ref[at, :] = jnp.dot(
            place_ref[at, :], bins_ref[...], preferred_element_type=F32
        ).astype(BF16)


def unpack_kernel(received_ref, out_ref, wide_ref, *, inputs_dev):
    fine_dev = out_ref.shape[0]
    rows, lanes = received_ref.shape
    devices = rows // fine_dev
    blocks = lanes // (2 * inputs_dev)
    wide_ref[...] = received_ref[...].astype(F32)
    inputs = inputs_dev * devices
    source = lax.broadcasted_iota(jnp.int32, (inputs, inputs), 0)
    target = lax.broadcasted_iota(jnp.int32, (inputs, inputs), 1)
    spread = jnp.where((source % devices) * inputs_dev + source // devices == target, 1.0, 0.0)
    spread = spread.astype(BF16)
    pieces = []
    for channel in range(fine_dev):
        turned = wide_ref[pl.ds(channel, devices, stride=fine_dev), :].T.astype(BF16)
        for q in range(2):
            pieces.append(
                jnp.concatenate(
                    [
                        turned[(q * inputs_dev + i) * blocks : (q * inputs_dev + i + 1) * blocks, :]
                        for i in range(inputs_dev)
                    ],
                    1,
                )
            )
    joined = jnp.concatenate(pieces, 0)
    placed = jnp.dot(joined, spread, preferred_element_type=F32).astype(BF16)
    out_ref[...] = placed.reshape(out_ref.shape)


def correlate_kernel(mine_ref, own_ref, ahead_ref, behind_ref, across_ref, *rest, scale, first):
    out_ref, block_ref, sems = rest[-3:]
    mine = pl.ds(pl.multiple_of(mine_ref[0], 128), 128)
    half = own_ref.shape[1] // 2
    copies = []
    for channel in range(across_ref.shape[0]):
        refs = [ref.at[first + channel] for ref in (own_ref, ahead_ref, behind_ref)]
        refs.append(across_ref.at[channel])
        right = jnp.concatenate([ref[...] for ref in refs], 0)
        real, imag = [], []
        for ref in refs:
            block = ref[:, mine]
            real.append(block)
            imag.append(block[half:])
            imag.append(-block[:half])
        left = jnp.concatenate([jnp.concatenate(real, 0), jnp.concatenate(imag, 0)], 1)
        product = lax.dot_general(
            left, right, (((0,), (0,)), ((), ())), preferred_element_type=F32
        )
        product = (product * scale).astype(BF16)
        block_ref[channel, 0] = product[:128]
        block_ref[channel, 1] = product[128:]
        copies.append(
            pltpu.make_async_copy(
                block_ref.at[channel], out_ref.at[first + channel], sems.at[channel]
            )
        )
        copies[-1].start()
    for copy in copies:
        copy.wait()


WHOLE = pl.BlockSpec(memory_space=VMEM)
SCALARS = pl.BlockSpec(memory_space=pltpu.SMEM)
APART = pl.BlockSpec(memory_space=pl.ANY)


def tail_part(voltage, fir_taps, zoom_width, zoom_shift, fine):
    inputs_dev, blocks, samples = voltage.shape
    groups = samples // 256
    return pl.pallas_call(
        tail_kernel,
        out_shape=(
            jax.ShapeDtypeStruct((fine // 2 + fine // 4, 128), BF16),
            jax.ShapeDtypeStruct((32, 256), F32),
            jax.ShapeDtypeStruct((samples // 512,), jnp.int32),
        ),
        in_specs=[APART] * 4,
        out_specs=(WHOLE, WHOLE, SCALARS),
        scratch_shapes=[
            pltpu.SMEM(zoom_width.shape, jnp.int32),
            pltpu.SMEM(zoom_shift.shape, jnp.int32),
            pltpu.VMEM(fir_taps.shape, F32),
            pltpu.VMEM(voltage.shape, BF16),
            pltpu.VMEM((samples // 512 * WIDE, 256), BF16),
            pltpu.VMEM((groups * 48, 256), BF16),
            pltpu.VMEM((groups * 48, 256), BF16),
            pltpu.VMEM((groups * 48, 256), BF16),
            pltpu.VMEM((fine + 256, 128), F32),
            pltpu.SemaphoreType.DMA((4,)),
        ],
        compiler_params=pltpu.CompilerParams(vmem_limit_bytes=MOST),
        name="tail_part",
    )(zoom_width, zoom_shift, voltage, fir_taps)


def own_part(voltage, rest, base, fine):
    inputs_dev, blocks, samples = voltage.shape
    groups = samples // 256
    return pl.pallas_call(
        own_kernel,
        out_shape=jax.ShapeDtypeStruct((fine + 256, 128), F32),
        in_specs=[APART] * 3,
        out_specs=WHOLE,
        scratch_shapes=[
            pltpu.SMEM(base.shape, jnp.int32),
            pltpu.VMEM(rest.shape, F32),
            pltpu.VMEM(voltage.shape, BF16),
            pltpu.VMEM((groups * 64, 256), BF16),
            pltpu.VMEM((groups * 64, 256), BF16),
            pltpu.VMEM((groups * 128, 256), BF16),
            pltpu.SemaphoreType.DMA((3,)),
        ],
        compiler_params=pltpu.CompilerParams(vmem_limit_bytes=MOST),
        cost_estimate=pl.CostEstimate(flops=5_000_000_000, bytes_accessed=4_000_000, transcendentals=0),
        name="own_part",
    )(base, voltage, rest)


def place_part(slot):
    fine = slot.shape[1]
    return pl.pallas_call(
        place_kernel,
        out_shape=jax.ShapeDtypeStruct((fine, fine), BF16),
        in_specs=[WHOLE],
        out_specs=WHOLE,
        compiler_params=pltpu.CompilerParams(vmem_limit_bytes=LIMIT),
        cost_estimate=pl.CostEstimate(flops=5_000_000_000, bytes_accessed=4_000_000, transcendentals=0),
        name="place_part",
    )(slot)


def send_part(window, tail, place):
    slots, fine = place.shape
    return pl.pallas_call(
        send_kernel,
        out_shape=jax.ShapeDtypeStruct((slots, 128), BF16),
        in_specs=[WHOLE] * 3,
        out_specs=WHOLE,
        scratch_shapes=[pltpu.VMEM((fine, 128), BF16)],
        compiler_params=pltpu.CompilerParams(vmem_limit_bytes=LIMIT),
        name="send_part",
    )(window, tail, place)


def unpack(received, fine_dev, inputs_dev):
    rows, lanes = received.shape
    devices = rows // fine_dev
    blocks = lanes // (2 * inputs_dev)
    whole = pl.BlockSpec(memory_space=VMEM)
    return pl.pallas_call(
        functools.partial(unpack_kernel, inputs_dev=inputs_dev),
        out_shape=jax.ShapeDtypeStruct((fine_dev, 2 * blocks, devices * inputs_dev), BF16),
        in_specs=[whole],
        out_specs=whole,
        scratch_shapes=[pltpu.VMEM((rows, lanes), F32)],
        compiler_params=pltpu.CompilerParams(vmem_limit_bytes=LIMIT),
        name="unpack",
    )(received)


def correlate(near, across, mine, scale, first, earlier=None):
    fine_dev, rows, inputs = near[0].shape
    fine_part = across.shape[0]
    whole = pl.BlockSpec(memory_space=VMEM)
    apart = pl.BlockSpec(memory_space=pl.ANY)
    held = [] if earlier is None else [earlier]
    return pl.pallas_call(
        functools.partial(correlate_kernel, scale=scale, first=first),
        out_shape=jax.ShapeDtypeStruct((fine_dev, 2, 128, inputs), BF16),
        in_specs=[pl.BlockSpec(memory_space=pltpu.SMEM)] + [whole] * 4 + [apart] * len(held),
        out_specs=apart,
        scratch_shapes=[
            pltpu.VMEM((fine_part, 2, 128, inputs), BF16),
            pltpu.SemaphoreType.DMA((fine_part,)),
        ],
        input_output_aliases={5: 0} if held else {},
        compiler_params=pltpu.CompilerParams(vmem_limit_bytes=LIMIT),
        cost_estimate=pl.CostEstimate(
            flops=2 * fine_part * 256 * inputs * 4 * rows,
            bytes_accessed=4_000_000,
            transcendentals=0,
        ),
        name="correlate",
    )(mine, *near, across, *held)


def local(voltage, fir_taps, zoom_width, zoom_shift, owner_slot):
    inputs_dev, blocks, samples = voltage.shape
    devices = lax.axis_size("chan")
    groups = lax.axis_size("tm")
    fine = owner_slot.shape[0]
    fine_dev = fine // devices
    up = [(i, i + 1) for i in range(groups - 1)]
    tail, rest, base = tail_part(voltage, fir_taps, zoom_width, zoom_shift, fine)
    tail = lax.ppermute(tail, "tm", up)
    window = own_part(voltage, rest, base, fine)
    slot, window = lax.optimization_barrier((owner_slot, window))
    place = place_part(slot[None, :])
    sent = send_part(window, tail, place)
    lanes = sent.shape[1]
    received = lax.all_to_all(
        sent.reshape(devices, fine_dev // 2, 2, lanes), "chan", split_axis=0, concat_axis=0, tiled=True
    )
    own = unpack(received.reshape(fine, lanes), fine_dev, inputs_dev)

    def around(turn):
        pairs = []
        for c in range(devices):
            for g in range(groups):
                to = (g + (turn if c % 2 == 0 else -turn)) % groups
                pairs.append((c * groups + g, c * groups + to))
        return pairs

    both = ("chan", "tm")
    ahead = lax.ppermute(own, both, around(1))
    spectra = jnp.transpose(own.reshape(fine_dev, 2, blocks, own.shape[2]), (0, 2, 1, 3))
    later, spectra = lax.optimization_barrier((own, spectra))
    behind = lax.ppermute(later, both, around(-1))
    first = fine_dev * 8 // 14
    across_a = lax.ppermute(ahead[:first], both, around(1))
    across_b = lax.ppermute(ahead[first:], both, around(1))
    mine = (lax.axis_index("tm") * 128).astype(jnp.int32)[None]
    scale = 1.0 / (blocks * groups)
    near = (own, ahead, behind)
    summed = correlate(near, across_a, mine, scale, 0)
    summed = correlate(near, across_b, mine, scale, first, summed)
    return spectra, summed


def solution(mesh):
    return jax.shard_map(
        local,
        mesh=mesh,
        in_specs=(P("chan", "tm", None), P(), P(), P(), P()),
        out_specs=(P("chan", "tm", None, None), P("chan", None, "tm", None)),
        check_vma=False,
    )
```

```python
import functools
import math

import jax
import jax.numpy as jnp
from jax import lax
from jax.experimental import pallas as pl
from jax.experimental.pallas import tpu as pltpu
from jax.sharding import PartitionSpec as P

VMEM = pltpu.VMEM
BF16 = jnp.bfloat16
F32 = jnp.float32
LIMIT = 32 * 1024 * 1024
MOST = 64 * 1000 * 1000
WIDE = 272


def dft_weights(phases, coarse):
    shape = (2 * phases, 2 * phases * coarse)
    source = lax.broadcasted_iota(jnp.int32, shape, 0)
    target = lax.broadcasted_iota(jnp.int32, shape, 1)
    j, p = source % phases, source // phases
    b, d, q = target % phases, (target // phases) % coarse, target // (phases * coarse)
    turn = (j * b + jnp.where(p == q, 0, jnp.where(q == 0, 3, 1) * phases // 4)) % phases
    table = jnp.zeros(shape, F32)
    for k in range(phases):
        exact = round(math.cos(2.0 * math.pi * k / phases), 15) / math.sqrt(phases)
        table = jnp.where(turn == k, jnp.float32(exact), table)
    return split_sum(jnp.concatenate([jnp.where(d == c, table, 0.0) for c in range(coarse)], 0))


def spread_taps(taps):
    phases = taps.shape[1]
    wide = jnp.concatenate([taps, jnp.zeros((taps.shape[0], 128 - phases), F32)], 1)
    while phases < 128:
        wide = wide + pltpu.roll(wide, phases, 1)
        phases *= 2
    return wide


def tap_tables(taps):
    row = lax.broadcasted_iota(jnp.int32, (8, 128), 0)
    tap = [jnp.broadcast_to(taps[m : m + 1, :], (8, 128)) for m in range(taps.shape[0])]
    zero = jnp.zeros((8, 128), F32)
    same = [jnp.where(row >= k, tap[k], zero) for k in range(1, 8)]
    beyond = [jnp.where(row < k, tap[8 + k], zero) for k in range(1, 4)]
    before = [jnp.where(row < k, tap[k], tap[8 + k] if k < 4 else zero) for k in range(1, 8)]
    return tap[0], tap[8], same, before, beyond


def split_sum(value):
    high = value.astype(BF16)
    return high, (value - high.astype(F32)).astype(BF16)


def fetch(sems, *pairs):
    copies = [
        pltpu.make_async_copy(source, target, sems.at[i]) for i, (source, target) in enumerate(pairs)
    ]
    for copy in copies:
        copy.start()
    return copies


def window_table(krow):
    shape = (WIDE, krow.shape[1])
    row = lax.broadcasted_iota(jnp.int32, shape, 0).astype(jnp.int16)
    column = jnp.broadcast_to(krow, shape).astype(jnp.int16)
    return jnp.where(row == column, jnp.ones(shape, BF16), jnp.zeros(shape, BF16))


def store_windows(window_ref, base, picked, step):
    base = pl.multiple_of(base, 16)
    lanes = slice(0, picked.shape[1])
    if step > 0:
        meet = pl.ds(base, 16)
        window_ref[meet, lanes] = window_ref[meet, lanes] + picked[:16]
        window_ref[pl.ds(pl.multiple_of(base + 16, 16), WIDE - 16), lanes] = picked[16:]
    else:
        window_ref[0:WIDE, lanes] = picked


def tail_kernel(
    width_from, shift_from, voltage_ref, taps_from,
    out_ref, rest_ref, base_ref,
    width_ref, shift_ref, taps_ref, held_ref, member_ref, split_high_ref, split_low_ref, table_ref, window_ref, sems,
):
    inputs, _, samples = held_ref.shape
    fine = window_ref.shape[0] - 256
    lanes = 128
    phases = 16
    copies = fetch(
        sems,
        (width_from, width_ref),
        (shift_from, shift_ref),
        (taps_from, taps_ref),
        (voltage_ref, held_ref),
    )
    high_table, low_table = dft_weights(phases, 8)
    weights = jnp.concatenate([high_table, high_table, low_table], 0)
    copies[0].wait()
    copies[1].wait()
    lane = lax.broadcasted_iota(jnp.int32, (1, lanes), 1)
    place = lane // phases
    bins = lane % phases
    first = jnp.int32(0)
    bases = []
    for step in range(samples // 512):
        base = (first // 16) * 16
        base_ref[step] = base
        bases.append(base)
        rows = []
        for half in range(2):
            width = jnp.zeros((1, lanes), jnp.int32)
            shift = jnp.zeros((1, lanes), jnp.int32)
            begin = jnp.zeros((1, lanes), jnp.int32)
            for c in range(8):
                at = step * 16 + half * 8 + c
                here = place == c
                wide = width_ref[at]
                width = jnp.where(here, wide, width)
                shift = jnp.where(here, shift_ref[at], shift)
                begin = jnp.where(here, first, begin)
                first = first + wide
            room = (phases + 1 - width).astype(F32)
            whole = jnp.floor((shift.astype(F32) + 0.5) / room)
            start = shift - (whole * room).astype(jnp.int32)
            offset = bins - start
            inside = (offset >= 0) & (offset < width)
            rows.append(jnp.where(inside, begin + offset, -1))
        krow = jnp.concatenate(rows, 1) - base
        rest_ref[step : step + 1, :] = krow.astype(F32)
        member_ref[step * WIDE : (step + 1) * WIDE, :] = window_table(krow)

    copies[2].wait()
    taps = spread_taps(taps_ref[...])
    rest_ref[16 : 16 + taps.shape[0], 0:lanes] = taps
    _, eighth, _, before, beyond = tap_tables(taps)
    window_ref[:, 96:lanes] = jnp.zeros((window_ref.shape[0], lanes - 96), F32)
    copies[3].wait()

    def group(step, carry):
        for sub in range(2):
            spot = pl.ds(pl.multiple_of(step * 256 + sub * lanes, lanes), lanes)
            tops, bottoms = [], []
            for i in range(inputs):
                series = held_ref[i, :, spot].astype(F32)
                older, recent = series[:8], series[8:]
                top = eighth * recent
                bottom = jnp.zeros((8, lanes), F32)
                for k in range(1, 8):
                    recent_k = pltpu.roll(recent, k, 0)
                    top = top + before[k - 1] * recent_k
                    if k < 4:
                        top = top + beyond[k - 1] * pltpu.roll(older, k, 0)
                        bottom = bottom + beyond[k - 1] * recent_k
                tops.append(top)
                bottoms.append(bottom if i % 2 == 0 else pltpu.roll(bottom, 4, 0))
            packed = [bottoms[i] + bottoms[i + 1] for i in range(0, inputs, 2)]
            high, low = split_sum(jnp.concatenate(tops + packed, 0))
            at = pl.ds(pl.multiple_of(step * 48, 16), 48)
            split_high_ref[at, sub * lanes : (sub + 1) * lanes] = high
            split_low_ref[at, sub * lanes : (sub + 1) * lanes] = low
        return carry

    lax.fori_loop(0, samples // 256, group, 0, unroll=4)
    for step in range(samples // 1024):
        at = slice(step * 192, step * 192 + 192)
        high = split_high_ref[at, :]
        split = jnp.concatenate([high, split_low_ref[at, :], high], 1)
        spectra = jnp.dot(split, weights, preferred_element_type=F32).astype(BF16)
        for j in range(4):
            for q in range(2):
                to = (step * 2 + j // 2) * 96
                half = slice((j % 2) * lanes, (j % 2 + 1) * lanes)
                piece = spectra[j * 48 : (j + 1) * 48, q * lanes : (q + 1) * lanes]
                table_ref[to + q * 32 : to + q * 32 + 32, half] = piece[:32]
                table_ref[to + 64 + q * 16 : to + 64 + q * 16 + 16, half] = piece[32:]
    for step in range(samples // 512):
        picked = lax.dot_general(
            member_ref[step * WIDE : (step + 1) * WIDE, :],
            table_ref[step * 96 : (step + 1) * 96, :],
            (((1,), (1,)), ((), ())),
            preferred_element_type=F32,
        )
        store_windows(window_ref, bases[step], picked, step)
    half, quarter = fine // 2, fine // 4
    at = lax.broadcasted_iota(jnp.int32, (half, lanes), 1)
    out_ref[0:half, :] = jnp.where(
        at < 64, window_ref[0:half, :], pltpu.roll(window_ref[half:fine, :], 64, 1)
    ).astype(BF16)
    at = lax.broadcasted_iota(jnp.int32, (quarter, lanes), 1)
    packed = jnp.zeros((quarter, lanes), F32)
    for j in range(4):
        moved = pltpu.roll(window_ref[j * quarter : (j + 1) * quarter, :], (64 + j * 32) % lanes, 1)
        packed = jnp.where(at // 32 == j, moved, packed)
    out_ref[half : half + quarter, :] = packed.astype(BF16)


def own_kernel(
    base_from, voltage_ref, rest_from,
    window_ref,
    base_ref, rest_ref, held_ref, split_high_ref, split_low_ref, table_ref, sems,
):
    inputs, blocks, samples = held_ref.shape
    lanes = 128
    copies = fetch(sems, (rest_from, rest_ref), (base_from, base_ref), (voltage_ref, held_ref))
    high_table, low_table = dft_weights(16, 8)
    weights = jnp.concatenate([high_table, high_table, low_table], 0)
    for copy in copies:
        copy.wait()
    first, eighth, same, before, _ = tap_tables(rest_ref[16:28, 0:lanes])

    def group(step, carry):
        for i in range(inputs):
            for sub in range(2):
                spot = pl.ds(pl.multiple_of(step * 256 + sub * lanes, lanes), lanes)
                series = held_ref[i, :, spot].astype(F32)
                early, late = series[:8], series[8:]
                top = first * early
                bottom = first * late + eighth * early
                for k in range(1, 8):
                    early_k = pltpu.roll(early, k, 0)
                    top = top + same[k - 1] * early_k
                    bottom = bottom + before[k - 1] * early_k
                    bottom = bottom + same[k - 1] * pltpu.roll(late, k, 0)
                at = pl.ds(pl.multiple_of(step * 64 + i * blocks, blocks), blocks)
                high, low = split_sum(jnp.concatenate([top, bottom], 0))
                split_high_ref[at, sub * lanes : (sub + 1) * lanes] = high
                split_low_ref[at, sub * lanes : (sub + 1) * lanes] = low
        return carry

    lax.fori_loop(0, samples // 256, group, 0, unroll=2)
    for step in range(samples // 1024):
        at = slice(step * 256, step * 256 + 256)
        high = split_high_ref[at, :]
        split = jnp.concatenate([high, split_low_ref[at, :], high], 1)
        parts = split_sum(jnp.dot(split, weights, preferred_element_type=F32))
        for j in range(4):
            for q in range(2):
                for p in range(2):
                    to = (step * 2 + j // 2) * 256 + p * 128 + q * 64
                    table_ref[to : to + 64, (j % 2) * 128 : (j % 2) * 128 + 128] = parts[p][
                        j * 64 : (j + 1) * 64, q * 128 : (q + 1) * 128
                    ]
    for step in range(samples // 512):
        picked = lax.dot_general(
            window_table(rest_ref[step : step + 1, :].astype(jnp.int32)),
            table_ref[step * 256 : (step + 1) * 256, :],
            (((1,), (1,)), ((), ())),
            preferred_element_type=F32,
        )
        store_windows(window_ref, base_ref[step], picked[:, :lanes] + picked[:, lanes:], step)


def place_kernel(slot_ref, place_ref):
    fine = slot_ref.shape[1]
    rows = 16
    row = lax.broadcasted_iota(jnp.int32, (rows, fine), 0)
    slot = jnp.broadcast_to(slot_ref[...], (rows, fine))
    row, slot = row.astype(jnp.int16), slot.astype(jnp.int16)
    one, zero = jnp.ones((rows, fine), BF16), jnp.zeros((rows, fine), BF16)

    def places(step, carry):
        at = pl.multiple_of(step * rows, rows)
        here = row + at.astype(jnp.int16)
        place_ref[pl.ds(at, rows), :] = jnp.where(here == slot, one, zero)
        return carry

    lax.fori_loop(0, place_ref.shape[0] // rows, places, 0, unroll=4)


def send_kernel(window_ref, tail_ref, place_ref, out_ref, bins_ref):
    fine, lanes = bins_ref.shape
    half, quarter = fine // 2, fine // 4
    source = lax.broadcasted_iota(jnp.int32, (lanes, lanes), 0)
    target = lax.broadcasted_iota(jnp.int32, (lanes, lanes), 1)
    late = source - 64
    early_lane = (source // 8) * 16 + source % 8
    late_lane = (late // 4) * 16 + 8 + late % 4
    spread = jnp.where(
        ((source < 64) & (target == early_lane))
        | ((source >= 64) & (source < 96) & (late % 4 < 3) & (target == late_lane)),
        1.0,
        0.0,
    ).astype(BF16)
    at = lax.broadcasted_iota(jnp.int32, (quarter, lanes), 1)
    for j in range(4):
        rows = slice((j % 2) * quarter, (j % 2 + 1) * quarter)
        early = tail_ref[rows, :].astype(F32)
        if j >= 2:
            early = pltpu.roll(early, 64, 1)
        late = tail_ref[half : half + quarter, :].astype(F32)
        late = pltpu.roll(late, (64 - j * 32) % lanes, 1)
        tail = jnp.where(at < 64, early, late).astype(BF16)
        added = jnp.dot(tail, spread, preferred_element_type=F32)
        rows = slice(j * quarter, (j + 1) * quarter)
        bins_ref[rows, :] = (window_ref[rows, :] + added).astype(BF16)
    step_rows = 448
    for step in range(out_ref.shape[0] // step_rows):
        at = slice(step * step_rows, (step + 1) * step_rows)
        out_ref[at, :] = jnp.dot(
            place_ref[at, :], bins_ref[...], preferred_element_type=F32
        ).astype(BF16)


def unpack_kernel(received_ref, out_ref, wide_ref, *, inputs_dev):
    fine_dev = out_ref.shape[0]
    rows, lanes = received_ref.shape
    devices = rows // fine_dev
    blocks = lanes // (2 * inputs_dev)
    wide_ref[...] = received_ref[...].astype(F32)
    inputs = inputs_dev * devices
    source = lax.broadcasted_iota(jnp.int32, (inputs, inputs), 0)
    target = lax.broadcasted_iota(jnp.int32, (inputs, inputs), 1)
    spread = jnp.where((source % devices) * inputs_dev + source // devices == target, 1.0, 0.0)
    spread = spread.astype(BF16)
    pieces = []
    for channel in range(fine_dev):
        turned = wide_ref[pl.ds(channel, devices, stride=fine_dev), :].T.astype(BF16)
        for q in range(2):
            pieces.append(
                jnp.concatenate(
                    [
                        turned[(q * inputs_dev + i) * blocks : (q * inputs_dev + i + 1) * blocks, :]
                        for i in range(inputs_dev)
                    ],
                    1,
                )
            )
    joined = jnp.concatenate(pieces, 0)
    placed = jnp.dot(joined, spread, preferred_element_type=F32).astype(BF16)
    out_ref[...] = placed.reshape(out_ref.shape)


def correlate_kernel(mine_ref, own_ref, ahead_ref, behind_ref, across_ref, *rest, scale, first):
    out_ref, block_ref, sems = rest[-3:]
    mine = pl.ds(pl.multiple_of(mine_ref[0], 128), 128)
    half = own_ref.shape[1] // 2
    copies = []
    for channel in range(across_ref.shape[0]):
        refs = [ref.at[first + channel] for ref in (own_ref, ahead_ref, behind_ref)]
        refs.append(across_ref.at[channel])
        right = jnp.concatenate([ref[...] for ref in refs], 0)
        real, imag = [], []
        for ref in refs:
            block = ref[:, mine]
            real.append(block)
            imag.append(block[half:])
            imag.append(-block[:half])
        left = jnp.concatenate([jnp.concatenate(real, 0), jnp.concatenate(imag, 0)], 1)
        product = lax.dot_general(
            left, right, (((0,), (0,)), ((), ())), preferred_element_type=F32
        )
        product = (product * scale).astype(BF16)
        block_ref[channel, 0] = product[:128]
        block_ref[channel, 1] = product[128:]
        copies.append(
            pltpu.make_async_copy(
                block_ref.at[channel], out_ref.at[first + channel], sems.at[channel]
            )
        )
        copies[-1].start()
    for copy in copies:
        copy.wait()


WHOLE = pl.BlockSpec(memory_space=VMEM)
SCALARS = pl.BlockSpec(memory_space=pltpu.SMEM)
APART = pl.BlockSpec(memory_space=pl.ANY)


def tail_part(voltage, fir_taps, zoom_width, zoom_shift, fine):
    inputs_dev, blocks, samples = voltage.shape
    groups = samples // 256
    return pl.pallas_call(
        tail_kernel,
        out_shape=(
            jax.ShapeDtypeStruct((fine // 2 + fine // 4, 128), BF16),
            jax.ShapeDtypeStruct((32, 256), F32),
            jax.ShapeDtypeStruct((samples // 512,), jnp.int32),
        ),
        in_specs=[APART] * 4,
        out_specs=(WHOLE, WHOLE, SCALARS),
        scratch_shapes=[
            pltpu.SMEM(zoom_width.shape, jnp.int32),
            pltpu.SMEM(zoom_shift.shape, jnp.int32),
            pltpu.VMEM(fir_taps.shape, F32),
            pltpu.VMEM(voltage.shape, BF16),
            pltpu.VMEM((samples // 512 * WIDE, 256), BF16),
            pltpu.VMEM((groups * 48, 256), BF16),
            pltpu.VMEM((groups * 48, 256), BF16),
            pltpu.VMEM((groups * 48, 256), BF16),
            pltpu.VMEM((fine + 256, 128), F32),
            pltpu.SemaphoreType.DMA((4,)),
        ],
        compiler_params=pltpu.CompilerParams(vmem_limit_bytes=MOST),
        name="tail_part",
    )(zoom_width, zoom_shift, voltage, fir_taps)


def own_part(voltage, rest, base, fine):
    inputs_dev, blocks, samples = voltage.shape
    groups = samples // 256
    return pl.pallas_call(
        own_kernel,
        out_shape=jax.ShapeDtypeStruct((fine + 256, 128), F32),
        in_specs=[APART] * 3,
        out_specs=WHOLE,
        scratch_shapes=[
            pltpu.SMEM(base.shape, jnp.int32),
            pltpu.VMEM(rest.shape, F32),
            pltpu.VMEM(voltage.shape, BF16),
            pltpu.VMEM((groups * 64, 256), BF16),
            pltpu.VMEM((groups * 64, 256), BF16),
            pltpu.VMEM((groups * 128, 256), BF16),
            pltpu.SemaphoreType.DMA((3,)),
        ],
        compiler_params=pltpu.CompilerParams(vmem_limit_bytes=MOST),
        cost_estimate=pl.CostEstimate(flops=5_000_000_000, bytes_accessed=4_000_000, transcendentals=0),
        name="own_part",
    )(base, voltage, rest)


def place_part(slot):
    fine = slot.shape[1]
    return pl.pallas_call(
        place_kernel,
        out_shape=jax.ShapeDtypeStruct((fine, fine), BF16),
        in_specs=[WHOLE],
        out_specs=WHOLE,
        compiler_params=pltpu.CompilerParams(vmem_limit_bytes=LIMIT),
        cost_estimate=pl.CostEstimate(flops=5_000_000_000, bytes_accessed=4_000_000, transcendentals=0),
        name="place_part",
    )(slot)


def send_part(window, tail, place):
    slots, fine = place.shape
    return pl.pallas_call(
        send_kernel,
        out_shape=jax.ShapeDtypeStruct((slots, 128), BF16),
        in_specs=[WHOLE] * 3,
        out_specs=WHOLE,
        scratch_shapes=[pltpu.VMEM((fine, 128), BF16)],
        compiler_params=pltpu.CompilerParams(vmem_limit_bytes=LIMIT),
        name="send_part",
    )(window, tail, place)


def unpack(received, fine_dev, inputs_dev):
    rows, lanes = received.shape
    devices = rows // fine_dev
    blocks = lanes // (2 * inputs_dev)
    whole = pl.BlockSpec(memory_space=VMEM)
    return pl.pallas_call(
        functools.partial(unpack_kernel, inputs_dev=inputs_dev),
        out_shape=jax.ShapeDtypeStruct((fine_dev, 2 * blocks, devices * inputs_dev), BF16),
        in_specs=[whole],
        out_specs=whole,
        scratch_shapes=[pltpu.VMEM((rows, lanes), F32)],
        compiler_params=pltpu.CompilerParams(vmem_limit_bytes=LIMIT),
        name="unpack",
    )(received)


def correlate(near, across, mine, scale, first, earlier=None):
    fine_dev, rows, inputs = near[0].shape
    fine_part = across.shape[0]
    whole = pl.BlockSpec(memory_space=VMEM)
    apart = pl.BlockSpec(memory_space=pl.ANY)
    held = [] if earlier is None else [earlier]
    return pl.pallas_call(
        functools.partial(correlate_kernel, scale=scale, first=first),
        out_shape=jax.ShapeDtypeStruct((fine_dev, 2, 128, inputs), BF16),
        in_specs=[pl.BlockSpec(memory_space=pltpu.SMEM)] + [whole] * 4 + [apart] * len(held),
        out_specs=apart,
        scratch_shapes=[
            pltpu.VMEM((fine_part, 2, 128, inputs), BF16),
            pltpu.SemaphoreType.DMA((fine_part,)),
        ],
        input_output_aliases={5: 0} if held else {},
        compiler_params=pltpu.CompilerParams(vmem_limit_bytes=LIMIT),
        cost_estimate=pl.CostEstimate(
            flops=2 * fine_part * 256 * inputs * 4 * rows,
            bytes_accessed=4_000_000,
            transcendentals=0,
        ),
        name="correlate",
    )(mine, *near, across, *held)


def local(voltage, fir_taps, zoom_width, zoom_shift, owner_slot):
    inputs_dev, blocks, samples = voltage.shape
    devices = lax.axis_size("chan")
    groups = lax.axis_size("tm")
    fine = owner_slot.shape[0]
    fine_dev = fine // devices
    up = [(i, i + 1) for i in range(groups - 1)]
    tail, rest, base = tail_part(voltage, fir_taps, zoom_width, zoom_shift, fine)
    tail = lax.ppermute(tail, "tm", up)
    window = own_part(voltage, rest, base, fine)
    slot, window = lax.optimization_barrier((owner_slot, window))
    place = place_part(slot[None, :])
    sent = send_part(window, tail, place)
    lanes = sent.shape[1]
    received = lax.all_to_all(
        sent.reshape(devices, fine_dev // 2, 2, lanes), "chan", split_axis=0, concat_axis=0, tiled=True
    )
    own = unpack(received.reshape(fine, lanes), fine_dev, inputs_dev)

    def around(turn):
        pairs = []
        for c in range(devices):
            for g in range(groups):
                to = (g + (turn if c % 2 == 0 else -turn)) % groups
                pairs.append((c * groups + g, c * groups + to))
        return pairs

    both = ("chan", "tm")
    ahead = lax.ppermute(own, both, around(1))
    spectra = jnp.transpose(own.reshape(fine_dev, 2, blocks, own.shape[2]), (0, 2, 1, 3))
    later, spectra = lax.optimization_barrier((own, spectra))
    behind = lax.ppermute(later, both, around(-1))
    first = fine_dev * 10 // 14
    across_a = lax.ppermute(ahead[:first], both, around(1))
    across_b = lax.ppermute(ahead[first:], both, around(1))
    mine = (lax.axis_index("tm") * 128).astype(jnp.int32)[None]
    scale = 1.0 / (blocks * groups)
    near = (own, ahead, behind)
    summed = correlate(near, across_a, mine, scale, 0)
    summed = correlate(near, across_b, mine, scale, first, summed)
    return spectra, summed


def solution(mesh):
    return jax.shard_map(
        local,
        mesh=mesh,
        in_specs=(P("chan", "tm", None), P(), P(), P(), P()),
        out_specs=(P("chan", "tm", None, None), P("chan", None, "tm", None)),
        check_vma=False,
    )
```

```python
import functools
import math

import jax
import jax.numpy as jnp
from jax import lax
from jax.experimental import pallas as pl
from jax.experimental.pallas import tpu as pltpu
from jax.sharding import PartitionSpec as P

VMEM = pltpu.VMEM
BF16 = jnp.bfloat16
F32 = jnp.float32
LIMIT = 32 * 1024 * 1024
MOST = 64 * 1000 * 1000
WIDE = 272


def dft_weights(phases, coarse):
    shape = (2 * phases, 2 * phases * coarse)
    source = lax.broadcasted_iota(jnp.int32, shape, 0)
    target = lax.broadcasted_iota(jnp.int32, shape, 1)
    j, p = source % phases, source // phases
    b, d, q = target % phases, (target // phases) % coarse, target // (phases * coarse)
    turn = (j * b + jnp.where(p == q, 0, jnp.where(q == 0, 3, 1) * phases // 4)) % phases
    table = jnp.zeros(shape, F32)
    for k in range(phases):
        exact = round(math.cos(2.0 * math.pi * k / phases), 15) / math.sqrt(phases)
        table = jnp.where(turn == k, jnp.float32(exact), table)
    return split_sum(jnp.concatenate([jnp.where(d == c, table, 0.0) for c in range(coarse)], 0))


def spread_taps(taps):
    phases = taps.shape[1]
    wide = jnp.concatenate([taps, jnp.zeros((taps.shape[0], 128 - phases), F32)], 1)
    while phases < 128:
        wide = wide + pltpu.roll(wide, phases, 1)
        phases *= 2
    return wide


def tap_tables(taps):
    row = lax.broadcasted_iota(jnp.int32, (8, 128), 0)
    tap = [jnp.broadcast_to(taps[m : m + 1, :], (8, 128)) for m in range(taps.shape[0])]
    zero = jnp.zeros((8, 128), F32)
    same = [jnp.where(row >= k, tap[k], zero) for k in range(1, 8)]
    beyond = [jnp.where(row < k, tap[8 + k], zero) for k in range(1, 4)]
    before = [jnp.where(row < k, tap[k], tap[8 + k] if k < 4 else zero) for k in range(1, 8)]
    return tap[0], tap[8], same, before, beyond


def split_sum(value):
    high = value.astype(BF16)
    return high, (value - high.astype(F32)).astype(BF16)


def fetch(sems, *pairs):
    copies = [
        pltpu.make_async_copy(source, target, sems.at[i]) for i, (source, target) in enumerate(pairs)
    ]
    for copy in copies:
        copy.start()
    return copies


def window_table(krow):
    shape = (WIDE, krow.shape[1])
    row = lax.broadcasted_iota(jnp.int32, shape, 0).astype(jnp.int16)
    column = jnp.broadcast_to(krow, shape).astype(jnp.int16)
    return jnp.where(row == column, jnp.ones(shape, BF16), jnp.zeros(shape, BF16))


def store_windows(window_ref, base, picked, step):
    base = pl.multiple_of(base, 16)
    lanes = slice(0, picked.shape[1])
    if step > 0:
        meet = pl.ds(base, 16)
        window_ref[meet, lanes] = window_ref[meet, lanes] + picked[:16]
        window_ref[pl.ds(pl.multiple_of(base + 16, 16), WIDE - 16), lanes] = picked[16:]
    else:
        window_ref[0:WIDE, lanes] = picked


def late_rows(fine):
    return (fine + 79) // 80 * 16


def tail_kernel(
    width_from, shift_from, voltage_ref, taps_from,
    out_ref, rest_ref, base_ref,
    width_ref, shift_ref, taps_ref, held_ref, member_ref, split_high_ref, split_low_ref, table_ref, window_ref, sems,
):
    inputs, _, samples = held_ref.shape
    fine = window_ref.shape[0] - 256
    lanes = 128
    phases = 16
    copies = fetch(
        sems,
        (width_from, width_ref),
        (shift_from, shift_ref),
        (taps_from, taps_ref),
        (voltage_ref, held_ref),
    )
    high_table, low_table = dft_weights(phases, 8)
    weights = jnp.concatenate([high_table, high_table, low_table], 0)
    copies[0].wait()
    copies[1].wait()
    lane = lax.broadcasted_iota(jnp.int32, (1, lanes), 1)
    place = lane // phases
    bins = lane % phases
    first = jnp.int32(0)
    bases = []
    for step in range(samples // 512):
        base = (first // 16) * 16
        base_ref[step] = base
        bases.append(base)
        rows = []
        for half in range(2):
            width = jnp.zeros((1, lanes), jnp.int32)
            shift = jnp.zeros((1, lanes), jnp.int32)
            begin = jnp.zeros((1, lanes), jnp.int32)
            for c in range(8):
                at = step * 16 + half * 8 + c
                here = place == c
                wide = width_ref[at]
                width = jnp.where(here, wide, width)
                shift = jnp.where(here, shift_ref[at], shift)
                begin = jnp.where(here, first, begin)
                first = first + wide
            room = (phases + 1 - width).astype(F32)
            whole = jnp.floor((shift.astype(F32) + 0.5) / room)
            start = shift - (whole * room).astype(jnp.int32)
            offset = bins - start
            inside = (offset >= 0) & (offset < width)
            rows.append(jnp.where(inside, begin + offset, -1))
        krow = jnp.concatenate(rows, 1) - base
        rest_ref[step : step + 1, :] = krow.astype(F32)
        member_ref[step * WIDE : (step + 1) * WIDE, :] = window_table(krow)

    copies[2].wait()
    taps = spread_taps(taps_ref[...])
    rest_ref[16 : 16 + taps.shape[0], 0:lanes] = taps
    _, eighth, _, before, beyond = tap_tables(taps)
    window_ref[:, 96:lanes] = jnp.zeros((window_ref.shape[0], lanes - 96), F32)
    copies[3].wait()

    def group(step, carry):
        for sub in range(2):
            spot = pl.ds(pl.multiple_of(step * 256 + sub * lanes, lanes), lanes)
            tops, bottoms = [], []
            for i in range(inputs):
                series = held_ref[i, :, spot].astype(F32)
                older, recent = series[:8], series[8:]
                top = eighth * recent
                bottom = jnp.zeros((8, lanes), F32)
                for k in range(1, 8):
                    recent_k = pltpu.roll(recent, k, 0)
                    top = top + before[k - 1] * recent_k
                    if k < 4:
                        top = top + beyond[k - 1] * pltpu.roll(older, k, 0)
                        bottom = bottom + beyond[k - 1] * recent_k
                tops.append(top)
                bottoms.append(bottom if i % 2 == 0 else pltpu.roll(bottom, 4, 0))
            packed = [bottoms[i] + bottoms[i + 1] for i in range(0, inputs, 2)]
            high, low = split_sum(jnp.concatenate(tops + packed, 0))
            at = pl.ds(pl.multiple_of(step * 48, 16), 48)
            split_high_ref[at, sub * lanes : (sub + 1) * lanes] = high
            split_low_ref[at, sub * lanes : (sub + 1) * lanes] = low
        return carry

    lax.fori_loop(0, samples // 256, group, 0, unroll=4)
    for step in range(samples // 1024):
        at = slice(step * 192, step * 192 + 192)
        high = split_high_ref[at, :]
        split = jnp.concatenate([high, split_low_ref[at, :], high], 1)
        spectra = jnp.dot(split, weights, preferred_element_type=F32).astype(BF16)
        for j in range(4):
            for q in range(2):
                to = (step * 2 + j // 2) * 96
                half = slice((j % 2) * lanes, (j % 2 + 1) * lanes)
                piece = spectra[j * 48 : (j + 1) * 48, q * lanes : (q + 1) * lanes]
                table_ref[to + q * 32 : to + q * 32 + 32, half] = piece[:32]
                table_ref[to + 64 + q * 16 : to + 64 + q * 16 + 16, half] = piece[32:]
    for step in range(samples // 512):
        picked = lax.dot_general(
            member_ref[step * WIDE : (step + 1) * WIDE, :],
            table_ref[step * 96 : (step + 1) * 96, :],
            (((1,), (1,)), ((), ())),
            preferred_element_type=F32,
        )
        store_windows(window_ref, bases[step], picked, step)
    half, block = fine // 2, late_rows(fine)
    at = lax.broadcasted_iota(jnp.int32, (half, lanes), 1)
    out_ref[0:half, :] = jnp.where(
        at < 64, window_ref[0:half, :], pltpu.roll(window_ref[half:fine, :], 64, 1)
    ).astype(BF16)
    source = lax.broadcasted_iota(jnp.int32, (lanes, lanes), 0)
    target = lax.broadcasted_iota(jnp.int32, (lanes, lanes), 1)
    packed = jnp.zeros((block, lanes), F32)
    for j in range(5):
        part = window_ref[j * block : min((j + 1) * block, fine), :].astype(BF16)
        if part.shape[0] < block:
            part = jnp.concatenate([part, jnp.zeros((block - part.shape[0], lanes), BF16)], 0)
        slot = target - 24 * j
        chosen = (slot >= 0) & (slot < 24) & (source == 64 + (slot // 3) * 4 + slot % 3)
        packed = packed + jnp.dot(
            part, jnp.where(chosen, 1.0, 0.0).astype(BF16), preferred_element_type=F32
        )
    out_ref[half : half + block, :] = packed.astype(BF16)


def own_kernel(
    base_from, voltage_ref, rest_from,
    window_ref,
    base_ref, rest_ref, held_ref, split_high_ref, split_low_ref, table_ref, sems,
):
    inputs, blocks, samples = held_ref.shape
    lanes = 128
    copies = fetch(sems, (rest_from, rest_ref), (base_from, base_ref), (voltage_ref, held_ref))
    high_table, low_table = dft_weights(16, 8)
    weights = jnp.concatenate([high_table, high_table, low_table], 0)
    for copy in copies:
        copy.wait()
    first, eighth, same, before, _ = tap_tables(rest_ref[16:28, 0:lanes])

    def group(step, carry):
        for i in range(inputs):
            for sub in range(2):
                spot = pl.ds(pl.multiple_of(step * 256 + sub * lanes, lanes), lanes)
                series = held_ref[i, :, spot].astype(F32)
                early, late = series[:8], series[8:]
                top = first * early
                bottom = first * late + eighth * early
                for k in range(1, 8):
                    early_k = pltpu.roll(early, k, 0)
                    top = top + same[k - 1] * early_k
                    bottom = bottom + before[k - 1] * early_k
                    bottom = bottom + same[k - 1] * pltpu.roll(late, k, 0)
                at = pl.ds(pl.multiple_of(step * 64 + i * blocks, blocks), blocks)
                high, low = split_sum(jnp.concatenate([top, bottom], 0))
                split_high_ref[at, sub * lanes : (sub + 1) * lanes] = high
                split_low_ref[at, sub * lanes : (sub + 1) * lanes] = low
        return carry

    lax.fori_loop(0, samples // 256, group, 0, unroll=2)
    for step in range(samples // 1024):
        at = slice(step * 256, step * 256 + 256)
        high = split_high_ref[at, :]
        split = jnp.concatenate([high, split_low_ref[at, :], high], 1)
        parts = split_sum(jnp.dot(split, weights, preferred_element_type=F32))
        for j in range(4):
            for q in range(2):
                for p in range(2):
                    to = (step * 2 + j // 2) * 256 + p * 128 + q * 64
                    table_ref[to : to + 64, (j % 2) * 128 : (j % 2) * 128 + 128] = parts[p][
                        j * 64 : (j + 1) * 64, q * 128 : (q + 1) * 128
                    ]
    for step in range(samples // 512):
        picked = lax.dot_general(
            window_table(rest_ref[step : step + 1, :].astype(jnp.int32)),
            table_ref[step * 256 : (step + 1) * 256, :],
            (((1,), (1,)), ((), ())),
            preferred_element_type=F32,
        )
        store_windows(window_ref, base_ref[step], picked[:, :lanes] + picked[:, lanes:], step)


def place_kernel(slot_ref, place_ref):
    fine = slot_ref.shape[1]
    rows = 16
    row = lax.broadcasted_iota(jnp.int32, (rows, fine), 0)
    slot = jnp.broadcast_to(slot_ref[...], (rows, fine))
    row, slot = row.astype(jnp.int16), slot.astype(jnp.int16)
    one, zero = jnp.ones((rows, fine), BF16), jnp.zeros((rows, fine), BF16)

    def places(step, carry):
        at = pl.multiple_of(step * rows, rows)
        here = row + at.astype(jnp.int16)
        place_ref[pl.ds(at, rows), :] = jnp.where(here == slot, one, zero)
        return carry

    lax.fori_loop(0, place_ref.shape[0] // rows, places, 0, unroll=4)


def send_kernel(window_ref, tail_ref, place_ref, out_ref, bins_ref):
    fine, lanes = bins_ref.shape
    half, block = fine // 2, late_rows(fine)
    source = lax.broadcasted_iota(jnp.int32, (lanes, lanes), 0)
    target = lax.broadcasted_iota(jnp.int32, (lanes, lanes), 1)

    def table(slot, size, per, first):
        chosen = (slot >= 0) & (slot < size) & (target == (slot // per) * 16 + first + slot % per)
        return jnp.where(chosen, 1.0, 0.0).astype(BF16)

    early = [table(source - 64 * h, 64, 8, 0) for h in range(2)]
    late = [table(source - 24 * j, 24, 3, 8) for j in range(5)]
    cuts = sorted({0, half, fine} | {j * block for j in range(1, 5)})
    for at, end in zip(cuts, cuts[1:]):
        h, j = at // half, at // block
        first = tail_ref[at - h * half : end - h * half, :]
        second = tail_ref[half + at - j * block : half + end - j * block, :]
        added = jnp.dot(
            jnp.concatenate([first, second], 1),
            jnp.concatenate([early[h], late[j]], 0),
            preferred_element_type=F32,
        )
        bins_ref[at:end, :] = (window_ref[at:end, :] + added).astype(BF16)
    step_rows = 448
    for step in range(out_ref.shape[0] // step_rows):
        at = slice(step * step_rows, (step + 1) * step_rows)
        out_ref[at, :] = jnp.dot(
            place_ref[at, :], bins_ref[...], preferred_element_type=F32
        ).astype(BF16)


def unpack_kernel(received_ref, out_ref, wide_ref, *, inputs_dev):
    fine_dev = out_ref.shape[0]
    rows, lanes = received_ref.shape
    devices = rows // fine_dev
    blocks = lanes // (2 * inputs_dev)
    wide_ref[...] = received_ref[...].astype(F32)
    inputs = inputs_dev * devices
    source = lax.broadcasted_iota(jnp.int32, (inputs, inputs), 0)
    target = lax.broadcasted_iota(jnp.int32, (inputs, inputs), 1)
    spread = jnp.where((source % devices) * inputs_dev + source // devices == target, 1.0, 0.0)
    spread = spread.astype(BF16)
    pieces = []
    for channel in range(fine_dev):
        turned = wide_ref[pl.ds(channel, devices, stride=fine_dev), :].T.astype(BF16)
        for q in range(2):
            pieces.append(
                jnp.concatenate(
                    [
                        turned[(q * inputs_dev + i) * blocks : (q * inputs_dev + i + 1) * blocks, :]
                        for i in range(inputs_dev)
                    ],
                    1,
                )
            )
    joined = jnp.concatenate(pieces, 0)
    placed = jnp.dot(joined, spread, preferred_element_type=F32).astype(BF16)
    out_ref[...] = placed.reshape(out_ref.shape)


def correlate_kernel(mine_ref, own_ref, ahead_ref, behind_ref, across_ref, *rest, scale, first):
    out_ref, block_ref, sems = rest[-3:]
    mine = pl.ds(pl.multiple_of(mine_ref[0], 128), 128)
    half = own_ref.shape[1] // 2
    copies = []
    for channel in range(across_ref.shape[0]):
        refs = [ref.at[first + channel] for ref in (own_ref, ahead_ref, behind_ref)]
        refs.append(across_ref.at[channel])
        right = jnp.concatenate([ref[...] for ref in refs], 0)
        real, imag = [], []
        for ref in refs:
            block = ref[:, mine]
            real.append(block)
            imag.append(block[half:])
            imag.append(-block[:half])
        left = jnp.concatenate([jnp.concatenate(real, 0), jnp.concatenate(imag, 0)], 1)
        product = lax.dot_general(
            left, right, (((0,), (0,)), ((), ())), preferred_element_type=F32
        )
        product = (product * scale).astype(BF16)
        block_ref[channel, 0] = product[:128]
        block_ref[channel, 1] = product[128:]
        copies.append(
            pltpu.make_async_copy(
                block_ref.at[channel], out_ref.at[first + channel], sems.at[channel]
            )
        )
        copies[-1].start()
    for copy in copies:
        copy.wait()


WHOLE = pl.BlockSpec(memory_space=VMEM)
SCALARS = pl.BlockSpec(memory_space=pltpu.SMEM)
APART = pl.BlockSpec(memory_space=pl.ANY)


def tail_part(voltage, fir_taps, zoom_width, zoom_shift, fine):
    inputs_dev, blocks, samples = voltage.shape
    groups = samples // 256
    return pl.pallas_call(
        tail_kernel,
        out_shape=(
            jax.ShapeDtypeStruct((fine // 2 + late_rows(fine), 128), BF16),
            jax.ShapeDtypeStruct((32, 256), F32),
            jax.ShapeDtypeStruct((samples // 512,), jnp.int32),
        ),
        in_specs=[APART] * 4,
        out_specs=(WHOLE, WHOLE, SCALARS),
        scratch_shapes=[
            pltpu.SMEM(zoom_width.shape, jnp.int32),
            pltpu.SMEM(zoom_shift.shape, jnp.int32),
            pltpu.VMEM(fir_taps.shape, F32),
            pltpu.VMEM(voltage.shape, BF16),
            pltpu.VMEM((samples // 512 * WIDE, 256), BF16),
            pltpu.VMEM((groups * 48, 256), BF16),
            pltpu.VMEM((groups * 48, 256), BF16),
            pltpu.VMEM((groups * 48, 256), BF16),
            pltpu.VMEM((fine + 256, 128), F32),
            pltpu.SemaphoreType.DMA((4,)),
        ],
        compiler_params=pltpu.CompilerParams(vmem_limit_bytes=MOST),
        name="tail_part",
    )(zoom_width, zoom_shift, voltage, fir_taps)


def own_part(voltage, rest, base, fine):
    inputs_dev, blocks, samples = voltage.shape
    groups = samples // 256
    return pl.pallas_call(
        own_kernel,
        out_shape=jax.ShapeDtypeStruct((fine + 256, 128), F32),
        in_specs=[APART] * 3,
        out_specs=WHOLE,
        scratch_shapes=[
            pltpu.SMEM(base.shape, jnp.int32),
            pltpu.VMEM(rest.shape, F32),
            pltpu.VMEM(voltage.shape, BF16),
            pltpu.VMEM((groups * 64, 256), BF16),
            pltpu.VMEM((groups * 64, 256), BF16),
            pltpu.VMEM((groups * 128, 256), BF16),
            pltpu.SemaphoreType.DMA((3,)),
        ],
        compiler_params=pltpu.CompilerParams(vmem_limit_bytes=MOST),
        cost_estimate=pl.CostEstimate(flops=5_000_000_000, bytes_accessed=4_000_000, transcendentals=0),
        name="own_part",
    )(base, voltage, rest)


def place_part(slot):
    fine = slot.shape[1]
    return pl.pallas_call(
        place_kernel,
        out_shape=jax.ShapeDtypeStruct((fine, fine), BF16),
        in_specs=[WHOLE],
        out_specs=WHOLE,
        compiler_params=pltpu.CompilerParams(vmem_limit_bytes=LIMIT),
        cost_estimate=pl.CostEstimate(flops=5_000_000_000, bytes_accessed=4_000_000, transcendentals=0),
        name="place_part",
    )(slot)


def send_part(window, tail, place):
    slots, fine = place.shape
    return pl.pallas_call(
        send_kernel,
        out_shape=jax.ShapeDtypeStruct((slots, 128), BF16),
        in_specs=[WHOLE] * 3,
        out_specs=WHOLE,
        scratch_shapes=[pltpu.VMEM((fine, 128), BF16)],
        compiler_params=pltpu.CompilerParams(vmem_limit_bytes=LIMIT),
        name="send_part",
    )(window, tail, place)


def unpack(received, fine_dev, inputs_dev):
    rows, lanes = received.shape
    devices = rows // fine_dev
    blocks = lanes // (2 * inputs_dev)
    whole = pl.BlockSpec(memory_space=VMEM)
    return pl.pallas_call(
        functools.partial(unpack_kernel, inputs_dev=inputs_dev),
        out_shape=jax.ShapeDtypeStruct((fine_dev, 2 * blocks, devices * inputs_dev), BF16),
        in_specs=[whole],
        out_specs=whole,
        scratch_shapes=[pltpu.VMEM((rows, lanes), F32)],
        compiler_params=pltpu.CompilerParams(vmem_limit_bytes=LIMIT),
        name="unpack",
    )(received)


def correlate(near, across, mine, scale, first, earlier=None):
    fine_dev, rows, inputs = near[0].shape
    fine_part = across.shape[0]
    whole = pl.BlockSpec(memory_space=VMEM)
    apart = pl.BlockSpec(memory_space=pl.ANY)
    held = [] if earlier is None else [earlier]
    return pl.pallas_call(
        functools.partial(correlate_kernel, scale=scale, first=first),
        out_shape=jax.ShapeDtypeStruct((fine_dev, 2, 128, inputs), BF16),
        in_specs=[pl.BlockSpec(memory_space=pltpu.SMEM)] + [whole] * 4 + [apart] * len(held),
        out_specs=apart,
        scratch_shapes=[
            pltpu.VMEM((fine_part, 2, 128, inputs), BF16),
            pltpu.SemaphoreType.DMA((fine_part,)),
        ],
        input_output_aliases={5: 0} if held else {},
        compiler_params=pltpu.CompilerParams(vmem_limit_bytes=LIMIT),
        cost_estimate=pl.CostEstimate(
            flops=2 * fine_part * 256 * inputs * 4 * rows,
            bytes_accessed=4_000_000,
            transcendentals=0,
        ),
        name="correlate",
    )(mine, *near, across, *held)


def local(voltage, fir_taps, zoom_width, zoom_shift, owner_slot):
    inputs_dev, blocks, samples = voltage.shape
    devices = lax.axis_size("chan")
    groups = lax.axis_size("tm")
    fine = owner_slot.shape[0]
    fine_dev = fine // devices
    up = [(i, i + 1) for i in range(groups - 1)]
    tail, rest, base = tail_part(voltage, fir_taps, zoom_width, zoom_shift, fine)
    tail = lax.ppermute(tail, "tm", up)
    window = own_part(voltage, rest, base, fine)
    slot, window = lax.optimization_barrier((owner_slot, window))
    place = place_part(slot[None, :])
    sent = send_part(window, tail, place)
    lanes = sent.shape[1]
    received = lax.all_to_all(
        sent.reshape(devices, fine_dev // 2, 2, lanes), "chan", split_axis=0, concat_axis=0, tiled=True
    )
    own = unpack(received.reshape(fine, lanes), fine_dev, inputs_dev)

    def around(turn):
        pairs = []
        for c in range(devices):
            for g in range(groups):
                to = (g + (turn if c % 2 == 0 else -turn)) % groups
                pairs.append((c * groups + g, c * groups + to))
        return pairs

    both = ("chan", "tm")
    ahead = lax.ppermute(own, both, around(1))
    spectra = jnp.transpose(own.reshape(fine_dev, 2, blocks, own.shape[2]), (0, 2, 1, 3))
    later, spectra = lax.optimization_barrier((own, spectra))
    behind = lax.ppermute(later, both, around(-1))
    first = fine_dev * 10 // 14
    across_a = lax.ppermute(ahead[:first], both, around(1))
    across_b = lax.ppermute(ahead[first:], both, around(1))
    mine = (lax.axis_index("tm") * 128).astype(jnp.int32)[None]
    scale = 1.0 / (blocks * groups)
    near = (own, ahead, behind)
    summed = correlate(near, across_a, mine, scale, 0)
    summed = correlate(near, across_b, mine, scale, first, summed)
    return spectra, summed


def solution(mesh):
    return jax.shard_map(
        local,
        mesh=mesh,
        in_specs=(P("chan", "tm", None), P(), P(), P(), P()),
        out_specs=(P("chan", "tm", None, None), P("chan", None, "tm", None)),
        check_vma=False,
    )
```
